32 devices in a mesh: rows: 8 (over z, y), hid: 4 (over x, core).
Axes of the slice: x: 2, y: 2, z: 4, core: 2. Of those that a mesh axis runs over, the one named last changes fastest.
Arguments:
- grid_input: bfloat16 [131072, 78], P('rows'), may hold values from -6 to 6
- grid_target: bfloat16 [131072, 78], P('rows'), may hold values from -6 to 6
- live_points: int32 [8], P('rows'), may hold values from 5461 to 16384, as said below
- level_weight: int32 [78], replicated, may hold values from 1 to 10
- g2m_index: int32 [16384, 8], P('rows'), may hold values from 0 to 16383
- m2m_index: int32 [16384, 6], P('rows'), may hold values from 0 to 2047
- m2g_index: int32 [131072, 3], P('rows'), may hold values from 0 to 2047
- grid_first: float32 [78, 256], P(None, 'hid'), may hold values from -0.625 to 0.625
- wide_first: float32 [3, 512, 256], P(None, None, 'hid'), may hold values from -0.25 to 0.25
- second_layer: float32 [3, 256, 256], P(None, 'hid'), may hold values from -0.375 to 0.375
- decode_second: float32 [256, 78], P('hid'), may hold values from -0.375 to 0.375
- hidden_bias: float32 [4, 256], P(None, 'hid'), may hold values from -3 to 3
- norm_params: float32 [2, 3, 256], replicated, may hold values from 0.5 to 1.5
- decode_bias: float32 [78], replicated, may hold values from -2 to 2
- grid_first_avg: float32 [78, 256], P(None, 'hid'), may hold values from -0.0008544922 to 0.0008544922
- wide_first_avg: float32 [3, 512, 256], P(None, None, 'hid'), may hold values from -0.0008544922 to 0.0008544922
- second_layer_avg: float32 [3, 256, 256], P(None, 'hid'), may hold values from -0.0008544922 to 0.0008544922
- decode_second_avg: float32 [256, 78], P('hid'), may hold values from -0.0008544922 to 0.0008544922
- hidden_bias_avg: float32 [4, 256], P(None, 'hid'), may hold values from -0.0034179688 to 0.0034179688
- norm_params_avg: float32 [2, 3, 256], replicated, may hold values from -0.0034179688 to 0.0034179688
- decode_bias_avg: float32 [78], replicated, may hold values from -0.0034179688 to 0.0034179688
- grid_first_sq: float32 [78, 256], P(None, 'hid'), may hold values from 3.0517577e-09 to 1.2207031e-08
- wide_first_sq: float32 [3, 512, 256], P(None, None, 'hid'), may hold values from 3.0517577e-09 to 1.2207031e-08
- second_layer_sq: float32 [3, 256, 256], P(None, 'hid'), may hold values from 3.0517577e-09 to 1.2207031e-08
- decode_second_sq: float32 [256, 78], P('hid'), may hold values from 3.0517577e-09 to 1.2207031e-08
- hidden_bias_sq: float32 [4, 256], P(None, 'hid'), may hold values from 4.8828124e-08 to 1.953125e-07
- norm_params_sq: float32 [2, 3, 256], replicated, may hold values from 4.8828124e-08 to 1.953125e-07
- decode_bias_sq: float32 [78], replicated, may hold values from 4.8828124e-08 to 1.953125e-07
Outputs:
- loss_total: float32 [], replicated
- loss_weight: float32 [], replicated
- grid_first_new: float32 [78, 256], P(None, 'hid')
- wide_first_new: float32 [3, 512, 256], P(None, None, 'hid')
- second_layer_new: float32 [3, 256, 256], P(None, 'hid')
- decode_second_new: float32 [256, 78], P('hid')
- hidden_bias_new: float32 [4, 256], P(None, 'hid')
- norm_params_new: float32 [2, 3, 256], replicated
- decode_bias_new: float32 [78], replicated
- grid_first_avg_new: float32 [78, 256], P(None, 'hid')
- wide_first_avg_new: float32 [3, 512, 256], P(None, None, 'hid')
- second_layer_avg_new: float32 [3, 256, 256], P(None, 'hid')
- decode_second_avg_new: float32 [256, 78], P('hid')
- hidden_bias_avg_new: float32 [4, 256], P(None, 'hid')
- norm_params_avg_new: float32 [2, 3, 256], replicated
- decode_bias_avg_new: float32 [78], replicated
- grid_first_sq_new: float32 [78, 256], P(None, 'hid')
- wide_first_sq_new: float32 [3, 512, 256], P(None, None, 'hid')
- second_layer_sq_new: float32 [3, 256, 256], P(None, 'hid')
- decode_second_sq_new: float32 [256, 78], P('hid')
- hidden_bias_sq_new: float32 [4, 256], P(None, 'hid')
- norm_params_sq_new: float32 [2, 3, 256], replicated
- decode_bias_sq_new: float32 [78], replicated
- grid_first_half: bfloat16 [78, 256], P(None, 'hid')
- wide_first_half: bfloat16 [3, 512, 256], P(None, None, 'hid')
- second_layer_half: bfloat16 [3, 256, 256], P(None, 'hid')
- decode_second_half: bfloat16 [256, 78], P('hid')
The draws below stay inside these ranges and needn't reach their ends.
Inputs may be any that keep to these rules, and one draw needn't show every extreme that they name: `live_points`: index 0 of rows holds 5461 live points, the last index 16384; the counts never fall along rows.
All inputs are finite; a program needn't handle non-finite values.
Results may differ from the reference program's by a relative error of at most 0.00145.
The reference program's roundings to bfloat16 on the way count: a program that leaves them out, or rounds other values in their place, can miss the bound.
Values may be sent and summed in bfloat16 or wider, within the bound.
A program may use at most 320 MiB of HBM per device.

```python
import math
import jax
import jax.numpy as jnp
from jax import lax

CH = 78
LATENT = 256
HIDDEN_SIZE = 256
GRID_DEV = 16384
MESH_DEV = 2048
G2M_DEG = 8
M2M_DEG = 6
M2G_DEG = 3
STEP_COUNT = 5
ROW_GROUPS = 8
GRID_TOTAL = 131072
MESH_TOTAL = 16384


def draw_live_points(key, part):
    key = jax.random.fold_in(key, 7)
    groups = ROW_GROUPS
    least = GRID_DEV // 3
    drawn = jnp.sort(jax.random.randint(key, (groups,), least, GRID_DEV + 1))
    place = jnp.arange(groups, dtype=jnp.int32)
    counts = jnp.where(place == 0, least, jnp.where(place == groups - 1, GRID_DEV, drawn))
    return counts.astype(jnp.int32)


def plant(array, rng, smallest, largest):
    longest = array.shape.index(max(array.shape))
    spots = []
    for shift in (0, 1):
        where = [jax.random.randint(jax.random.fold_in(rng, axis), (), 0, length) for axis, length in enumerate(array.shape)]
        where[longest] = (where[longest] + shift) % array.shape[longest]
        spots.append(tuple(where))
    return array.at[spots[0]].set(smallest).at[spots[1]].set(largest)


def block_levels(own_key, shape, cuts, smallest, largest):
    factor_of = 1.0
    for position, shards_of in cuts:
        steps = jax.random.uniform(jax.random.fold_in(jax.random.fold_in(own_key, 6), position), (shards_of,), jnp.float32, smallest / len(cuts), largest / len(cuts))
        factor_of = factor_of * jnp.repeat(jnp.exp(steps), shape[position] // shards_of).reshape((-1,) + (1,) * (len(shape) - 1 - position))
    return factor_of


def scatter_about(own_key, shape, width, most, split=(), kind=jnp.bfloat16):
    values = width * jax.random.normal(own_key, shape, jnp.float32)
    if split:
        values = values * block_levels(own_key, shape, split, -0.22, 0.18)
    return jnp.clip(values, -most, most).astype(kind)


def setup_inputs(seed: int = 0) -> dict:
    splits = jax.random.split(jax.random.key(seed), 29)
    grid_input = scatter_about(splits[0], (GRID_TOTAL, CH), 1.0, 6.0, ((0, 8),))
    grid_target = scatter_about(splits[1], (GRID_TOTAL, CH), 1.0, 6.0, ((0, 8),))
    live_points = draw_live_points(jax.random.fold_in(splits[28], 71), 0)
    level_weight = plant(jax.random.randint(splits[3], (CH,), 1, 11), jax.random.fold_in(splits[3], 1), 1, 10).astype(jnp.int32)
    g2m_index = plant(jax.random.randint(splits[4], (MESH_TOTAL, G2M_DEG), 0, GRID_DEV), jax.random.fold_in(splits[4], 1), 0, GRID_DEV - 1).astype(jnp.int32)
    m2m_index = plant(jax.random.randint(splits[5], (MESH_TOTAL, M2M_DEG), 0, MESH_DEV), jax.random.fold_in(splits[5], 1), 0, MESH_DEV - 1).astype(jnp.int32)
    m2g_index = plant(jax.random.randint(splits[6], (GRID_TOTAL, M2G_DEG), 0, MESH_DEV), jax.random.fold_in(splits[6], 1), 0, MESH_DEV - 1).astype(jnp.int32)
    grid_first = scatter_about(splits[7], (CH, HIDDEN_SIZE), CH ** -0.5, 0.625, ((1, 4),), jnp.float32)
    wide_first = scatter_about(splits[8], (3, 2 * LATENT, HIDDEN_SIZE), (2 * LATENT) ** -0.5, 0.25, ((2, 4),), jnp.float32)
    second_layer = scatter_about(splits[9], (3, HIDDEN_SIZE, LATENT), HIDDEN_SIZE ** -0.5, 0.375, ((1, 4),), jnp.float32)
    decode_second = scatter_about(splits[10], (HIDDEN_SIZE, CH), HIDDEN_SIZE ** -0.5, 0.375, ((0, 4),), jnp.float32)
    hidden_bias = scatter_about(splits[11], (4, HIDDEN_SIZE), 0.5, 3.0, ((1, 4),), jnp.float32)
    norm_params = jnp.clip(jax.random.uniform(splits[12], (2, 3, LATENT), jnp.float32, 0.5, 1.5), 0.5, 1.5)
    decode_bias = scatter_about(splits[13], (CH,), 0.3, 2.0, (), jnp.float32)
    grid_first_avg = scatter_about(splits[14], (CH, HIDDEN_SIZE), (0.02 / (GRID_DEV * ROW_GROUPS) ** 0.5), 0.0008544922, ((1, 4),), jnp.float32)
    wide_first_avg = scatter_about(splits[15], (3, 2 * LATENT, HIDDEN_SIZE), (0.02 / (GRID_DEV * ROW_GROUPS) ** 0.5), 0.0008544922, ((2, 4),), jnp.float32)
    second_layer_avg = scatter_about(splits[16], (3, HIDDEN_SIZE, LATENT), (0.02 / (GRID_DEV * ROW_GROUPS) ** 0.5), 0.0008544922, ((1, 4),), jnp.float32)
    decode_second_avg = scatter_about(splits[17], (HIDDEN_SIZE, CH), (0.02 / (GRID_DEV * ROW_GROUPS) ** 0.5), 0.0008544922, ((0, 4),), jnp.float32)
    hidden_bias_avg = scatter_about(splits[18], (4, HIDDEN_SIZE), (0.08 / (GRID_DEV * ROW_GROUPS) ** 0.5), 0.0034179688, ((1, 4),), jnp.float32)
    norm_params_avg = scatter_about(splits[19], (2, 3, LATENT), (0.08 / (GRID_DEV * ROW_GROUPS) ** 0.5), 0.0034179688, (), jnp.float32)
    decode_bias_avg = scatter_about(splits[20], (CH,), (0.08 / (GRID_DEV * ROW_GROUPS) ** 0.5), 0.0034179688, (), jnp.float32)
    grid_first_sq = jnp.clip(jnp.exp(math.log(1.2207030941624453e-08) - 1.3862944 * jax.random.uniform(splits[21], (CH, HIDDEN_SIZE), jnp.float32) ** block_levels(splits[21], (CH, HIDDEN_SIZE), ((1, 4),), -0.2, 0.2)), 3.051757735406113e-09, 1.2207030941624453e-08)
    wide_first_sq = jnp.clip(jnp.exp(math.log(1.2207030941624453e-08) - 1.3862944 * jax.random.uniform(splits[22], (3, 2 * LATENT, HIDDEN_SIZE), jnp.float32) ** block_levels(splits[22], (3, 2 * LATENT, HIDDEN_SIZE), ((2, 4),), -0.2, 0.2)), 3.051757735406113e-09, 1.2207030941624453e-08)
    second_layer_sq = jnp.clip(jnp.exp(math.log(1.2207030941624453e-08) - 1.3862944 * jax.random.uniform(splits[23], (3, HIDDEN_SIZE, LATENT), jnp.float32) ** block_levels(splits[23], (3, HIDDEN_SIZE, LATENT), ((1, 4),), -0.2, 0.2)), 3.051757735406113e-09, 1.2207030941624453e-08)
    decode_second_sq = jnp.clip(jnp.exp(math.log(1.2207030941624453e-08) - 1.3862944 * jax.random.uniform(splits[24], (HIDDEN_SIZE, CH), jnp.float32) ** block_levels(splits[24], (HIDDEN_SIZE, CH), ((0, 4),), -0.2, 0.2)), 3.051757735406113e-09, 1.2207030941624453e-08)
    hidden_bias_sq = jnp.clip(jnp.exp(math.log(1.9531249506599124e-07) - 1.3862944 * jax.random.uniform(splits[25], (4, HIDDEN_SIZE), jnp.float32) ** block_levels(splits[25], (4, HIDDEN_SIZE), ((1, 4),), -0.2, 0.2)), 4.882812376649781e-08, 1.9531249506599124e-07)
    norm_params_sq = jnp.clip(jnp.exp(jax.random.uniform(splits[26], (2, 3, LATENT), jnp.float32, math.log(4.882812376649781e-08), math.log(1.9531249506599124e-07))), 4.882812376649781e-08, 1.9531249506599124e-07)
    decode_bias_sq = jnp.clip(jnp.exp(jax.random.uniform(splits[27], (CH,), jnp.float32, math.log(4.882812376649781e-08), math.log(1.9531249506599124e-07))), 4.882812376649781e-08, 1.9531249506599124e-07)
    return {"grid_input": grid_input, "grid_target": grid_target, "live_points": live_points, "level_weight": level_weight, "g2m_index": g2m_index, "m2m_index": m2m_index, "m2g_index": m2g_index, "grid_first": grid_first, "wide_first": wide_first, "second_layer": second_layer, "decode_second": decode_second, "hidden_bias": hidden_bias, "norm_params": norm_params, "decode_bias": decode_bias, "grid_first_avg": grid_first_avg, "wide_first_avg": wide_first_avg, "second_layer_avg": second_layer_avg, "decode_second_avg": decode_second_avg, "hidden_bias_avg": hidden_bias_avg, "norm_params_avg": norm_params_avg, "decode_bias_avg": decode_bias_avg, "grid_first_sq": grid_first_sq, "wide_first_sq": wide_first_sq, "second_layer_sq": second_layer_sq, "decode_second_sq": decode_second_sq, "hidden_bias_sq": hidden_bias_sq, "norm_params_sq": norm_params_sq, "decode_bias_sq": decode_bias_sq}


HIGH = lax.Precision.HIGHEST

@jax.custom_vjp
def low(v):
    return lax.optimization_barrier(v.astype(jnp.bfloat16)).astype(jnp.float32)

@jax.custom_vjp
def low_back(v):
    return v

def low_keep(v):
    return (low(v), None)

def low_pass(kept, grad):
    return (grad,)

def back_keep(v):
    return (v, None)

def back_low(kept, grad):
    return (low(grad),)
low.defvjp(low_keep, low_pass)
low_back.defvjp(back_keep, back_low)

def layer_mlp(inputs, first, bias, second):
    pre = jnp.dot(inputs, first, precision=HIGH) + bias
    pre = low_back(pre)
    act = low(jax.nn.silu(pre))
    return low_back(jnp.dot(act, second, precision=HIGH))

def layer_norm(values, gain, shift):
    centre = values - lax.optimization_barrier(jnp.mean(values, -1, keepdims=True))
    var = lax.optimization_barrier(jnp.mean(centre * centre, -1, keepdims=True))
    return centre * lax.rsqrt(var + 1e-05) * gain + shift

def adamw(weight, avg, sq, grad, rate, decay):
    avg_new = 0.5 * avg + 0.5 * grad
    sq_new = 0.5 * sq + 0.5 * grad * grad
    fix = 1.0 - 0.5 ** STEP_COUNT
    step = avg_new / fix / (jnp.sqrt(sq_new / fix) + 1e-08)
    return (weight - rate * (step + decay * weight), avg_new, sq_new)

def reference(grid_input, grid_target, live_points, level_weight, g2m_index, m2m_index, m2g_index, grid_first, wide_first, second_layer, decode_second, hidden_bias, norm_params, decode_bias, grid_first_avg, wide_first_avg, second_layer_avg, decode_second_avg, hidden_bias_avg, norm_params_avg, decode_bias_avg, grid_first_sq, wide_first_sq, second_layer_sq, decode_second_sq, hidden_bias_sq, norm_params_sq, decode_bias_sq):
    inputs = grid_input.astype(jnp.float32)
    target = grid_target.astype(jnp.float32)
    grid_block = (jnp.arange(GRID_TOTAL) // GRID_DEV).astype(jnp.int32)
    mesh_block = (jnp.arange(MESH_TOTAL) // MESH_DEV).astype(jnp.int32)
    g2m = g2m_index + (mesh_block * GRID_DEV)[:, None]
    m2m = m2m_index + (mesh_block * MESH_DEV)[:, None]
    m2g = m2g_index + (grid_block * MESH_DEV)[:, None]
    local_row = (jnp.arange(GRID_TOTAL) % GRID_DEV).astype(jnp.int32)
    mask = (local_row < live_points[grid_block]).astype(jnp.float32)[:, None]
    delta = (target - inputs) * mask
    count = jnp.sum(mask)
    var = lax.optimization_barrier(jnp.sum(delta * delta, 0)) / count + 1e-06
    weights = level_weight.astype(jnp.float32)
    loss_weight = count * jnp.sum(weights)

    def forward(params):
        gfirst, wfirst, second, dsecond, hbias, nparams, dbias = params
        glat = layer_norm(layer_mlp(inputs, gfirst, hbias[0], second[0]), nparams[0, 0], nparams[1, 0])
        h0 = lax.optimization_barrier(jnp.mean(glat[g2m], 1))
        recv = jnp.broadcast_to(h0[:, None, :], (MESH_TOTAL, M2M_DEG, LATENT))
        edge_in = jnp.concatenate([recv, h0[m2m]], -1).reshape(-1, 2 * LATENT)
        elat = layer_norm(layer_mlp(low(edge_in), wfirst[0], hbias[1], second[1]), nparams[0, 1], nparams[1, 1])
        agg = lax.optimization_barrier(jnp.sum(elat.reshape(MESH_TOTAL, M2M_DEG, LATENT), 1))
        node_in = low(jnp.concatenate([h0, agg], -1))
        h1 = h0 + layer_norm(layer_mlp(node_in, wfirst[1], hbias[2], second[2]), nparams[0, 2], nparams[1, 2])
        back = lax.optimization_barrier(jnp.mean(h1[m2g], 1))
        dec_in = low(jnp.concatenate([glat, back], -1))
        pred = inputs + layer_mlp(dec_in, wfirst[2], hbias[3], dsecond) + dbias
        err = pred - target
        total = jnp.sum(mask * weights * err * err / var)
        return (total / loss_weight, total)

    def half(v):
        return v.astype(jnp.bfloat16).astype(jnp.float32)
    params = (half(grid_first), half(wide_first), half(second_layer), half(decode_second), hidden_bias, norm_params, decode_bias)
    loss, back_fn, loss_total = jax.vjp(forward, params, has_aux=True)
    grads = back_fn(jnp.float32(1.0))[0]
    masters = (grid_first, wide_first, second_layer, decode_second, hidden_bias, norm_params, decode_bias)
    avgs = (grid_first_avg, wide_first_avg, second_layer_avg, decode_second_avg, hidden_bias_avg, norm_params_avg, decode_bias_avg)
    sqs = (grid_first_sq, wide_first_sq, second_layer_sq, decode_second_sq, hidden_bias_sq, norm_params_sq, decode_bias_sq)
    news, avg_news, sq_news = ([], [], [])
    for index in range(7):
        rate = 0.05 if index < 4 else 0.3
        decay = 0.1 if index < 4 else 0.0
        fresh, avg_new, sq_new = adamw(masters[index], avgs[index], sqs[index], grads[index], rate, decay)
        news.append(fresh)
        avg_news.append(avg_new)
        sq_news.append(sq_new)
    return (loss_total, loss_weight, news[0], news[1], news[2], news[3], news[4], news[5], news[6], avg_news[0], avg_news[1], avg_news[2], avg_news[3], avg_news[4], avg_news[5], avg_news[6], sq_news[0], sq_news[1], sq_news[2], sq_news[3], sq_news[4], sq_news[5], sq_news[6], news[0].astype(jnp.bfloat16), news[1].astype(jnp.bfloat16), news[2].astype(jnp.bfloat16), news[3].astype(jnp.bfloat16))
```

```python
import functools

import jax
import jax.numpy as jnp
from jax import lax
from jax.experimental import pallas as pl
from jax.experimental.pallas import tpu as pltpu
from jax.sharding import PartitionSpec as P

STEP_COUNT = 5
MESH = pl.DeviceIdType.MESH
bf16 = jnp.bfloat16
f32 = jnp.float32
TILE = 512
PAD = 80
COLS = {"g1": 0, "g2": 128, "e1": 384, "e2": 896, "n1": 1152, "n2": 1664, "d1": 1920, "d2": 2432}
GROUPS = {"g": (0, 384), "e": (384, 768), "n": (1152, 768), "d": (1920, 640)}
PACK = 2560


def mm(left, right):
    return lax.dot_general(left, right, (((1,), (0,)), ((), ())), preferred_element_type=f32)


def mt(left, right):
    return lax.dot_general(left, right, (((1,), (1,)), ((), ())), preferred_element_type=f32)


def flip(values):
    return values.astype(f32).T.astype(bf16)


def split2(values):
    high = values.astype(bf16)
    low = (values - high.astype(f32)).astype(bf16)
    return high, low


def fold(values):
    total = values[:, :128]
    for at in range(128, values.shape[1], 128):
        total = total + values[:, at : at + 128]
    return total


def ones_at(index, base, rows):
    lanes = index.shape[1]
    local = lax.broadcasted_iota(jnp.int32, (256, lanes), 0).astype(f32).astype(bf16)
    parts = []
    for block in range(rows // 256):
        total = None
        for k in range(index.shape[0]):
            shifted = (index[k : k + 1] - (base + block * 256)).astype(f32).astype(bf16)
            hit = jnp.where(
                jnp.broadcast_to(shifted, (256, lanes)) == local,
                jnp.asarray(1, bf16),
                jnp.asarray(0, bf16),
            )
            total = hit if total is None else total + hit
        parts.append(total)
    return parts


def act_forward(pre):
    sigma = 0.5 * jnp.tanh(0.5 * pre) + 0.5
    act = pre * sigma
    return act.astype(bf16), sigma + act * (1.0 - sigma)


def norm_forward(values):
    size = values.shape[0]
    centre = values - jnp.sum(values, 0, keepdims=True) * (1.0 / size)
    var = jnp.sum(centre * centre, 0, keepdims=True) * (1.0 / size)
    scale = lax.rsqrt(var + 1e-05)
    return centre * scale, scale


def norm_backward(upstream, normed, scale, gain):
    size = upstream.shape[0]
    scaled = upstream * gain
    first = jnp.sum(scaled, 0, keepdims=True) * (1.0 / size)
    second = jnp.sum(scaled * normed, 0, keepdims=True) * (1.0 / size)
    return scale * (scaled - first - normed * second)


def pick_kernel(place_ref, index_ref, xt_ref, tt_ref, xm_ref, tm_ref, xg_ref, rows, got):
    grid_rows = xt_ref.shape[1]
    channels = xt_ref.shape[0]
    degree, share = index_ref.shape
    mine = xm_ref.shape[1]

    def padded(values, to):
        return jnp.concatenate(
            [values.astype(f32), jnp.zeros((to - channels, values.shape[1]), f32)], 0
        )

    def turn(i, carry):
        at = pl.multiple_of(i * TILE, TILE)
        rows[pl.ds(at, TILE), :] = padded(xt_ref[:, pl.ds(at, TILE)], 128).T
        return carry

    lax.fori_loop(0, grid_rows // TILE, turn, 0)
    step = 16
    for k in range(degree):

        def pick(i, carry):
            for u in range(step):
                got[pl.ds(k * share + i * step + u, 1), :] = rows[
                    pl.ds(index_ref[k, i * step + u], 1), :
                ]
            return carry

        lax.fori_loop(0, share // step, pick, 0)

    def back(i, carry):
        at = pl.multiple_of(i * TILE, TILE)
        here = pl.ds(at, TILE)
        there = pl.ds(pl.multiple_of(place_ref[0] * mine + i * TILE, TILE), TILE)
        xg_ref[:, here] = got[here, :].T[:PAD].astype(bf16)
        xm_ref[:, here] = padded(xt_ref[:, there], PAD).astype(bf16)
        tm_ref[:, here] = padded(tt_ref[:, there], PAD).astype(bf16)
        return carry

    lax.fori_loop(0, mine // TILE, back, 0)


class Mail:
    def __init__(self, send, recv):
        self.send, self.recv, self.used = send, recv, 0

    def copy(self, source, target, device):
        at = self.used
        self.used += 1
        if self.send is None:
            return None
        copy = pltpu.make_async_remote_copy(
            src_ref=source,
            dst_ref=target,
            send_sem=self.send.at[at],
            recv_sem=self.recv.at[at],
            device_id=device,
            device_id_type=MESH,
        )
        copy.start()
        return copy


def count_copies(row_groups):
    near = min(row_groups, 8)
    far = row_groups // near
    sums = 3 + (row_groups - 1)
    rows_sum = 2 * (near - 1) + (far - 1)
    return 15 + 9 + 8 + sums + 4 * (4 + rows_sum) + 3


def main_kernel(
    live_ref,
    x_ref,
    t_ref,
    xg_ref,
    g2m_ref,
    m2m_ref,
    m2g_ref,
    wown_ref,
    bown_ref,
    norm_ref,
    chan_ref,
    out_ref,
    all_ref,
    tot_ref,
    w,
    wt,
    bias,
    h0full,
    h1full,
    hgfull,
    onehot,
    ds_g,
    act_g,
    nrm_g,
    scale_g,
    dec_in,
    dp_d,
    dglat,
    ds_e,
    act_e,
    hs_e,
    nrm_e,
    scale_e,
    dsum,
    land_a,
    land_b,
    grad,
    gland_a,
    gland_b,
    held,
    rland,
    fland,
    nacc,
    bacc,
    cacc,
    h0_mine,
    node_in,
    mesh_tmp,
    small,
    sland_h,
    sland_r,
    send,
    recv,
    *,
    row_groups,
    g2m_deg,
    m2g_deg,
):
    hid = lax.axis_index("hid")
    row = lax.axis_index("rows")
    near = min(row_groups, 8)
    far = row_groups // near
    row_near = lax.rem(row, near)
    row_far = row // near
    core = hid + 1 - 2 * lax.rem(hid, 2)
    across = lax.rem(hid + 2, 4)
    corner = lax.rem(core + 2, 4)
    mail = Mail(send, recv)
    mine = x_ref.shape[1]
    share = h0_mine.shape[1]
    mesh_rows = h0full.shape[1]
    tiles = mine // TILE
    degree = m2m_ref.shape[0]
    latent = h0_mine.shape[0]

    def peer(device):
        return {"hid": device, "rows": row}

    def row_peer(device):
        return {"hid": hid, "rows": device}

    barrier = pltpu.get_barrier_semaphore()
    for device in (core, across, corner):
        pl.semaphore_signal(barrier, inc=1, device_id=peer(device), device_id_type=MESH)
    for step in range(1, row_groups):
        pl.semaphore_signal(
            barrier,
            inc=1,
            device_id=row_peer(lax.rem(row + step, row_groups)),
            device_id_type=MESH,
        )
    pl.semaphore_wait(barrier, 3 + row_groups - 1)

    def gather_start(view):
        near_copy = mail.copy(view(hid), view(hid), peer(core))
        far_copy = mail.copy(view(hid), view(hid), peer(across))
        return near_copy, far_copy

    def gather_pass(view, copies):
        near_copy, far_copy = copies
        far_copy.wait_recv()
        return near_copy, far_copy, mail.copy(view(across), view(across), peer(core))

    def gather_wait(copies):
        near_copy, far_copy, passed = copies
        near_copy.wait_recv()
        passed.wait_recv()
        near_copy.wait_send()
        far_copy.wait_send()
        passed.wait_send()

    def rows_of(ref, block, size, start=0, width=None):
        width = ref.shape[1] if width is None else width
        return ref.at[pl.ds(pl.multiple_of(block * size, size), size), pl.ds(start, width)]

    def lanes_of(ref, block, size):
        return ref.at[:, pl.ds(pl.multiple_of(block * size, size), size)]

    w[pl.ds(pl.multiple_of(hid * 64, 64), 64), :] = wown_ref[...]
    bias[pl.ds(pl.multiple_of(hid * 64, 64), 64), :] = bown_ref[...]
    flights = {}
    for name in "gend":
        start, width = GROUPS[name]
        view = functools.partial(rows_of, w, size=64, start=start, width=width)
        flights[name] = gather_start(lambda block, view=view: view(block))
        if name == "g":
            flights["b"] = gather_start(lambda block: rows_of(bias, block, 64))

    def weights_pass(name):
        if name == "b":
            flights[name] = gather_pass(lambda block: rows_of(bias, block, 64), flights[name])
            return
        start, width = GROUPS[name]
        flights[name] = gather_pass(
            lambda block: rows_of(w, block, 64, start, width), flights[name]
        )

    lane = lax.broadcasted_iota(jnp.int32, (1, TILE), 1)
    first_row = hid * mine

    def live_mask(i):
        return (first_row + i * TILE + lane < live_ref[0]).astype(f32)

    cacc[...] = jnp.zeros_like(cacc)

    def squares(i, carry):
        here = pl.ds(pl.multiple_of(i * TILE, TILE), TILE)
        mask = live_mask(i)
        delta = (t_ref[:, here].astype(f32) - x_ref[:, here].astype(f32)) * mask
        cacc[0] += fold(delta * delta)
        cacc[1] += fold(jnp.broadcast_to(mask, (PAD, TILE)))
        return carry

    lax.fori_loop(0, tiles, squares, 0)
    col = lax.broadcasted_iota(jnp.int32, (PAD, 128), 1)
    small[...] = jnp.where(
        col == 0,
        jnp.sum(cacc[0], 1, keepdims=True),
        jnp.where(col == 1, jnp.sum(cacc[1], 1, keepdims=True), 0.0),
    )
    sum_hid = [
        mail.copy(small, sland_h.at[slot], peer(device))
        for slot, device in enumerate((core, across, corner))
    ]

    for name in "gb":
        weights_pass(name)
    gather_wait(flights["g"])
    gather_wait(flights["b"])
    b_g, b_e, b_n, b_d = (bias[:, k : k + 1] for k in range(4))
    gains = [norm_ref[:, k : k + 1] for k in range(3)]
    shifts = [norm_ref[:, k + 3 : k + 4] for k in range(3)]
    wt[:, 0:256] = flip(w[:, COLS["g2"] : COLS["g2"] + 256])
    w1g = w[:, 0:128][:, :PAD]

    def embed(inputs):
        pre = mm(w1g, inputs) + b_g
        act, slope = act_forward(pre)
        normed, scale = norm_forward(mm(wt[:, 0:256], act))
        return act, slope, normed, scale

    mesh_tmp[0] = jnp.zeros((latent, share), f32)

    def pool(i, carry):
        here = pl.ds(pl.multiple_of(i * TILE, TILE), TILE)
        mesh_tmp[0] += embed(xg_ref[:, here])[2] * gains[0] + shifts[0]
        return carry

    lax.fori_loop(0, g2m_deg, pool, 0)
    h0_mine[...] = mesh_tmp[0] * (1.0 / g2m_deg)
    my_mesh = pl.ds(pl.multiple_of(hid * share, share), share)
    h0_half = h0_mine[...].astype(bf16)
    h0full[:, my_mesh] = h0_half
    node_in[:latent, :] = h0_half
    h0_view = functools.partial(lanes_of, h0full, size=share)
    h0_flight = gather_start(lambda block: h0_view(block))

    for copy in sum_hid:
        copy.wait()
    small[...] = small[...] + sland_h[0] + sland_h[1] + sland_h[2]
    sum_rows = [
        mail.copy(small, sland_r.at[step - 1], row_peer(lax.rem(row + step, row_groups)))
        for step in range(1, row_groups)
    ]

    def own(i, carry):
        here = pl.ds(pl.multiple_of(i * TILE, TILE), TILE)
        act, slope, normed, scale = embed(x_ref[:, here])
        ds_g[:, here] = slope
        act_g[:, here] = act
        nrm_g[:, here] = normed
        scale_g[:, here] = scale
        dec_in[:latent, here] = (normed * gains[0] + shifts[0]).astype(bf16)
        return carry

    def own_range(a, b):
        lax.fori_loop(a, b, own, 0)

    own_range(0, tiles // 2)
    h0_flight = gather_pass(lambda block: h0_view(block), h0_flight)
    weights_pass("e")
    weights_pass("n")
    weights_pass("d")
    own_range(tiles // 2, tiles)
    for name in "end":
        gather_wait(flights[name])
    wt[:, 256:512] = flip(w[:, COLS["e2"] : COLS["e2"] + 256])
    wt[:, 512:768] = flip(w[:, COLS["n2"] : COLS["n2"] + 256])
    wt[:128, 768:1024] = flip(w[:, COLS["d2"] : COLS["d2"] + 128])
    gather_wait(h0_flight)

    e1 = COLS["e1"]
    mesh_tmp[0] = mm(w[:, e1 : e1 + 256], node_in[:latent, :]) + b_e
    mesh_tmp[1] = jnp.zeros((latent, share), f32)

    def edge_index(k):
        return m2m_ref[pl.ds(k, 1), my_mesh]

    def fill(index, base, rows):
        for block, part in enumerate(ones_at(index, base, rows)):
            onehot[block * 256 : block * 256 + 256, :] = part

    def edge(k, carry):
        fill(edge_index(k), 0, mesh_rows)
        sent = mm(h0full[...], onehot[...]).astype(bf16)
        hs_e[k] = sent
        pre = mesh_tmp[0] + mm(w[:, e1 + 256 : e1 + 512], sent)
        act, slope = act_forward(pre)
        act_e[k] = act
        ds_e[k] = slope
        normed, scale = norm_forward(mm(wt[:, 256:512], act))
        nrm_e[k] = normed
        scale_e[pl.ds(k, 1), :] = scale
        mesh_tmp[1] += normed * gains[1] + shifts[1]
        return carry

    lax.fori_loop(0, degree, edge, 0)

    n1 = COLS["n1"]
    node_in[latent:, :] = mesh_tmp[1].astype(bf16)
    act_n, slope_n = act_forward(mm(w[:, n1 : n1 + 512], node_in[...]) + b_n)
    normed_n, scale_n = norm_forward(mm(wt[:, 512:768], act_n))
    h1 = h0_mine[...] + (normed_n * gains[2] + shifts[2])
    ds_e[degree] = slope_n
    act_e[degree] = act_n
    nrm_e[degree] = normed_n
    scale_e[degree : degree + 1, :] = scale_n
    high, low = split2(h1)
    h1full[:latent, my_mesh] = high
    h1full[latent:, my_mesh] = low
    h1_view = functools.partial(lanes_of, h1full, size=share)
    h1_flight = gather_start(lambda block: h1_view(block))

    for copy in sum_rows:
        copy.wait()
    totals = small[...]
    for step in range(1, row_groups):
        totals = totals + sland_r[step - 1]
    tot_ref[...] = totals
    count = totals[:, 1:2]
    var = totals[:, 0:1] / count + 1e-06
    d_bias = chan_ref[:, 0:1]
    level = chan_ref[:, 1:2]
    loss_weight = count * jnp.sum(level, 0, keepdims=True)
    weight_var = level / var
    pull = 2.0 * weight_var / loss_weight
    nacc[...] = jnp.zeros_like(nacc)
    bacc[...] = jnp.zeros_like(bacc)
    cacc[...] = jnp.zeros_like(cacc)
    grad[...] = jnp.zeros_like(grad)
    dsum[...] = jnp.zeros_like(dsum)

    h1_flight = gather_pass(lambda block: h1_view(block), h1_flight)
    gather_wait(h1_flight)

    d1, d2 = COLS["d1"], COLS["d2"]
    my_grid = hid * mine

    def decode(i, carry):
        here = pl.ds(pl.multiple_of(i * TILE, TILE), TILE)
        fill(m2g_ref[:, pl.ds(pl.multiple_of(my_grid + i * TILE, TILE), TILE)], 0, mesh_rows)
        both = mm(h1full[...], onehot[...])
        back = (both[:latent] + both[latent:]) * (1.0 / m2g_deg)
        dec_in[latent:, here] = back.astype(bf16)
        pre = mm(w[:, d1 : d1 + 512], dec_in[:, here]) + b_d
        act, slope = act_forward(pre)
        out = mm(wt[:128, 768:1024], act)[:PAD]
        err = x_ref[:, here].astype(f32) + out + d_bias - t_ref[:, here].astype(f32)
        kept = err * live_mask(i)
        cacc[1] += fold(weight_var * kept * err)
        pred_grad = pull * kept
        cacc[0] += fold(pred_grad)
        upstream = pred_grad.astype(bf16)
        act_grad = mm(w[:, d2 : d2 + 128][:, :PAD], upstream)
        pre_grad = (act_grad * slope).astype(bf16)
        dp_d[:, here] = pre_grad
        dsum[...] += mt(pre_grad, onehot[...])
        grad[:, d2 : d2 + PAD] += mt(act, upstream)
        return carry

    lax.fori_loop(0, tiles, decode, 0)

    def spread_start(view, land):
        return (
            mail.copy(view(corner), land.at[1], peer(core)),
            mail.copy(view(core), land.at[0], peer(core)),
        )

    def spread_across(view, land, land_far, copies):
        copies[0].wait()
        view(across)[...] = view(across)[...] + land[1]
        return copies + (mail.copy(view(across), land_far, peer(across)),)

    def spread_end(view, land, land_far, copies):
        copies[1].wait()
        copies[2].wait()
        return view(hid)[...] + land[0] + land_far[...]

    d_view = functools.partial(lanes_of, dsum, size=share)

    def view_d(block):
        return d_view(block)

    d_flight = spread_start(view_d, land_a.at[0])
    w1d_low = flip(w[:, d1 : d1 + 256])
    wt[:, 1024:1280] = w1d_low
    d_flight = spread_across(view_d, land_a.at[0], land_b.at[0], d_flight)

    def decode_rest(i, carry):
        here = pl.ds(pl.multiple_of(i * TILE, TILE), TILE)
        pre_grad = dp_d[:, here]
        dglat[:, here] = mm(wt[:, 1024:1280], pre_grad)
        grad[:, d1 : d1 + 512] += mt(pre_grad, dec_in[:, here])
        bacc[3] += fold(pre_grad.astype(f32))
        return carry

    lax.fori_loop(0, tiles, decode_rest, 0)
    wt[:, 1024:1280] = flip(w[:, d1 + 256 : d1 + 512])
    wt[:, 1280:1536] = flip(w[:, n1 : n1 + 256])
    wt[:, 1536:1792] = flip(w[:, n1 + 256 : n1 + 512])
    wt[:, 1792:2048] = flip(w[:, e1 : e1 + 256])
    wt[:, 2048:2304] = flip(w[:, e1 + 256 : e1 + 512])

    high, low = split2(spread_end(view_d, land_a.at[0], land_b.at[0], d_flight))
    h1_grad = (mm(wt[:, 1024:1280], high) + mm(wt[:, 1024:1280], low)) * (1.0 / m2g_deg)
    nacc[2] += fold(h1_grad * nrm_e[degree])
    nacc[5] += fold(h1_grad)
    up_n = norm_backward(
        h1_grad, nrm_e[degree], scale_e[degree : degree + 1, :], gains[2]
    ).astype(bf16)
    n2 = COLS["n2"]
    pre_grad_n = (mm(w[:, n2 : n2 + 256], up_n) * ds_e[degree]).astype(bf16)
    mesh_tmp[0] = h1_grad + mm(wt[:, 1280:1536], pre_grad_n)
    mesh_tmp[1] = mm(wt[:, 1536:1792], pre_grad_n)

    dsum[...] = jnp.zeros_like(dsum)
    e2 = COLS["e2"]

    def edge_back(k, carry):
        upstream = mesh_tmp[1]
        normed = nrm_e[k]
        nacc[1] += fold(upstream * normed)
        nacc[4] += fold(upstream)
        up = norm_backward(upstream, normed, scale_e[pl.ds(k, 1), :], gains[1]).astype(bf16)
        pre_grad = (mm(w[:, e2 : e2 + 256], up) * ds_e[k]).astype(bf16)
        fill(edge_index(k), 0, mesh_rows)
        dsum[...] += mt(pre_grad, onehot[...])
        mesh_tmp[0] += mm(wt[:, 1792:2048], pre_grad)
        grad[:, e2 : e2 + 256] += mt(act_e[k], up)
        grad[:, e1 : e1 + 256] += mt(pre_grad, node_in[:latent, :])
        grad[:, e1 + 256 : e1 + 512] += mt(pre_grad, hs_e[k])
        bacc[1] += fold(pre_grad.astype(f32))
        return carry

    lax.fori_loop(0, degree, edge_back, 0)
    e_flight = spread_start(view_d, land_a.at[1])
    grad[:, n2 : n2 + 256] = mt(act_e[degree], up_n)
    e_flight = spread_across(view_d, land_a.at[1], land_b.at[1], e_flight)
    grad[:, n1 : n1 + 512] = mt(pre_grad_n, node_in[...])
    bacc[2] += fold(pre_grad_n.astype(f32))
    high, low = split2(spread_end(view_d, land_a.at[1], land_b.at[1], e_flight))
    h0_grad = mesh_tmp[0] + mm(wt[:, 2048:2304], high) + mm(wt[:, 2048:2304], low)
    high, low = split2(h0_grad * (1.0 / g2m_deg))
    hgfull[:latent, my_mesh] = high
    hgfull[latent:, my_mesh] = low
    hg_view = functools.partial(lanes_of, hgfull, size=share)
    hg_flight = gather_start(lambda block: hg_view(block))

    def chunk(start, width, block):
        return rows_of(grad, block, 64, start, width)

    def reduce_start(name):
        start, width = GROUPS[name]
        flight = (
            mail.copy(
                chunk(start, width, corner), gland_a.at[1, :, pl.ds(start, width)], peer(core)
            ),
            mail.copy(
                chunk(start, width, core), gland_a.at[0, :, pl.ds(start, width)], peer(core)
            ),
        )
        return flight

    def reduce_across(name, flight):
        start, width = GROUPS[name]
        cols = pl.ds(start, width)
        flight[0].wait()
        view = chunk(start, width, across)
        view[...] = view[...] + gland_a[1, :, cols]
        return flight + (mail.copy(view, gland_b.at[:, cols], peer(across)),)

    def reduce_rows(name, flight):
        start, width = GROUPS[name]
        cols = pl.ds(start, width)
        flight[1].wait()
        flight[2].wait()
        part = 64 // near
        held[:, cols] = chunk(start, width, hid)[...] + gland_a[0, :, cols] + gland_b[:, cols]
        copies = []
        for step in range(1, near):
            to = lax.rem(row_near + step, near)
            copies.append(
                mail.copy(
                    held.at[pl.ds(pl.multiple_of(to * part, part), part), cols],
                    rland.at[step - 1, :, cols],
                    row_peer(row_far * near + to),
                )
            )
        return copies

    def reduce_share(name, copies):
        start, width = GROUPS[name]
        cols = pl.ds(start, width)
        part = 64 // near
        own_rows = pl.ds(pl.multiple_of(row_near * part, part), part)
        own_part = out_ref.at[own_rows, cols]
        for copy in copies:
            copy.wait()
        total = held[own_rows, cols]
        for step in range(1, near):
            total = total + rland[step - 1, :, cols]
        if far > 1:
            fland[far - 1, :, cols] = total
            more = []
            for step in range(1, far):
                to = lax.rem(row_far + step, far)
                more.append(
                    mail.copy(
                        fland.at[far - 1, :, cols],
                        fland.at[step - 1, :, cols],
                        row_peer(to * near + row_near),
                    )
                )
            for copy in more:
                copy.wait()
            total = fland[far - 1, :, cols]
            for step in range(1, far):
                total = total + fland[step - 1, :, cols]
        own_part[...] = total
        out = []
        for step in range(1, near):
            to = lax.rem(row_near + step, near)
            out.append(mail.copy(own_part, own_part, row_peer(row_far * near + to)))
        return out

    hg_flight = gather_pass(lambda block: hg_view(block), hg_flight)
    gather_wait(hg_flight)

    def grid_back(i, carry):
        here = pl.ds(pl.multiple_of(i * TILE, TILE), TILE)
        base = my_grid + i * TILE
        both = None
        for at in range(0, mesh_rows, TILE):
            parts = ones_at(g2m_ref[:, at : at + TILE], base, TILE)
            for block, part in enumerate(parts):
                onehot[block * 256 + 0 : block * 256 + 256, :] = part
            term = mt(hgfull[:, at : at + TILE], onehot[:TILE, :])
            both = term if both is None else both + term
        upstream = dglat[:, here] + both[:latent] + both[latent:]
        normed = nrm_g[:, here]
        nacc[0] += fold(upstream * normed)
        nacc[3] += fold(upstream)
        up = norm_backward(upstream, normed, scale_g[:, here], gains[0]).astype(bf16)
        pre_grad = (mm(w[:, COLS["g2"] : COLS["g2"] + 256], up) * ds_g[:, here]).astype(bf16)
        grad[:, COLS["g2"] : COLS["g2"] + 256] += mt(act_g[:, here], up)
        grad[:, 0:PAD] += mt(pre_grad, x_ref[:, here])
        bacc[0] += fold(pre_grad.astype(f32))
        return carry

    lax.fori_loop(0, tiles, grid_back, 0)

    narrow = grad[:, 0:128]
    at_col = lax.broadcasted_iota(jnp.int32, (latent, 128), 1)
    for k in range(4):
        narrow = jnp.where(at_col == PAD + k, jnp.sum(bacc[k], 1, keepdims=True), narrow)
    for k in range(6):
        narrow = jnp.where(at_col == 96 + k, jnp.sum(nacc[k], 1, keepdims=True), narrow)
    grad[:, 0:128] = narrow
    side = grad[:PAD, 0:128]
    for k in range(2):
        side = jnp.where(col == 102 + k, jnp.sum(cacc[k], 1, keepdims=True), side)
    grad[:PAD, 0:128] = side

    names = "dneg"
    stage = {name: reduce_start(name) for name in names}
    stage = {name: reduce_across(name, stage[name]) for name in names}
    stage = {name: reduce_rows(name, stage[name]) for name in names}
    stage = {name: reduce_share(name, stage[name]) for name in names}
    for name in names:
        for copy in stage[name]:
            copy.wait()
    all_ref[pl.ds(pl.multiple_of(hid * 64, 64), 64), :] = out_ref[:, 0:128]
    last = [
        mail.copy(rows_of(all_ref, hid, 64), rows_of(all_ref, hid, 64), peer(device))
        for device in (core, across, corner)
    ]
    for copy in last:
        copy.wait()


def adam_step(weight, avg, sq, grad, rate, decay):
    avg_new = 0.5 * avg + 0.5 * grad
    sq_new = 0.5 * sq + 0.5 * grad * grad
    fix = 1.0 - 0.5**STEP_COUNT
    step = avg_new / fix / (jnp.sqrt(sq_new / fix) + 1e-08)
    return (weight - rate * (step + decay * weight), avg_new, sq_new)


def adam_kernel(out_ref, all_ref, *refs):
    ins, outs = refs[:21], refs[21:]

    def update(array, at, grad, rate, decay):
        fresh, avg_new, sq_new = adam_step(
            ins[array][at], ins[7 + array][at], ins[14 + array][at], grad, rate, decay
        )
        outs[array][at] = fresh
        outs[7 + array][at] = avg_new
        outs[14 + array][at] = sq_new
        if array < 4:
            outs[21 + array][at] = fresh.astype(bf16)

    everything = (slice(None), slice(None))
    channels = ins[0].shape[1]
    update(0, everything, out_ref[:, 0:128][:, :channels], 0.05, 0.1)
    for layer, name in enumerate(("e1", "n1", "d1")):
        update(1, (layer,) + everything, out_ref[:, COLS[name] : COLS[name] + 512], 0.05, 0.1)
    for layer, name in enumerate(("g2", "e2", "n2")):
        update(2, (layer,) + everything, out_ref[:, COLS[name] : COLS[name] + 256], 0.05, 0.1)
    update(3, everything, out_ref[:, COLS["d2"] : COLS["d2"] + 128][:, :channels], 0.05, 0.1)
    turned = out_ref[:, 0:128].T
    update(4, everything, turned[PAD : PAD + 4, :], 0.3, 0.0)
    wide = all_ref[...].T
    update(5, everything, wide[96:102, :], 0.3, 0.0)
    update(6, everything, wide[102:103, :128], 0.3, 0.0)


def body(
    grid_input,
    grid_target,
    live_points,
    level_weight,
    g2m_index,
    m2m_index,
    m2g_index,
    *params,
):
    groups = lax.axis_size("hid")
    row_groups = lax.axis_size("rows")
    place = lax.axis_index("hid")
    masters, avgs, squares = params[:7], params[7:14], params[14:21]
    grid_first, wide_first, second_layer, decode_second, hidden_bias, norm_params, decode_bias = (
        masters
    )
    grid_rows, channels = grid_input.shape
    mesh_rows, degree = m2m_index.shape
    latent = norm_params.shape[2]
    share = mesh_rows // groups
    mine = grid_rows // groups
    g2m_deg = g2m_index.shape[1]
    m2g_deg = m2g_index.shape[1]
    whole = pl.BlockSpec(memory_space=pltpu.VMEM)
    scalar = pl.BlockSpec(memory_space=pltpu.SMEM)

    g2m = g2m_index.T
    xm, tm, xg = pl.pallas_call(
        pick_kernel,
        out_shape=[jax.ShapeDtypeStruct((PAD, mine), bf16)] * 2
        + [jax.ShapeDtypeStruct((PAD, g2m_deg * share), bf16)],
        in_specs=[scalar, scalar, whole, whole],
        out_specs=[whole] * 3,
        scratch_shapes=[
            pltpu.VMEM((grid_rows, 128), f32),
            pltpu.VMEM((g2m_deg * share, 128), f32),
        ],
        compiler_params=pltpu.CompilerParams(vmem_limit_bytes=48 * 2**20),
        name="pick",
    )(
        place[None].astype(jnp.int32),
        lax.dynamic_slice_in_dim(g2m, place * share, share, 1),
        grid_input.T,
        grid_target.T,
    )

    def half(values, width):
        values = values.astype(bf16)
        return jnp.pad(values, ((0, 0), (0, width - values.shape[1])))

    wide_t = wide_first.transpose(0, 2, 1)
    pack = jnp.concatenate(
        [
            half(grid_first.T, 128),
            half(second_layer[0], 256),
            half(wide_t[0], 512),
            half(second_layer[1], 256),
            half(wide_t[1], 512),
            half(second_layer[2], 256),
            half(wide_t[2], 512),
            half(decode_second, 128),
        ],
        1,
    )
    bias_cols = jnp.pad(hidden_bias.T, ((0, 0), (0, 124)))
    norm_cols = jnp.pad(norm_params.reshape(6, latent).T, ((0, 0), (0, 122)))
    chan_cols = jnp.pad(
        jnp.stack([decode_bias, level_weight.astype(f32)], 1), ((0, PAD - channels), (0, 126))
    )
    copies = count_copies(row_groups)
    near = min(row_groups, 8)
    far = row_groups // near
    summed, spare, totals = pl.pallas_call(
        functools.partial(
            main_kernel, row_groups=row_groups, g2m_deg=g2m_deg, m2g_deg=m2g_deg
        ),
        out_shape=[
            jax.ShapeDtypeStruct((64, PACK), f32),
            jax.ShapeDtypeStruct((256, 128), f32),
            jax.ShapeDtypeStruct((PAD, 128), f32),
        ],
        in_specs=[scalar] + [whole] * 10,
        out_specs=[whole] * 3,
        scratch_shapes=[
            pltpu.VMEM((256, PACK), bf16),
            pltpu.VMEM((256, 2304), bf16),
            pltpu.VMEM((256, 128), f32),
            pltpu.VMEM((latent, mesh_rows), bf16),
            pltpu.VMEM((2 * latent, mesh_rows), bf16),
            pltpu.VMEM((2 * latent, mesh_rows), bf16),
            pltpu.VMEM((mesh_rows, TILE), bf16),
            pltpu.VMEM((latent, mine), f32),
            pltpu.VMEM((latent, mine), bf16),
            pltpu.VMEM((latent, mine), f32),
            pltpu.VMEM((1, mine), f32),
            pltpu.VMEM((2 * latent, mine), bf16),
            pltpu.VMEM((latent, mine), bf16),
            pltpu.VMEM((latent, mine), f32),
            pltpu.VMEM((degree + 1, latent, share), f32),
            pltpu.VMEM((degree + 1, latent, share), bf16),
            pltpu.VMEM((degree, latent, share), bf16),
            pltpu.VMEM((degree + 1, latent, share), f32),
            pltpu.VMEM((8, share), f32),
            pltpu.VMEM((latent, mesh_rows), f32),
            pltpu.VMEM((2, 2, latent, share), f32),
            pltpu.VMEM((2, latent, share), f32),
            pltpu.VMEM((256, PACK), f32),
            pltpu.VMEM((2, 64, PACK), f32),
            pltpu.VMEM((64, PACK), f32),
            pltpu.VMEM((64, PACK), f32),
            pltpu.VMEM((near - 1, 64 // near, PACK), f32),
            pltpu.VMEM((far, 64 // near, PACK), f32),
            pltpu.VMEM((6, latent, 128), f32),
            pltpu.VMEM((4, latent, 128), f32),
            pltpu.VMEM((2, PAD, 128), f32),
            pltpu.VMEM((latent, share), f32),
            pltpu.VMEM((2 * latent, share), bf16),
            pltpu.VMEM((2, latent, share), f32),
            pltpu.VMEM((PAD, 128), f32),
            pltpu.VMEM((3, PAD, 128), f32),
            pltpu.VMEM((row_groups - 1, PAD, 128), f32),
            pltpu.SemaphoreType.DMA((copies,)),
            pltpu.SemaphoreType.DMA((copies,)),
        ],
        compiler_params=pltpu.CompilerParams(
            collective_id=0, has_side_effects=True, vmem_limit_bytes=64 * 2**20
        ),
        name="step",
    )(
        live_points,
        xm,
        tm,
        xg,
        g2m,
        m2m_index.T,
        m2g_index.T,
        pack,
        bias_cols,
        norm_cols,
        chan_cols,
    )

    def flat(arrays):
        first, wide, second, last, bias, norm, out_bias = arrays
        return (
            first.T,
            wide.transpose(0, 2, 1),
            second,
            last,
            bias,
            norm.reshape(6, latent),
            jnp.pad(out_bias[None], ((0, 0), (0, 128 - channels))),
        )

    def unflat(arrays):
        first, wide, second, last, bias, norm, out_bias = arrays
        return (
            first.T,
            wide.transpose(0, 2, 1),
            second,
            last,
            bias,
            norm.reshape(2, 3, latent),
            out_bias[0, :channels],
        )

    operands = flat(masters) + flat(avgs) + flat(squares)
    shapes = [jax.ShapeDtypeStruct(v.shape, f32) for v in operands]
    shapes += [jax.ShapeDtypeStruct(v.shape, bf16) for v in operands[:4]]
    outs = pl.pallas_call(
        adam_kernel,
        out_shape=shapes,
        in_specs=[whole] * 23,
        out_specs=[whole] * 25,
        compiler_params=pltpu.CompilerParams(vmem_limit_bytes=32 * 2**20),
        name="adam",
    )(summed, spare, *operands)
    halves = outs[21:]
    loss_total = jnp.sum(spare[:PAD, 103])
    loss_weight = totals[0, 1] * jnp.sum(level_weight.astype(f32))
    return (
        (loss_total, loss_weight)
        + unflat(outs[0:7])
        + unflat(outs[7:14])
        + unflat(outs[14:21])
        + (halves[0].T, halves[1].transpose(0, 2, 1), halves[2], halves[3])
    )


def solution(mesh):
    weights = (
        P(None, "hid"),
        P(None, None, "hid"),
        P(None, "hid", None),
        P("hid", None),
        P(None, "hid"),
        P(),
        P(),
    )
    in_specs = (
        P("rows", None),
        P("rows", None),
        P("rows"),
        P(),
        P("rows", None),
        P("rows", None),
        P("rows", None),
    ) + weights * 3
    out_specs = (P(), P()) + weights * 3 + weights[:4]
    return jax.shard_map(body, mesh=mesh, in_specs=in_specs, out_specs=out_specs, check_vma=False)
```

```python
import functools

import jax
import jax.numpy as jnp
from jax import lax
from jax.experimental import pallas as pl
from jax.experimental.pallas import tpu as pltpu
from jax.sharding import PartitionSpec as P

STEP_COUNT = 5
MESH = pl.DeviceIdType.MESH
bf16 = jnp.bfloat16
f32 = jnp.float32
TILE = 512
PAD = 80
COLS = {"g1": 0, "g2": 128, "e1": 384, "e2": 896, "n1": 1152, "n2": 1664, "d1": 1920, "d2": 2432}
GROUPS = {"g": (0, 384), "e": (384, 768), "n": (1152, 768), "d": (1920, 640)}
PACK = 2560


def mm(left, right):
    return lax.dot_general(left, right, (((1,), (0,)), ((), ())), preferred_element_type=f32)


def mt(left, right):
    return lax.dot_general(left, right, (((1,), (1,)), ((), ())), preferred_element_type=f32)


def flip(values):
    return values.astype(f32).T.astype(bf16)


def split2(values):
    high = values.astype(bf16)
    low = (values - high.astype(f32)).astype(bf16)
    return high, low


def fold(values):
    total = values[:, :128]
    for at in range(128, values.shape[1], 128):
        total = total + values[:, at : at + 128]
    return total


def ones_at(index, base, rows):
    lanes = index.shape[1]
    local = lax.broadcasted_iota(jnp.int32, (256, lanes), 0).astype(f32).astype(bf16)
    parts = []
    for block in range(rows // 256):
        total = None
        for k in range(index.shape[0]):
            shifted = (index[k : k + 1] - (base + block * 256)).astype(f32).astype(bf16)
            hit = jnp.where(
                jnp.broadcast_to(shifted, (256, lanes)) == local,
                jnp.asarray(1, bf16),
                jnp.asarray(0, bf16),
            )
            total = hit if total is None else total + hit
        parts.append(total)
    return parts


def act_forward(pre):
    sigma = 0.5 * jnp.tanh(0.5 * pre) + 0.5
    act = pre * sigma
    return act.astype(bf16), sigma + act * (1.0 - sigma)


def norm_forward(values):
    size = values.shape[0]
    centre = values - jnp.sum(values, 0, keepdims=True) * (1.0 / size)
    var = jnp.sum(centre * centre, 0, keepdims=True) * (1.0 / size)
    scale = lax.rsqrt(var + 1e-05)
    return centre * scale, scale


def norm_backward(upstream, normed, scale, gain):
    size = upstream.shape[0]
    scaled = upstream * gain
    first = jnp.sum(scaled, 0, keepdims=True) * (1.0 / size)
    second = jnp.sum(scaled * normed, 0, keepdims=True) * (1.0 / size)
    return scale * (scaled - first - normed * second)


class Mail:
    def __init__(self, send, recv):
        self.send, self.recv, self.used = send, recv, 0

    def copy(self, source, target, device):
        at = self.used
        self.used += 1
        if self.send is None:
            return None
        copy = pltpu.make_async_remote_copy(
            src_ref=source,
            dst_ref=target,
            send_sem=self.send.at[at],
            recv_sem=self.recv.at[at],
            device_id=device,
            device_id_type=MESH,
        )
        copy.start()
        return copy


def count_copies(row_groups):
    near = min(row_groups, 8)
    far = row_groups // near
    sums = 3 + (row_groups - 1)
    rows_sum = 2 * (near - 1) + (far - 1)
    return 15 + 9 + 6 + 2 * sums + 4 * (3 + rows_sum)


def put(ref, at, values):
    for c in range(0, TILE, 128):
        ref[pl.ds(pl.multiple_of(at + 2 * c, 256), 256), :] = values[:, c : c + 128]


def take(ref, at):
    return jnp.concatenate(
        [ref[pl.ds(pl.multiple_of(at + 2 * c, 256), 256), :] for c in range(0, TILE, 128)], 1
    )


def main_kernel(
    live_ref,
    pick_ref,
    xt_hbm,
    tt_hbm,
    g2m_hbm,
    m2m_hbm,
    m2g_hbm,
    first_hbm,
    wide_hbm,
    second_hbm,
    last_hbm,
    hbias_hbm,
    norm_hbm,
    dbias_hbm,
    level_hbm,
    out_ref,
    all_ref,
    tot_ref,
    xt,
    tt,
    g2m_ref,
    m2m_ref,
    m2g_ref,
    first_f,
    last_f,
    hbias_f,
    norm_f,
    dbias_f,
    level_f,
    local_sem,
    square_tmp,
    norm_ref,
    chan_ref,
    big,
    x_ref,
    w,
    wt,
    bias,
    h0full,
    h1full,
    hgfull,
    onehot,
    spots,
    act_g,
    scale_g,
    dec_in,
    dp_d,
    ds_e,
    act_e,
    hs_e,
    nrm_e,
    scale_e,
    dsum,
    land_a,
    land_b,
    half_out,
    grad,
    gland_a,
    gland_b,
    held,
    rland,
    fland,
    nacc,
    cacc,
    h0_mine,
    node_in,
    mesh_tmp,
    small,
    sland_h,
    sland_r,
    narrow,
    nland_h,
    nland_r,
    send,
    recv,
    *,
    row_groups,
    g2m_deg,
    m2g_deg,
):
    hid = lax.axis_index("hid")
    row = lax.axis_index("rows")
    near = min(row_groups, 8)
    far = row_groups // near
    row_near = lax.rem(row, near)
    row_far = row // near
    core = hid + 1 - 2 * lax.rem(hid, 2)
    across = lax.rem(hid + 2, 4)
    corner = lax.rem(core + 2, 4)
    mail = Mail(send, recv)
    channels, grid_rows = xt.shape
    mine = x_ref.shape[1]
    share = h0_mine.shape[1]
    mesh_rows = h0full.shape[1]
    tiles = mine // TILE
    degree = m2m_ref.shape[0]
    latent = h0_mine.shape[0]

    def peer(device):
        return {"hid": device, "rows": row}

    def row_peer(device):
        return {"hid": hid, "rows": device}

    barrier = pltpu.get_barrier_semaphore()
    for device in (core, across, corner):
        pl.semaphore_signal(barrier, inc=1, device_id=peer(device), device_id_type=MESH)
    for step in range(1, row_groups):
        pl.semaphore_signal(
            barrier,
            inc=1,
            device_id=row_peer(lax.rem(row + step, row_groups)),
            device_id_type=MESH,
        )

    my_grid = pl.multiple_of(hid * mine, mine)
    pairs = (
        (first_hbm, first_f),
        (hbias_hbm, hbias_f),
        *((second_hbm.at[k], gland_a.at[1, :, pl.ds(256 * k, 256)]) for k in range(3)),
        *((wide_hbm.at[k], gland_a.at[0, :, pl.ds(512 * k, 512)]) for k in range(3)),
        (last_hbm, last_f),
        (xt_hbm, xt),
        (norm_hbm, norm_f),
        (dbias_hbm, dbias_f),
        (level_hbm, level_f),
        (tt_hbm.at[:, pl.ds(my_grid, mine)], tt),
        (m2m_hbm, m2m_ref),
        (m2g_hbm.at[:, pl.ds(my_grid, mine)], m2g_ref),
        (g2m_hbm, g2m_ref),
    )
    fetches = [
        pltpu.make_async_copy(source, target, local_sem.at[at])
        for at, (source, target) in enumerate(pairs)
    ]
    for fetch in fetches:
        fetch.start()

    def gather_start(view):
        near_copy = mail.copy(view(hid), view(hid), peer(core))
        far_copy = mail.copy(view(hid), view(hid), peer(across))
        return near_copy, far_copy

    def gather_pass(view, copies):
        near_copy, far_copy = copies
        far_copy.wait_recv()
        return near_copy, far_copy, mail.copy(view(across), view(across), peer(core))

    def gather_wait(copies):
        near_copy, far_copy, passed = copies
        near_copy.wait_recv()
        passed.wait_recv()
        near_copy.wait_send()
        far_copy.wait_send()
        passed.wait_send()

    def rows_of(ref, block, size, start=0, width=None):
        width = ref.shape[1] if width is None else width
        return ref.at[pl.ds(pl.multiple_of(block * size, size), size), pl.ds(start, width)]

    def lanes_of(ref, block, size):
        return ref.at[:, pl.ds(pl.multiple_of(block * size, size), size)]

    own_rows = pl.ds(pl.multiple_of(hid * 64, 64), 64)
    square_tmp[...] = jnp.zeros_like(square_tmp)
    for fetch in fetches[:5]:
        fetch.wait()
    square_tmp[0:64, 0:channels] = first_f[...]
    w[own_rows, 0:128] = square_tmp[0:64, :].astype(bf16)
    square_tmp[...] = jnp.zeros_like(square_tmp)
    square_tmp[0:4, 0:64] = hbias_f[...]
    bias[own_rows, :] = square_tmp[...].T[:64]
    for layer, name in enumerate(("g2", "e2", "n2")):
        w[own_rows, COLS[name] : COLS[name] + 256] = gland_a[1, :, 256 * layer : 256 * layer + 256].astype(bf16)
    for fetch in fetches[5:9]:
        fetch.wait()
    for layer, name in enumerate(("e1", "n1", "d1")):
        w[own_rows, COLS[name] : COLS[name] + 512] = gland_a[0, :, 512 * layer : 512 * layer + 512].astype(bf16)
    square_tmp[...] = jnp.zeros_like(square_tmp)
    square_tmp[0:64, 0:channels] = last_f[...]
    w[own_rows, COLS["d2"] : COLS["d2"] + 128] = square_tmp[0:64, :].astype(bf16)
    pl.semaphore_wait(barrier, 3 + row_groups - 1)
    flights = {}
    for name in "gend":
        start, width = GROUPS[name]
        view = functools.partial(rows_of, w, size=64, start=start, width=width)
        flights[name] = gather_start(lambda block, view=view: view(block))
        if name == "g":
            flights["b"] = gather_start(lambda block: rows_of(bias, block, 64))

    def weights_pass(name):
        if name == "b":
            flights[name] = gather_pass(lambda block: rows_of(bias, block, 64), flights[name])
            return
        start, width = GROUPS[name]
        flights[name] = gather_pass(
            lambda block: rows_of(w, block, 64, start, width), flights[name]
        )

    for fetch in fetches[9:]:
        fetch.wait()

    def padded(values, to):
        return jnp.concatenate(
            [values.astype(f32), jnp.zeros((to - channels, values.shape[1]), f32)], 0
        )

    def turn(i, carry):
        at = pl.multiple_of(i * TILE, TILE)
        big[pl.ds(at, TILE), :] = padded(xt[:, pl.ds(at, TILE)], 128).T
        return carry

    lax.fori_loop(0, grid_rows // TILE, turn, 0)
    step_rows = 16
    for block in range(g2m_deg * share // 256):
        k, start = block * 256 // share, block * 256 % share

        def pick(i, carry):
            for u in range(step_rows):
                nacc[block, pl.ds(i * step_rows + u, 1), :] = big[
                    pl.ds(pick_ref[k, hid * share + start + i * step_rows + u], 1), :
                ]
            return carry

        lax.fori_loop(0, 256 // step_rows, pick, 0)

    def unpick(i, carry):
        at = pl.multiple_of(i * TILE, TILE)
        for half in range(2):
            there = pl.ds(pl.multiple_of(at + half * 256, 256), 256)
            dp_d[:PAD, there] = nacc[2 * i + half].T[:PAD].astype(bf16)
        x_ref[:, pl.ds(at, TILE)] = padded(
            xt[:, pl.ds(pl.multiple_of(my_grid + at, TILE), TILE)], PAD
        ).astype(bf16)
        return carry

    lax.fori_loop(0, tiles, unpick, 0)
    square_tmp[...] = jnp.zeros_like(square_tmp)
    for layer in range(3):
        square_tmp[2 * layer : 2 * layer + 2, :] = norm_f[layer][:, :128]
    norm_ref[:128, :] = square_tmp[...].T
    for layer in range(3):
        square_tmp[2 * layer : 2 * layer + 2, :] = norm_f[layer][:, 128:]
    norm_ref[128:, :] = square_tmp[...].T
    square_tmp[...] = jnp.zeros_like(square_tmp)
    square_tmp[0:1, 0:channels] = dbias_f[...]
    square_tmp[1:2, 0:channels] = level_f[...].astype(f32)
    chan_ref[...] = square_tmp[...].T[:PAD]

    for name in "gb":
        weights_pass(name)
    gather_wait(flights["g"])
    gather_wait(flights["b"])
    b_g, b_e, b_n, b_d = (bias[:, k : k + 1] for k in range(4))
    gains = [norm_ref[:, 2 * k : 2 * k + 1] for k in range(3)]
    shifts = [norm_ref[:, 2 * k + 1 : 2 * k + 2] for k in range(3)]
    wt[:, 0:256] = flip(w[:, COLS["g2"] : COLS["g2"] + 256])
    w1g = w[:, 0:128][:, :PAD]

    def embed(inputs):
        pre = mm(w1g, inputs) + b_g
        act, slope = act_forward(pre)
        normed, scale = norm_forward(mm(wt[:, 0:256], act))
        return act, slope, normed, scale

    mesh_tmp[0] = jnp.zeros((latent, share), f32)

    def pool(i, carry):
        here = pl.ds(pl.multiple_of(i * TILE, TILE), TILE)
        mesh_tmp[0] += embed(dp_d[:PAD, here])[2] * gains[0] + shifts[0]
        return carry

    lax.fori_loop(0, g2m_deg, pool, 0)
    h0_mine[...] = mesh_tmp[0] * (1.0 / g2m_deg)
    my_mesh = pl.ds(pl.multiple_of(hid * share, share), share)
    h0_half = h0_mine[...].astype(bf16)
    h0full[:, my_mesh] = h0_half
    node_in[:latent, :] = h0_half
    h0_view = functools.partial(lanes_of, h0full, size=share)
    h0_flight = gather_start(lambda block: h0_view(block))

    lane = lax.broadcasted_iota(jnp.int32, (1, TILE), 1)
    first_row = hid * mine

    def live_mask(i):
        return (first_row + i * TILE + lane < live_ref[0]).astype(f32)

    cacc[...] = jnp.zeros_like(cacc)

    def squares(i, carry):
        here = pl.ds(pl.multiple_of(i * TILE, TILE), TILE)
        delta = (padded(tt[:, here], PAD) - x_ref[:, here].astype(f32)) * live_mask(i)
        cacc[0] += fold(delta * delta)
        return carry

    lax.fori_loop(0, tiles, squares, 0)
    col = lax.broadcasted_iota(jnp.int32, (PAD, 128), 1)
    live_here = jnp.clip(live_ref[0] - first_row, 0, mine).astype(f32)
    square_tmp[...] = jnp.zeros_like(square_tmp)
    square_tmp[:PAD, :] = jnp.where(
        col == 0, jnp.sum(cacc[0], 1, keepdims=True), jnp.where(col == 1, live_here, 0.0)
    )
    small[...] = square_tmp[...].T[:8]
    sum_hid = [
        mail.copy(small, sland_h.at[slot], peer(device))
        for slot, device in enumerate((core, across, corner))
    ]

    def own(i, carry):
        here = pl.ds(pl.multiple_of(i * TILE, TILE), TILE)
        act, slope, normed, scale = embed(x_ref[:, here])
        put(big, 2 * i * 2 * TILE, slope)
        act_g[:, here] = act
        put(big, (2 * i + 1) * 2 * TILE, normed)
        scale_g[:, here] = scale
        dec_in[:latent, here] = (normed * gains[0] + shifts[0]).astype(bf16)
        return carry

    def own_range(a, b):
        lax.fori_loop(a, b, own, 0)

    own_range(0, tiles // 2)
    h0_flight = gather_pass(lambda block: h0_view(block), h0_flight)
    weights_pass("e")
    weights_pass("n")
    weights_pass("d")
    for copy in sum_hid:
        copy.wait()
    small[...] = small[...] + sland_h[0] + sland_h[1] + sland_h[2]
    sum_rows = [
        mail.copy(small, sland_r.at[step - 1], row_peer(lax.rem(row + step, row_groups)))
        for step in range(1, row_groups)
    ]
    own_range(tiles // 2, tiles)
    for name in "end":
        gather_wait(flights[name])
    wt[:, 256:512] = flip(w[:, COLS["e2"] : COLS["e2"] + 256])
    wt[:, 512:768] = flip(w[:, COLS["n2"] : COLS["n2"] + 256])
    wt[:128, 768:1024] = flip(w[:, COLS["d2"] : COLS["d2"] + 128])
    gather_wait(h0_flight)

    e1 = COLS["e1"]
    mesh_tmp[0] = mm(w[:, e1 : e1 + 256], node_in[:latent, :]) + b_e
    mesh_tmp[1] = jnp.zeros((latent, share), f32)

    def edge_index(k):
        return m2m_ref[pl.ds(k, 1), my_mesh]

    def fill(index, base, rows):
        for block, part in enumerate(ones_at(index, base, rows)):
            onehot[block * 256 : block * 256 + 256, :] = part

    def edge(k, carry):
        fill(edge_index(k), 0, mesh_rows)
        sent = mm(h0full[...], onehot[...]).astype(bf16)
        hs_e[k] = sent
        pre = mesh_tmp[0] + mm(w[:, e1 + 256 : e1 + 512], sent)
        act, slope = act_forward(pre)
        act_e[k] = act
        ds_e[k] = slope
        normed, scale = norm_forward(mm(wt[:, 256:512], act))
        nrm_e[k] = normed
        scale_e[pl.ds(k, 1), :] = scale
        mesh_tmp[1] += normed * gains[1] + shifts[1]
        return carry

    lax.fori_loop(0, degree, edge, 0)

    n1 = COLS["n1"]
    node_in[latent:, :] = mesh_tmp[1].astype(bf16)
    act_n, slope_n = act_forward(mm(w[:, n1 : n1 + 512], node_in[...]) + b_n)
    normed_n, scale_n = norm_forward(mm(wt[:, 512:768], act_n))
    h1 = h0_mine[...] + (normed_n * gains[2] + shifts[2])
    ds_e[degree] = slope_n
    act_e[degree] = act_n
    nrm_e[degree] = normed_n
    scale_e[degree : degree + 1, :] = scale_n
    h1full[:, my_mesh] = h1.astype(bf16)
    h1_view = functools.partial(lanes_of, h1full, size=share)
    h1_flight = gather_start(lambda block: h1_view(block))

    for copy in sum_rows:
        copy.wait()
    totals = small[...]
    for step in range(1, row_groups):
        totals = totals + sland_r[step - 1]
    square_tmp[...] = jnp.zeros_like(square_tmp)
    square_tmp[:8, :] = totals
    totals = square_tmp[...].T[:PAD]
    count = totals[:, 1:2]
    var = totals[:, 0:1] / count + 1e-06
    d_bias = chan_ref[:, 0:1]
    level = chan_ref[:, 1:2]
    loss_weight = count * jnp.sum(level, 0, keepdims=True)
    tot_ref[...] = jnp.broadcast_to(loss_weight[:8], (8, 128))
    weight_var = level / var
    pull = 2.0 * weight_var / loss_weight
    nacc[...] = jnp.zeros_like(nacc)
    cacc[...] = jnp.zeros_like(cacc)
    grad[...] = jnp.zeros_like(grad)
    dsum[...] = jnp.zeros_like(dsum)


    def spot(i, write):
        base = my_grid + i * TILE
        for at in range(0, mesh_rows, TILE):
            for block, part in enumerate(ones_at(g2m_ref[:, at : at + TILE], base, TILE)):
                write(block, at, part)

    def spot_store(i, carry):
        def write(block, at, part):
            spots[i, block * 256 : block * 256 + 256, at : at + TILE] = part

        spot(i, write)
        return carry

    ready = spots.shape[0]
    lax.fori_loop(0, ready - 1, spot_store, 0)
    h1_flight = gather_pass(lambda block: h1_view(block), h1_flight)
    lax.fori_loop(ready - 1, ready, spot_store, 0)
    gather_wait(h1_flight)

    def chunk(start, width, block):
        return rows_of(grad, block, 64, start, width)

    def reduce_start(name):
        start, width = GROUPS[name]
        flight = (
            mail.copy(
                chunk(start, width, corner), gland_a.at[1, :, pl.ds(start, width)], peer(core)
            ),
            mail.copy(
                chunk(start, width, core), gland_a.at[0, :, pl.ds(start, width)], peer(core)
            ),
        )
        return flight

    def reduce_across(name, flight):
        start, width = GROUPS[name]
        cols = pl.ds(start, width)
        flight[0].wait()
        view = chunk(start, width, across)
        view[...] = view[...] + gland_a[1, :, cols]
        return flight + (mail.copy(view, gland_b.at[:, cols], peer(across)),)

    def reduce_rows(name, flight):
        start, width = GROUPS[name]
        cols = pl.ds(start, width)
        flight[1].wait()
        flight[2].wait()
        part = 64 // near
        held[:, cols] = chunk(start, width, hid)[...] + gland_a[0, :, cols] + gland_b[:, cols]
        copies = []
        for step in range(1, near):
            to = lax.rem(row_near + step, near)
            copies.append(
                mail.copy(
                    held.at[pl.ds(pl.multiple_of(to * part, part), part), cols],
                    rland.at[step - 1, :, cols],
                    row_peer(row_far * near + to),
                )
            )
        return copies

    def reduce_share(name, copies):
        start, width = GROUPS[name]
        cols = pl.ds(start, width)
        part = 64 // near
        shared = pl.ds(pl.multiple_of(row_near * part, part), part)
        own_part = out_ref.at[shared, cols]
        for copy in copies:
            copy.wait()
        total = held[shared, cols]
        for step in range(1, near):
            total = total + rland[step - 1, :, cols]
        if far > 1:
            own_part[...] = total
            more = []
            for step in range(1, far):
                to = lax.rem(row_far + step, far)
                more.append(
                    mail.copy(
                        own_part,
                        fland.at[step - 1, :, cols],
                        row_peer(to * near + row_near),
                    )
                )
            for copy in more:
                copy.wait()
            for step in range(1, far):
                total = total + fland[step - 1, :, cols]
        own_part[...] = total
        out = []
        for step in range(1, near):
            to = lax.rem(row_near + step, near)
            out.append(mail.copy(own_part, own_part, row_peer(row_far * near + to)))
        return out

    d1, d2 = COLS["d1"], COLS["d2"]
    def decode(i, carry):
        here = pl.ds(pl.multiple_of(i * TILE, TILE), TILE)
        fill(m2g_ref[:, here], 0, mesh_rows)
        back = mm(h1full[...], onehot[...]) * (1.0 / m2g_deg)
        dec_in[latent:, here] = back.astype(bf16)
        pre = mm(w[:, d1 : d1 + 512], dec_in[:, here]) + b_d
        act, slope = act_forward(pre)
        out = mm(wt[:128, 768:1024], act)[:PAD]
        err = x_ref[:, here].astype(f32) + out + d_bias - padded(tt[:, here], PAD)
        kept = err * live_mask(i)
        cacc[1] += fold(weight_var * kept * err)
        pred_grad = pull * kept
        cacc[0] += fold(pred_grad)
        upstream = pred_grad.astype(bf16)
        act_grad = mm(w[:, d2 : d2 + 128][:, :PAD], upstream)
        pre_grad = (act_grad * slope).astype(bf16)
        dp_d[:, here] = pre_grad
        dsum[...] += mt(pre_grad, onehot[...])
        grad[:, d2 : d2 + PAD] += mt(act, upstream)
        return carry

    lax.fori_loop(0, tiles, decode, 0)

    def spread_start(view, land):
        return (
            mail.copy(view(corner), land.at[1], peer(core)),
            mail.copy(view(core), land.at[0], peer(core)),
        )

    def spread_across(view, land, land_far, out, copies):
        copies[0].wait()
        out[...] = (view(across)[...] + land[1]).astype(bf16)
        return copies + (mail.copy(out, land_far, peer(across)),)

    def spread_end(view, land, land_far, copies):
        copies[1].wait()
        copies[2].wait()
        return view(hid)[...] + land[0] + land_far[...].astype(f32)

    d_view = functools.partial(lanes_of, dsum, size=share)

    def view_d(block):
        return d_view(block)

    d_flight = spread_start(view_d, land_a.at[0])
    w1d_low = flip(w[:, d1 : d1 + 256])
    wt[:, 1024:1280] = w1d_low
    d_flight = spread_across(view_d, land_a.at[0], land_b.at[0], half_out, d_flight)

    def decode_rest(i, carry):
        here = pl.ds(pl.multiple_of(i * TILE, TILE), TILE)
        pre_grad = dp_d[:, here]
        grad[:, d1 : d1 + 512] += mt(pre_grad, dec_in[:, here])
        nacc[9] += fold(pre_grad.astype(f32))
        return carry

    lax.fori_loop(0, tiles, decode_rest, 0)
    stage = {"d": reduce_start("d")}
    wt[:, 2304:2560] = flip(w[:, d1 + 256 : d1 + 512])
    wt[:, 1280:1536] = flip(w[:, n1 : n1 + 256])
    wt[:, 1536:1792] = flip(w[:, n1 + 256 : n1 + 512])
    wt[:, 1792:2048] = flip(w[:, e1 : e1 + 256])
    wt[:, 2048:2304] = flip(w[:, e1 + 256 : e1 + 512])

    def write_late(start):
        def write(block, at, part):
            dec_in[block * 256 : block * 256 + 256, start + at : start + at + TILE] = part

        return write

    def write_last(block, at, part):
        (h0full, h1full)[block][:, at : at + TILE] = part

    spot(ready, write_late(0))
    spot(ready + 1, write_late(mesh_rows))
    spot(ready + 2, write_last)

    high, low = split2(spread_end(view_d, land_a.at[0], land_b.at[0], d_flight))
    stage["d"] = reduce_across("d", stage["d"])
    h1_grad = (mm(wt[:, 2304:2560], high) + mm(wt[:, 2304:2560], low)) * (1.0 / m2g_deg)
    nacc[2] += fold(h1_grad * nrm_e[degree])
    nacc[5] += fold(h1_grad)
    up_n = norm_backward(
        h1_grad, nrm_e[degree], scale_e[degree : degree + 1, :], gains[2]
    ).astype(bf16)
    n2 = COLS["n2"]
    pre_grad_n = (mm(w[:, n2 : n2 + 256], up_n) * ds_e[degree]).astype(bf16)
    mesh_tmp[0] = h1_grad + mm(wt[:, 1280:1536], pre_grad_n)
    mesh_tmp[1] = mm(wt[:, 1536:1792], pre_grad_n)

    e2 = COLS["e2"]

    def edge_back(k, carry):
        upstream = mesh_tmp[1]
        normed = nrm_e[k]
        nacc[1] += fold(upstream * normed)
        nacc[4] += fold(upstream)
        up = norm_backward(upstream, normed, scale_e[pl.ds(k, 1), :], gains[1]).astype(bf16)
        pre_grad = (mm(w[:, e2 : e2 + 256], up) * ds_e[k]).astype(bf16)
        mesh_tmp[0] += mm(wt[:, 1792:2048], pre_grad)
        grad[:, e2 : e2 + 256] += mt(act_e[k], up)
        act_e[k] = pre_grad
        nacc[7] += fold(pre_grad.astype(f32))
        return carry

    lax.fori_loop(0, degree, edge_back, 0)

    def senders(block):
        total = None
        for k in range(degree):
            place = k % 4 * TILE
            for half, part in enumerate(ones_at(edge_index(k), block * share, share)):
                onehot[place + half * 256 : place + half * 256 + 256, :] = part
            term = mt(act_e[k], onehot[place : place + TILE, :])
            total = term if total is None else total + term
        view_d(block)[...] = total

    senders(corner)
    e_first = mail.copy(view_d(corner), land_a.at[1, 1], peer(core))
    senders(core)
    e_flight = (e_first, mail.copy(view_d(core), land_a.at[1, 0], peer(core)))
    stage["d"] = reduce_rows("d", stage["d"])
    senders(across)
    e_flight = spread_across(view_d, land_a.at[1], land_b.at[1], half_out, e_flight)
    senders(hid)
    high, low = split2(spread_end(view_d, land_a.at[1], land_b.at[1], e_flight))
    h0_grad = mesh_tmp[0] + mm(wt[:, 2048:2304], high) + mm(wt[:, 2048:2304], low)
    hgfull[:, my_mesh] = (h0_grad * (1.0 / g2m_deg)).astype(bf16)
    hg_view = functools.partial(lanes_of, hgfull, size=share)
    hg_flight = gather_start(lambda block: hg_view(block))

    grad[:, n2 : n2 + 256] = mt(act_e[degree], up_n)
    grad[:, n1 : n1 + 512] = mt(pre_grad_n, node_in[...])
    nacc[8] += fold(pre_grad_n.astype(f32))
    stage["n"] = reduce_start("n")

    def edge_weights(k, carry):
        grad[:, e1 : e1 + 256] += mt(act_e[k], node_in[:latent, :])
        grad[:, e1 + 256 : e1 + 512] += mt(act_e[k], hs_e[k])
        return carry

    lax.fori_loop(0, degree // 2, edge_weights, 0)
    hg_flight = gather_pass(lambda block: hg_view(block), hg_flight)
    stage["n"] = reduce_across("n", stage["n"])
    lax.fori_loop(degree // 2, degree, edge_weights, 0)
    stage["e"] = reduce_start("e")
    stage["d"] = reduce_share("d", stage["d"])
    stage["e"] = reduce_across("e", stage["e"])
    gather_wait(hg_flight)

    def grid_back(i, both):
        here = pl.ds(pl.multiple_of(i * TILE, TILE), TILE)
        upstream = mm(wt[:, 1024:1280], dp_d[:, here]) + both
        normed = take(big, (2 * i + 1) * 2 * TILE)
        nacc[0] += fold(upstream * normed)
        nacc[3] += fold(upstream)
        up = norm_backward(upstream, normed, scale_g[:, here], gains[0]).astype(bf16)
        pre_grad = (mm(w[:, COLS["g2"] : COLS["g2"] + 256], up) * take(big, 2 * i * 2 * TILE)).astype(bf16)
        grad[:, COLS["g2"] : COLS["g2"] + 256] += mt(act_g[:, here], up)
        grad[:, 0:PAD] += mt(pre_grad, x_ref[:, here])
        nacc[6] += fold(pre_grad.astype(f32))

    def grid_ready(i, carry):
        grid_back(i, mt(hgfull[...], spots[i]))
        return carry

    def grid_late(i, carry):
        def write(block, at, part):
            onehot[at + block * 256 : at + block * 256 + 256, :] = part

        spot(i, write)
        both = mt(hgfull[:, 0:TILE], onehot[0:TILE, :])
        for at in range(TILE, mesh_rows, TILE):
            both = both + mt(hgfull[:, at : at + TILE], onehot[at : at + TILE, :])
        grid_back(i, both)
        return carry

    lax.fori_loop(0, ready, grid_ready, 0)
    for name in "ne":
        stage[name] = reduce_rows(name, stage[name])
    for half in range(2):
        grid_back(ready + half, mt(hgfull[...], dec_in[:, half * mesh_rows : (half + 1) * mesh_rows]))
    grid_back(ready + 2, jnp.concatenate([mt(hgfull[...], h0full[...]), mt(hgfull[...], h1full[...])], 1))
    lax.fori_loop(ready + 3, tiles, grid_late, 0)

    block = grad[:, 0:128]
    at_col = lax.broadcasted_iota(jnp.int32, (latent, 128), 1)
    for k in range(4):
        block = jnp.where(at_col == PAD + k, jnp.sum(nacc[6 + k], 1, keepdims=True), block)
    grad[:, 0:128] = block
    stage["g"] = reduce_start("g")
    block = jnp.zeros((latent, 128), f32)
    for k in range(6):
        block = jnp.where(at_col == 2 * (k % 3) + k // 3, jnp.sum(nacc[k], 1, keepdims=True), block)
    norm_ref[...] = block
    block = norm_ref[:PAD, :]
    for k in range(2):
        block = jnp.where(col == 6 + k, jnp.sum(cacc[k], 1, keepdims=True), block)
    norm_ref[:PAD, :] = block
    narrow[...] = norm_ref[...].T[:8]
    narrow_hid = [
        mail.copy(narrow, nland_h.at[slot], peer(device))
        for slot, device in enumerate((core, across, corner))
    ]
    stage["g"] = reduce_across("g", stage["g"])
    for name in "ne":
        stage[name] = reduce_share(name, stage[name])
    for copy in narrow_hid:
        copy.wait()
    narrow[...] = narrow[...] + nland_h[0] + nland_h[1] + nland_h[2]
    narrow_rows = [
        mail.copy(narrow, nland_r.at[step - 1], row_peer(lax.rem(row + step, row_groups)))
        for step in range(1, row_groups)
    ]
    stage["g"] = reduce_rows("g", stage["g"])
    stage["g"] = reduce_share("g", stage["g"])
    for copy in narrow_rows:
        copy.wait()
    total = narrow[...]
    for step in range(1, row_groups):
        total = total + nland_r[step - 1]
    all_ref[...] = total
    for name in "dneg":
        for copy in stage[name]:
            copy.wait()


def adam_step(weight, avg, sq, grad, rate, decay):
    avg_new = 0.5 * avg + 0.5 * grad
    sq_new = 0.5 * sq + 0.5 * grad * grad
    fix = 1.0 - 0.5**STEP_COUNT
    step = avg_new / fix / (jnp.sqrt(sq_new / fix) + 1e-08)
    return (weight - rate * (step + decay * weight), avg_new, sq_new)


def adam_kernel(out_ref, all_ref, tot_ref, *refs):
    ins_hbm, outs_hbm, loss_ref, weight_ref = refs[:21], refs[21:46], refs[46], refs[47]
    ins, outs, turned, sem_in, sem_out = refs[48:69], refs[69:94], refs[94], refs[95], refs[96]
    fetches = [
        pltpu.make_async_copy(source, target, sem_in.at[at])
        for at, (source, target) in enumerate(zip(ins_hbm, ins))
    ]
    for fetch in fetches:
        fetch.start()
    stores = []

    def arrive(array):
        for part in (array, 7 + array, 14 + array):
            fetches[part].wait()

    def leave(array):
        for part in (array, 7 + array, 14 + array) + ((21 + array,) if array < 4 else ()):
            store = pltpu.make_async_copy(outs[part], outs_hbm[part], sem_out.at[part])
            store.start()
            stores.append(store)

    def update(array, at, grad, rate, decay):
        fresh, avg_new, sq_new = adam_step(
            ins[array][at], ins[7 + array][at], ins[14 + array][at], grad, rate, decay
        )
        outs[array][at] = fresh
        outs[7 + array][at] = avg_new
        outs[14 + array][at] = sq_new
        if array < 4:
            outs[21 + array][at] = fresh.astype(bf16)

    everything = (slice(None), slice(None))
    channels = ins[0].shape[1]
    arrive(1)
    for layer, name in enumerate(("e1", "n1", "d1")):
        update(1, (layer,) + everything, out_ref[:, COLS[name] : COLS[name] + 512], 0.05, 0.1)
    leave(1)
    arrive(2)
    for layer, name in enumerate(("g2", "e2", "n2")):
        update(2, (layer,) + everything, out_ref[:, COLS[name] : COLS[name] + 256], 0.05, 0.1)
    leave(2)
    arrive(0)
    update(0, everything, out_ref[:, 0:128][:, :channels], 0.05, 0.1)
    leave(0)
    arrive(3)
    update(3, everything, out_ref[:, COLS["d2"] : COLS["d2"] + 128][:, :channels], 0.05, 0.1)
    leave(3)
    turned[...] = out_ref[:, 0:128].T
    arrive(4)
    update(4, everything, turned[PAD : PAD + 4, :], 0.3, 0.0)
    leave(4)
    arrive(5)
    for layer in range(3):
        update(5, (layer,) + everything, all_ref[2 * layer : 2 * layer + 2, :], 0.3, 0.0)
    leave(5)
    arrive(6)
    update(6, everything, all_ref[6:7, 0:channels], 0.3, 0.0)
    leave(6)
    loss_ref[...] = jnp.sum(all_ref[7:8, 0:PAD], 1, keepdims=True)
    weight_ref[...] = tot_ref[0:1, 0:1]
    for store in stores:
        store.wait()


def body(
    grid_input,
    grid_target,
    live_points,
    level_weight,
    g2m_index,
    m2m_index,
    m2g_index,
    *params,
):
    groups = lax.axis_size("hid")
    row_groups = lax.axis_size("rows")
    masters, avgs, squares = params[:7], params[7:14], params[14:21]
    grid_rows, channels = grid_input.shape
    mesh_rows, degree = m2m_index.shape
    latent = masters[5].shape[2]
    share = mesh_rows // groups
    mine = grid_rows // groups
    g2m_deg = g2m_index.shape[1]
    m2g_deg = m2g_index.shape[1]
    whole = pl.BlockSpec(memory_space=pltpu.VMEM)
    scalar = pl.BlockSpec(memory_space=pltpu.SMEM)
    far_memory = pl.BlockSpec(memory_space=pltpu.HBM)
    g2m = g2m_index.T

    def flat(arrays):
        first, wide, second, last, bias, norm, out_bias = arrays
        return (
            first.T,
            wide.transpose(0, 2, 1),
            second,
            last,
            bias,
            norm.transpose(1, 0, 2),
            out_bias[None],
        )

    operands = flat(masters) + flat(avgs) + flat(squares)
    loads = [
        grid_input.T,
        grid_target.T,
        g2m,
        m2m_index.T,
        m2g_index.T,
        *operands[:7],
        level_weight[None],
    ]
    kept = [jax.ShapeDtypeStruct(v.shape, v.dtype) for v in loads]
    for at in (1, 4):
        kept[at] = jax.ShapeDtypeStruct((kept[at].shape[0], mine), kept[at].dtype)
    copies = count_copies(row_groups)
    near = min(row_groups, 8)
    far = row_groups // near
    summed, spare, totals = pl.pallas_call(
        functools.partial(
            main_kernel, row_groups=row_groups, g2m_deg=g2m_deg, m2g_deg=m2g_deg
        ),
        out_shape=[
            jax.ShapeDtypeStruct((64, PACK), f32),
            jax.ShapeDtypeStruct((8, 256), f32),
            jax.ShapeDtypeStruct((8, 128), f32),
        ],
        in_specs=[scalar] * 2 + [far_memory] * 13,
        out_specs=[whole] * 3,
        scratch_shapes=[pltpu.VMEM(v.shape, v.dtype) for v in kept[:6] + kept[8:]]
        + [
            pltpu.SemaphoreType.DMA((17,)),
            pltpu.VMEM((128, 128), f32),
            pltpu.VMEM((latent, 128), f32),
            pltpu.VMEM((PAD, 128), f32),
            pltpu.VMEM((grid_rows, 128), f32),
            pltpu.VMEM((PAD, mine), bf16),
            pltpu.VMEM((256, PACK), bf16),
            pltpu.VMEM((256, 2560), bf16),
            pltpu.VMEM((256, 128), f32),
            pltpu.VMEM((latent, mesh_rows), bf16),
            pltpu.VMEM((latent, mesh_rows), bf16),
            pltpu.VMEM((latent, mesh_rows), bf16),
            pltpu.VMEM((mesh_rows, TILE), bf16),
            pltpu.VMEM((3, TILE, mesh_rows), bf16),
            pltpu.VMEM((latent, mine), bf16),
            pltpu.VMEM((1, mine), f32),
            pltpu.VMEM((2 * latent, mine), bf16),
            pltpu.VMEM((latent, mine), bf16),
            pltpu.VMEM((degree + 1, latent, share), f32),
            pltpu.VMEM((degree + 1, latent, share), bf16),
            pltpu.VMEM((degree, latent, share), bf16),
            pltpu.VMEM((degree + 1, latent, share), f32),
            pltpu.VMEM((8, share), f32),
            pltpu.VMEM((latent, mesh_rows), f32),
            pltpu.VMEM((2, 2, latent, share), f32),
            pltpu.VMEM((2, latent, share), bf16),
            pltpu.VMEM((latent, share), bf16),
            pltpu.VMEM((256, PACK), f32),
            pltpu.VMEM((2, 64, PACK), f32),
            pltpu.VMEM((64, PACK), f32),
            pltpu.VMEM((64, PACK), f32),
            pltpu.VMEM((near - 1, 64 // near, PACK), f32),
            pltpu.VMEM((max(far - 1, 1), 64 // near, PACK), f32),
            pltpu.VMEM((g2m_deg * share // 256, 256, 128), f32),
            pltpu.VMEM((2, PAD, 128), f32),
            pltpu.VMEM((latent, share), f32),
            pltpu.VMEM((2 * latent, share), bf16),
            pltpu.VMEM((2, latent, share), f32),
            pltpu.VMEM((8, 128), f32),
            pltpu.VMEM((3, 8, 128), f32),
            pltpu.VMEM((row_groups - 1, 8, 128), f32),
            pltpu.VMEM((8, 256), f32),
            pltpu.VMEM((3, 8, 256), f32),
            pltpu.VMEM((row_groups - 1, 8, 256), f32),
            pltpu.SemaphoreType.DMA((copies,)),
            pltpu.SemaphoreType.DMA((copies,)),
        ],
        compiler_params=pltpu.CompilerParams(
            collective_id=0, has_side_effects=True, vmem_limit_bytes=64 * 2**20
        ),
        name="step",
    )(
        live_points,
        g2m,
        *loads,
    )
    shapes = [jax.ShapeDtypeStruct(v.shape, f32) for v in operands]
    shapes += [jax.ShapeDtypeStruct(v.shape, bf16) for v in operands[:4]]
    outs = pl.pallas_call(
        adam_kernel,
        out_shape=shapes + [jax.ShapeDtypeStruct((1, 1), f32)] * 2,
        in_specs=[whole] * 3 + [far_memory] * 21,
        out_specs=[far_memory] * 25 + [whole] * 2,
        scratch_shapes=[pltpu.VMEM(v.shape, v.dtype) for v in operands + tuple(shapes)]
        + [
            pltpu.VMEM((128, 64), f32),
            pltpu.SemaphoreType.DMA((21,)),
            pltpu.SemaphoreType.DMA((25,)),
        ],
        compiler_params=pltpu.CompilerParams(vmem_limit_bytes=64 * 2**20),
        name="adam",
    )(summed, spare, totals, *operands)

    def unflat(arrays):
        first, wide, second, last, bias, norm, out_bias = arrays
        return (
            first.T,
            wide.transpose(0, 2, 1),
            second,
            last,
            bias,
            norm.transpose(1, 0, 2),
            out_bias[0],
        )

    halves = outs[21:25]
    return (
        (outs[25][0, 0], outs[26][0, 0])
        + unflat(outs[0:7])
        + unflat(outs[7:14])
        + unflat(outs[14:21])
        + (halves[0].T, halves[1].transpose(0, 2, 1), halves[2], halves[3])
    )


def solution(mesh):
    weights = (
        P(None, "hid"),
        P(None, None, "hid"),
        P(None, "hid", None),
        P("hid", None),
        P(None, "hid"),
        P(),
        P(),
    )
    in_specs = (
        P("rows", None),
        P("rows", None),
        P("rows"),
        P(),
        P("rows", None),
        P("rows", None),
        P("rows", None),
    ) + weights * 3
    out_specs = (P(), P()) + weights * 3 + weights[:4]
    return jax.shard_map(body, mesh=mesh, in_specs=in_specs, out_specs=out_specs, check_vma=False)
```

```python
import functools

import jax
import jax.numpy as jnp
from jax import lax
from jax.experimental import pallas as pl
from jax.experimental.pallas import tpu as pltpu
from jax.sharding import PartitionSpec as P

STEP_COUNT = 5
MESH = pl.DeviceIdType.MESH
bf16 = jnp.bfloat16
f32 = jnp.float32
TILE = 512
PAD = 80
COLS = {"g1": 0, "g2": 128, "e1": 384, "e2": 896, "n1": 1152, "n2": 1664, "d1": 1920, "d2": 2432}
GROUPS = {"g": (0, 384), "e": (384, 768), "n": (1152, 768), "d": (1920, 640)}
PACK = 2560


def mm(left, right):
    return lax.dot_general(left, right, (((1,), (0,)), ((), ())), preferred_element_type=f32)


def mt(left, right):
    return lax.dot_general(left, right, (((1,), (1,)), ((), ())), preferred_element_type=f32)


def flip(values):
    return values.astype(f32).T.astype(bf16)


def split2(values):
    high = values.astype(bf16)
    low = (values - high.astype(f32)).astype(bf16)
    return high, low


def fold(values):
    total = values[:, :128]
    for at in range(128, values.shape[1], 128):
        total = total + values[:, at : at + 128]
    return total


def ones_at(index, base, rows):
    lanes = index.shape[1]
    local = lax.broadcasted_iota(jnp.int32, (256, lanes), 0).astype(f32).astype(bf16)
    parts = []
    for block in range(rows // 256):
        total = None
        for k in range(index.shape[0]):
            shifted = (index[k : k + 1] - (base + block * 256)).astype(f32).astype(bf16)
            hit = jnp.where(
                jnp.broadcast_to(shifted, (256, lanes)) == local,
                jnp.asarray(1, bf16),
                jnp.asarray(0, bf16),
            )
            total = hit if total is None else total + hit
        parts.append(total)
    return parts


def act_forward(pre):
    sigma = 0.5 * jnp.tanh(0.5 * pre) + 0.5
    act = pre * sigma
    return act.astype(bf16), sigma + act * (1.0 - sigma)


def norm_forward(values):
    size = values.shape[0]
    centre = values - jnp.sum(values, 0, keepdims=True) * (1.0 / size)
    var = jnp.sum(centre * centre, 0, keepdims=True) * (1.0 / size)
    scale = lax.rsqrt(var + 1e-05)
    return centre * scale, scale


def norm_backward(upstream, normed, scale, gain):
    size = upstream.shape[0]
    scaled = upstream * gain
    first = jnp.sum(scaled, 0, keepdims=True) * (1.0 / size)
    second = jnp.sum(scaled * normed, 0, keepdims=True) * (1.0 / size)
    return scale * (scaled - first - normed * second)


class Mail:
    def __init__(self, send, recv):
        self.send, self.recv, self.used = send, recv, 0

    def copy(self, source, target, device):
        at = self.used
        self.used += 1
        if self.send is None:
            return None
        copy = pltpu.make_async_remote_copy(
            src_ref=source,
            dst_ref=target,
            send_sem=self.send.at[at],
            recv_sem=self.recv.at[at],
            device_id=device,
            device_id_type=MESH,
        )
        copy.start()
        return copy


def count_copies(row_groups):
    near = min(row_groups, 8)
    far = row_groups // near
    sums = 3 + (row_groups - 1)
    rows_sum = 3 * (2 + 2 * (near // 2 - 1)) + 2 * (near - 1) + 4 * (far - 1)
    return 15 + 9 + 6 + 2 * sums + 4 * 3 + rows_sum


def put(ref, at, values):
    for c in range(0, TILE, 128):
        ref[pl.ds(pl.multiple_of(at + 2 * c, 256), 256), :] = values[:, c : c + 128]


def take(ref, at):
    return jnp.concatenate(
        [ref[pl.ds(pl.multiple_of(at + 2 * c, 256), 256), :] for c in range(0, TILE, 128)], 1
    )


def main_kernel(
    live_ref,
    pick_ref,
    xt_hbm,
    tt_hbm,
    g2m_hbm,
    m2m_hbm,
    m2g_hbm,
    first_hbm,
    wide_hbm,
    second_hbm,
    last_hbm,
    hbias_hbm,
    norm_hbm,
    dbias_hbm,
    level_hbm,
    out_ref,
    all_ref,
    tot_ref,
    xt,
    tt,
    g2m_ref,
    m2m_ref,
    m2g_ref,
    first_f,
    last_f,
    hbias_f,
    norm_f,
    dbias_f,
    level_f,
    local_sem,
    square_tmp,
    norm_ref,
    chan_ref,
    big,
    x_ref,
    w,
    wt,
    bias,
    h0full,
    h1full,
    hgfull,
    onehot,
    spots,
    act_g,
    scale_g,
    dec_in,
    dp_d,
    ds_e,
    act_e,
    hs_e,
    nrm_e,
    scale_e,
    dsum,
    land_a,
    land_b,
    half_out,
    grad,
    gland_a,
    gland_b,
    held,
    yland,
    gland,
    rland,
    fland,
    nacc,
    cacc,
    h0_mine,
    node_in,
    mesh_tmp,
    small,
    sland_h,
    sland_r,
    narrow,
    nland_h,
    nland_r,
    send,
    recv,
    *,
    row_groups,
    g2m_deg,
    m2g_deg,
):
    hid = lax.axis_index("hid")
    row = lax.axis_index("rows")
    near = min(row_groups, 8)
    far = row_groups // near
    row_near = lax.rem(row, near)
    row_far = row // near
    core = hid + 1 - 2 * lax.rem(hid, 2)
    across = lax.rem(hid + 2, 4)
    corner = lax.rem(core + 2, 4)
    mail = Mail(send, recv)
    channels, grid_rows = xt.shape
    mine = x_ref.shape[1]
    share = h0_mine.shape[1]
    mesh_rows = h0full.shape[1]
    tiles = mine // TILE
    degree = m2m_ref.shape[0]
    latent = h0_mine.shape[0]

    def peer(device):
        return {"hid": device, "rows": row}

    def row_peer(device):
        return {"hid": hid, "rows": device}

    barrier = pltpu.get_barrier_semaphore()
    for device in (core, across, corner):
        pl.semaphore_signal(barrier, inc=1, device_id=peer(device), device_id_type=MESH)
    for step in range(1, row_groups):
        pl.semaphore_signal(
            barrier,
            inc=1,
            device_id=row_peer(lax.rem(row + step, row_groups)),
            device_id_type=MESH,
        )

    my_grid = pl.multiple_of(hid * mine, mine)
    pairs = (
        (first_hbm, first_f),
        (hbias_hbm, hbias_f),
        *((second_hbm.at[k], gland_a.at[1, :, pl.ds(256 * k, 256)]) for k in range(3)),
        *((wide_hbm.at[k], gland_a.at[0, :, pl.ds(512 * k, 512)]) for k in range(3)),
        (last_hbm, last_f),
        (xt_hbm, xt),
        (norm_hbm, norm_f),
        (dbias_hbm, dbias_f),
        (level_hbm, level_f),
        (tt_hbm.at[:, pl.ds(my_grid, mine)], tt),
        (m2m_hbm, m2m_ref),
        (m2g_hbm.at[:, pl.ds(my_grid, mine)], m2g_ref),
        (g2m_hbm, g2m_ref),
    )
    fetches = [
        pltpu.make_async_copy(source, target, local_sem.at[at])
        for at, (source, target) in enumerate(pairs)
    ]
    for fetch in fetches:
        fetch.start()

    def gather_start(view):
        near_copy = mail.copy(view(hid), view(hid), peer(core))
        far_copy = mail.copy(view(hid), view(hid), peer(across))
        return near_copy, far_copy

    def gather_pass(view, copies):
        near_copy, far_copy = copies
        far_copy.wait_recv()
        return near_copy, far_copy, mail.copy(view(across), view(across), peer(core))

    def gather_wait(copies):
        near_copy, far_copy, passed = copies
        near_copy.wait_recv()
        passed.wait_recv()
        near_copy.wait_send()
        far_copy.wait_send()
        passed.wait_send()

    def rows_of(ref, block, size, start=0, width=None):
        width = ref.shape[1] if width is None else width
        return ref.at[pl.ds(pl.multiple_of(block * size, size), size), pl.ds(start, width)]

    def lanes_of(ref, block, size):
        return ref.at[:, pl.ds(pl.multiple_of(block * size, size), size)]

    own_rows = pl.ds(pl.multiple_of(hid * 64, 64), 64)
    square_tmp[...] = jnp.zeros_like(square_tmp)
    for fetch in fetches[:5]:
        fetch.wait()
    square_tmp[0:64, 0:channels] = first_f[...]
    w[own_rows, 0:128] = square_tmp[0:64, :].astype(bf16)
    square_tmp[...] = jnp.zeros_like(square_tmp)
    square_tmp[0:4, 0:64] = hbias_f[...]
    bias[own_rows, :] = square_tmp[...].T[:64]
    for layer, name in enumerate(("g2", "e2", "n2")):
        w[own_rows, COLS[name] : COLS[name] + 256] = gland_a[1, :, 256 * layer : 256 * layer + 256].astype(bf16)
    for fetch in fetches[5:9]:
        fetch.wait()
    for layer, name in enumerate(("e1", "n1", "d1")):
        w[own_rows, COLS[name] : COLS[name] + 512] = gland_a[0, :, 512 * layer : 512 * layer + 512].astype(bf16)
    square_tmp[...] = jnp.zeros_like(square_tmp)
    square_tmp[0:64, 0:channels] = last_f[...]
    w[own_rows, COLS["d2"] : COLS["d2"] + 128] = square_tmp[0:64, :].astype(bf16)
    pl.semaphore_wait(barrier, 3 + row_groups - 1)
    flights = {}
    def weights_start(name):
        start, width = GROUPS[name]
        flights[name] = gather_start(lambda block: rows_of(w, block, 64, start, width))

    weights_start("g")
    flights["b"] = gather_start(lambda block: rows_of(bias, block, 64))

    def weights_pass(name):
        if name == "b":
            flights[name] = gather_pass(lambda block: rows_of(bias, block, 64), flights[name])
            return
        start, width = GROUPS[name]
        flights[name] = gather_pass(
            lambda block: rows_of(w, block, 64, start, width), flights[name]
        )

    for fetch in fetches[9:]:
        fetch.wait()

    def padded(values, to):
        return jnp.concatenate(
            [values.astype(f32), jnp.zeros((to - channels, values.shape[1]), f32)], 0
        )

    def turn(i, carry):
        at = pl.multiple_of(i * TILE, TILE)
        big[pl.ds(at, TILE), :] = padded(xt[:, pl.ds(at, TILE)], 128).T
        return carry

    lax.fori_loop(0, grid_rows // TILE, turn, 0)
    step_rows = 16

    def pick(k, block):
        for half in range(share // 256):

            def rows(i, carry):
                for u in range(step_rows):
                    at = i * step_rows + u
                    nacc[block + half, pl.ds(at, 1), :] = big[
                        pl.ds(pick_ref[k, hid * share + half * 256 + at], 1), :
                    ]
                return carry

            lax.fori_loop(0, 256 // step_rows, rows, 0, unroll=True)

    def picked(block):
        return jnp.concatenate(
            [nacc[block + half].T[:PAD].astype(bf16) for half in range(share // 256)], 1
        )

    pick(0, 0)
    square_tmp[...] = jnp.zeros_like(square_tmp)
    for layer in range(3):
        square_tmp[2 * layer : 2 * layer + 2, :] = norm_f[layer][:, :128]
    norm_ref[:128, :] = square_tmp[...].T
    for layer in range(3):
        square_tmp[2 * layer : 2 * layer + 2, :] = norm_f[layer][:, 128:]
    norm_ref[128:, :] = square_tmp[...].T
    square_tmp[...] = jnp.zeros_like(square_tmp)
    square_tmp[0:1, 0:channels] = dbias_f[...]
    square_tmp[1:2, 0:channels] = level_f[...].astype(f32)
    chan_ref[...] = square_tmp[...].T[:PAD]

    for name in "gb":
        weights_pass(name)
    for name in "end":
        weights_start(name)
    gather_wait(flights["g"])
    gather_wait(flights["b"])
    b_g, b_e, b_n, b_d = (bias[:, k : k + 1] for k in range(4))
    gains = [norm_ref[:, 2 * k : 2 * k + 1] for k in range(3)]
    shifts = [norm_ref[:, 2 * k + 1 : 2 * k + 2] for k in range(3)]
    wt[:, 0:256] = flip(w[:, COLS["g2"] : COLS["g2"] + 256])
    w1g = w[:, 0:128][:, :PAD]

    def embed(inputs):
        pre = mm(w1g, inputs) + b_g
        act, slope = act_forward(pre)
        normed, scale = norm_forward(mm(wt[:, 0:256], act))
        return act, slope, normed, scale

    mesh_tmp[0] = jnp.zeros((latent, share), f32)

    def pool(i, carry):
        for half in range(2):
            inputs = picked(2 * half)
            pick(lax.rem(2 * i + half + 1, g2m_deg), 2 - 2 * half)
            mesh_tmp[0] += embed(inputs)[2] * gains[0] + shifts[0]
        return carry

    lax.fori_loop(0, g2m_deg // 2, pool, 0)
    h0_mine[...] = mesh_tmp[0] * (1.0 / g2m_deg)
    my_mesh = pl.ds(pl.multiple_of(hid * share, share), share)
    h0_half = h0_mine[...].astype(bf16)
    h0full[:, my_mesh] = h0_half
    node_in[:latent, :] = h0_half
    h0_view = functools.partial(lanes_of, h0full, size=share)
    h0_flight = gather_start(lambda block: h0_view(block))

    lane = lax.broadcasted_iota(jnp.int32, (1, TILE), 1)
    first_row = hid * mine

    def live_mask(i):
        return (first_row + i * TILE + lane < live_ref[0]).astype(f32)

    def own(i, carry):
        here = pl.ds(pl.multiple_of(i * TILE, TILE), TILE)
        inputs = padded(
            xt[:, pl.ds(pl.multiple_of(my_grid + i * TILE, TILE), TILE)], PAD
        ).astype(bf16)
        x_ref[:, here] = inputs
        act, slope, normed, scale = embed(inputs)
        put(big, 2 * i * 2 * TILE, slope)
        act_g[:, here] = act
        put(big, (2 * i + 1) * 2 * TILE, normed)
        scale_g[:, here] = scale
        dec_in[:latent, here] = (normed * gains[0] + shifts[0]).astype(bf16)
        return carry

    def own_range(a, b):
        lax.fori_loop(a, b, own, 0)

    own_range(0, tiles // 2)
    h0_flight = gather_pass(lambda block: h0_view(block), h0_flight)
    weights_pass("e")
    weights_pass("n")
    weights_pass("d")
    own_range(tiles // 2, tiles)

    cacc[...] = jnp.zeros_like(cacc)

    def squares(i, carry):
        here = pl.ds(pl.multiple_of(i * TILE, TILE), TILE)
        delta = (padded(tt[:, here], PAD) - x_ref[:, here].astype(f32)) * live_mask(i)
        cacc[0] += fold(delta * delta)
        return carry

    lax.fori_loop(0, tiles, squares, 0)
    col = lax.broadcasted_iota(jnp.int32, (PAD, 128), 1)
    live_here = jnp.clip(live_ref[0] - first_row, 0, mine).astype(f32)
    square_tmp[...] = jnp.zeros_like(square_tmp)
    square_tmp[:PAD, :] = jnp.where(
        col == 0, jnp.sum(cacc[0], 1, keepdims=True), jnp.where(col == 1, live_here, 0.0)
    )
    small[...] = square_tmp[...].T[:8]
    sum_hid = [
        mail.copy(small, sland_h.at[slot], peer(device))
        for slot, device in enumerate((core, across, corner))
    ]

    for name in "end":
        gather_wait(flights[name])
    wt[:, 256:512] = flip(w[:, COLS["e2"] : COLS["e2"] + 256])
    wt[:, 512:768] = flip(w[:, COLS["n2"] : COLS["n2"] + 256])
    wt[:128, 768:1024] = flip(w[:, COLS["d2"] : COLS["d2"] + 128])
    gather_wait(h0_flight)

    e1 = COLS["e1"]
    mesh_tmp[0] = mm(w[:, e1 : e1 + 256], node_in[:latent, :]) + b_e
    mesh_tmp[1] = jnp.zeros((latent, share), f32)

    def edge_index(k):
        return m2m_ref[pl.ds(k, 1), my_mesh]

    def fill(index, base, rows):
        for block, part in enumerate(ones_at(index, base, rows)):
            onehot[block * 256 : block * 256 + 256, :] = part

    def edge(k, carry):
        fill(edge_index(k), 0, mesh_rows)
        sent = mm(h0full[...], onehot[...]).astype(bf16)
        hs_e[k] = sent
        pre = mesh_tmp[0] + mm(w[:, e1 + 256 : e1 + 512], sent)
        act, slope = act_forward(pre)
        act_e[k] = act
        ds_e[k] = slope
        normed, scale = norm_forward(mm(wt[:, 256:512], act))
        nrm_e[k] = normed
        scale_e[pl.ds(k, 1), :] = scale
        mesh_tmp[1] += normed * gains[1] + shifts[1]
        return carry

    lax.fori_loop(0, degree, edge, 0)

    for copy in sum_hid:
        copy.wait()
    small[...] = small[...] + sland_h[0] + sland_h[1] + sland_h[2]
    sum_rows = [
        mail.copy(small, sland_r.at[step - 1], row_peer(lax.rem(row + step, row_groups)))
        for step in range(1, row_groups)
    ]
    n1 = COLS["n1"]
    node_in[latent:, :] = mesh_tmp[1].astype(bf16)
    act_n, slope_n = act_forward(mm(w[:, n1 : n1 + 512], node_in[...]) + b_n)
    normed_n, scale_n = norm_forward(mm(wt[:, 512:768], act_n))
    h1 = h0_mine[...] + (normed_n * gains[2] + shifts[2])
    ds_e[degree] = slope_n
    act_e[degree] = act_n
    nrm_e[degree] = normed_n
    scale_e[degree : degree + 1, :] = scale_n
    h1full[:, my_mesh] = h1.astype(bf16)
    h1_view = functools.partial(lanes_of, h1full, size=share)
    h1_flight = gather_start(lambda block: h1_view(block))

    for copy in sum_rows:
        copy.wait()
    totals = small[...]
    for step in range(1, row_groups):
        totals = totals + sland_r[step - 1]
    square_tmp[...] = jnp.zeros_like(square_tmp)
    square_tmp[:8, :] = totals
    totals = square_tmp[...].T[:PAD]
    count = totals[:, 1:2]
    var = totals[:, 0:1] / count + 1e-06
    d_bias = chan_ref[:, 0:1]
    level = chan_ref[:, 1:2]
    loss_weight = count * jnp.sum(level, 0, keepdims=True)
    tot_ref[...] = jnp.broadcast_to(loss_weight[:8], (8, 128))
    weight_var = level / var
    pull = 2.0 * weight_var / loss_weight
    nacc[...] = jnp.zeros_like(nacc)
    cacc[...] = jnp.zeros_like(cacc)
    grad[...] = jnp.zeros_like(grad)
    dsum[...] = jnp.zeros_like(dsum)


    def spot(i, write):
        base = my_grid + i * TILE
        for at in range(0, mesh_rows, TILE):
            for block, part in enumerate(ones_at(g2m_ref[:, at : at + TILE], base, TILE)):
                write(block, at, part)

    def spot_store(i, carry):
        def write(block, at, part):
            spots[i, block * 256 : block * 256 + 256, at : at + TILE] = part

        spot(i, write)
        return carry

    ready = spots.shape[0]
    lax.fori_loop(0, ready - 1, spot_store, 0)
    h1_flight = gather_pass(lambda block: h1_view(block), h1_flight)
    lax.fori_loop(ready - 1, ready, spot_store, 0)
    gather_wait(h1_flight)

    def chunk(start, width, block):
        return rows_of(grad, block, 64, start, width)

    def reduce_start(name):
        start, width = GROUPS[name]
        flight = (
            mail.copy(
                chunk(start, width, corner), gland_a.at[1, :, pl.ds(start, width)], peer(core)
            ),
            mail.copy(
                chunk(start, width, core), gland_a.at[0, :, pl.ds(start, width)], peer(core)
            ),
        )
        return flight

    def reduce_across(name, flight):
        start, width = GROUPS[name]
        cols = pl.ds(start, width)
        flight[0].wait()
        view = chunk(start, width, across)
        view[...] = view[...] + gland_a[1, :, cols]
        return flight + (mail.copy(view, gland_b.at[:, cols], peer(across)),)

    def reduce_rows(name, flight):
        start, width = GROUPS[name]
        cols = pl.ds(start, width)
        flight[1].wait()
        flight[2].wait()
        part = 64 // near
        held[:, cols] = chunk(start, width, hid)[...] + gland_a[0, :, cols] + gland_b[:, cols]
        copies = []
        for step in range(1, near):
            to = lax.rem(row_near + step, near)
            copies.append(
                mail.copy(
                    held.at[pl.ds(pl.multiple_of(to * part, part), part), cols],
                    gland.at[step - 1],
                    row_peer(row_far * near + to),
                )
            )
        return copies

    def far_sum(own_part, cols, total):
        if far > 1:
            own_part[...] = total
            more = []
            for step in range(1, far):
                to = lax.rem(row_far + step, far)
                more.append(
                    mail.copy(
                        own_part,
                        fland.at[step - 1, :, cols],
                        row_peer(to * near + row_near),
                    )
                )
            for copy in more:
                copy.wait()
            for step in range(1, far):
                total = total + fland[step - 1, :, cols]
        return total

    side = lax.rem(row_near, 2)
    level = row_near // 2
    neighbour = row_far * near + 2 * level + 1 - side

    def half_rows(which):
        return pl.ds(pl.multiple_of(which * 32, 32), 32)

    def part_rows(where):
        return pl.ds(pl.multiple_of(side * 32 + where * 8, 8), 8)

    def level_peer(where):
        return row_peer(row_far * near + 2 * where + side)

    def rows_halve(name, flight):
        start, width = GROUPS[name]
        cols = pl.ds(start, width)
        flight[1].wait()
        flight[2].wait()
        held[:, cols] = chunk(start, width, hid)[...] + gland_a[0, :, cols] + gland_b[:, cols]
        return [
            mail.copy(held.at[half_rows(1 - side), cols], yland.at[:, cols], row_peer(neighbour))
        ]

    def rows_part(name, copies):
        start, width = GROUPS[name]
        cols = pl.ds(start, width)
        copies[0].wait()
        held[half_rows(side), cols] = held[half_rows(side), cols] + yland[:, cols]
        out = []
        for step in range(1, near // 2):
            to = lax.rem(level + step, near // 2)
            out.append(
                mail.copy(
                    held.at[part_rows(to), cols], rland.at[step - 1, :, cols], level_peer(to)
                )
            )
        return out

    def rows_total(name, copies):
        start, width = GROUPS[name]
        cols = pl.ds(start, width)
        for copy in copies:
            copy.wait()
        total = held[part_rows(level), cols]
        for step in range(1, near // 2):
            total = total + rland[step - 1, :, cols]
        own_part = out_ref.at[part_rows(level), cols]
        own_part[...] = far_sum(own_part, cols, total)
        out = []
        for step in range(1, near // 2):
            to = lax.rem(level + step, near // 2)
            out.append(mail.copy(own_part, own_part, level_peer(to)))
        return out

    def rows_back(name, copies):
        start, width = GROUPS[name]
        for copy in copies:
            copy.wait()
        view = out_ref.at[half_rows(side), pl.ds(start, width)]
        return [mail.copy(view, view, row_peer(neighbour))]

    def reduce_share(name, copies):
        start, width = GROUPS[name]
        cols = pl.ds(start, width)
        part = 64 // near
        shared = pl.ds(pl.multiple_of(row_near * part, part), part)
        own_part = out_ref.at[shared, cols]
        for copy in copies:
            copy.wait()
        total = held[shared, cols]
        for step in range(1, near):
            total = total + gland[step - 1]
        own_part[...] = far_sum(own_part, cols, total)
        out = []
        for step in range(1, near):
            to = lax.rem(row_near + step, near)
            out.append(mail.copy(own_part, own_part, row_peer(row_far * near + to)))
        return out

    d1, d2 = COLS["d1"], COLS["d2"]
    def decode(i, carry):
        here = pl.ds(pl.multiple_of(i * TILE, TILE), TILE)
        fill(m2g_ref[:, here], 0, mesh_rows)
        back = mm(h1full[...], onehot[...]) * (1.0 / m2g_deg)
        dec_in[latent:, here] = back.astype(bf16)
        pre = mm(w[:, d1 : d1 + 512], dec_in[:, here]) + b_d
        act, slope = act_forward(pre)
        out = mm(wt[:128, 768:1024], act)[:PAD]
        err = x_ref[:, here].astype(f32) + out + d_bias - padded(tt[:, here], PAD)
        kept = err * live_mask(i)
        cacc[1] += fold(weight_var * kept * err)
        pred_grad = pull * kept
        cacc[0] += fold(pred_grad)
        upstream = pred_grad.astype(bf16)
        act_grad = mm(w[:, d2 : d2 + 128][:, :PAD], upstream)
        pre_grad = (act_grad * slope).astype(bf16)
        dp_d[:, here] = pre_grad
        dsum[...] += mt(onehot[...], pre_grad)
        grad[:, d2 : d2 + PAD] += mt(act, upstream)
        return carry

    lax.fori_loop(0, tiles, decode, 0)

    def spread_start(view, land):
        return (
            mail.copy(view(corner), land.at[1], peer(core)),
            mail.copy(view(core), land.at[0], peer(core)),
        )

    def spread_across(view, land, land_far, out, copies):
        copies[0].wait()
        out[...] = (view(across)[...] + land[1]).astype(bf16)
        return copies + (mail.copy(out, land_far, peer(across)),)

    def spread_end(view, land, land_far, copies):
        copies[1].wait()
        copies[2].wait()
        return view(hid)[...] + land[0] + land_far[...].astype(f32)

    def view_d(block):
        return dsum.at[pl.ds(pl.multiple_of(block * share, share), share), :]

    d_flight = spread_start(view_d, land_a.at[0])
    w1d_low = flip(w[:, d1 : d1 + 256])
    wt[:, 1024:1280] = w1d_low
    d_flight = spread_across(view_d, land_a.at[0], land_b.at[0], half_out, d_flight)

    def decode_rest(i, carry):
        here = pl.ds(pl.multiple_of(i * TILE, TILE), TILE)
        pre_grad = dp_d[:, here]
        grad[:, d1 : d1 + 512] += mt(pre_grad, dec_in[:, here])
        nacc[9] += fold(pre_grad.astype(f32))
        return carry

    lax.fori_loop(0, tiles, decode_rest, 0)
    stage = {"d": reduce_start("d")}
    wt[:, 2304:2560] = flip(w[:, d1 + 256 : d1 + 512])
    wt[:, 1280:1536] = flip(w[:, n1 : n1 + 256])
    wt[:, 1536:1792] = flip(w[:, n1 + 256 : n1 + 512])
    wt[:, 1792:2048] = flip(w[:, e1 : e1 + 256])
    wt[:, 2048:2304] = flip(w[:, e1 + 256 : e1 + 512])

    def write_late(start):
        def write(block, at, part):
            dec_in[block * 256 : block * 256 + 256, start + at : start + at + TILE] = part

        return write

    def write_last(block, at, part):
        (h0full, h1full)[block][:, at : at + TILE] = part

    spot(ready, write_late(0))
    spot(ready + 1, write_late(mesh_rows))

    pieces = [hs_e.at[k] for k in range(degree)] + [act_e.at[k] for k in range(degree)]

    def write_pieces(block, at, part):
        pieces[block * (mesh_rows // TILE) + at // TILE][...] = part

    def write_whole(block, at, part):
        onehot[at + block * 256 : at + block * 256 + 256, :] = part

    high, low = split2(spread_end(view_d, land_a.at[0], land_b.at[0], d_flight))
    stage["d"] = reduce_across("d", stage["d"])
    h1_grad = (mt(wt[:, 2304:2560], high) + mt(wt[:, 2304:2560], low)) * (1.0 / m2g_deg)
    nacc[2] += fold(h1_grad * nrm_e[degree])
    nacc[5] += fold(h1_grad)
    up_n = norm_backward(
        h1_grad, nrm_e[degree], scale_e[degree : degree + 1, :], gains[2]
    ).astype(bf16)
    n2 = COLS["n2"]
    pre_grad_n = (mm(w[:, n2 : n2 + 256], up_n) * ds_e[degree]).astype(bf16)
    mesh_tmp[0] = h1_grad + mm(wt[:, 1280:1536], pre_grad_n)
    mesh_tmp[1] = mm(wt[:, 1536:1792], pre_grad_n)

    grad[:, n2 : n2 + 256] = mt(act_e[degree], up_n)
    grad[:, n1 : n1 + 512] = mt(pre_grad_n, node_in[...])
    nacc[8] += fold(pre_grad_n.astype(f32))
    stage["n"] = reduce_start("n")

    e2 = COLS["e2"]

    def edge_back(k, carry):
        upstream = mesh_tmp[1]
        normed = nrm_e[k]
        nacc[1] += fold(upstream * normed)
        nacc[4] += fold(upstream)
        up = norm_backward(upstream, normed, scale_e[pl.ds(k, 1), :], gains[1]).astype(bf16)
        pre_grad = (mm(w[:, e2 : e2 + 256], up) * ds_e[k]).astype(bf16)
        mesh_tmp[0] += mm(wt[:, 1792:2048], pre_grad)
        grad[:, e2 : e2 + 256] += mt(act_e[k], up)
        act_e[k] = pre_grad
        nacc[7] += fold(pre_grad.astype(f32))
        return carry

    lax.fori_loop(0, degree, edge_back, 0)
    stage["d"] = rows_halve("d", stage["d"])
    stage["n"] = reduce_across("n", stage["n"])

    def senders(block):
        total = None
        for k in range(degree):
            place = k % 4 * TILE
            for half, part in enumerate(ones_at(edge_index(k), block * share, share)):
                onehot[place + half * 256 : place + half * 256 + 256, :] = part
            term = mt(onehot[place : place + TILE, :], act_e[k])
            total = term if total is None else total + term
        view_d(block)[...] = total

    senders(corner)
    e_first = mail.copy(view_d(corner), land_a.at[1, 1], peer(core))
    senders(core)
    e_flight = (e_first, mail.copy(view_d(core), land_a.at[1, 0], peer(core)))
    senders(across)
    stage["d"] = rows_part("d", stage["d"])
    e_flight = spread_across(view_d, land_a.at[1], land_b.at[1], half_out, e_flight)
    senders(hid)

    def edge_weights(k, carry):
        grad[:, e1 : e1 + 256] += mt(act_e[k], node_in[:latent, :])
        grad[:, e1 + 256 : e1 + 512] += mt(act_e[k], hs_e[k])
        return carry

    lax.fori_loop(0, degree, edge_weights, 0)
    stage["e"] = reduce_start("e")
    stage["n"] = rows_halve("n", stage["n"])
    stage["d"] = rows_total("d", stage["d"])
    high, low = split2(spread_end(view_d, land_a.at[1], land_b.at[1], e_flight))
    h0_grad = mesh_tmp[0] + mt(wt[:, 2048:2304], high) + mt(wt[:, 2048:2304], low)
    hgfull[:, my_mesh] = (h0_grad * (1.0 / g2m_deg)).astype(bf16)
    hg_view = functools.partial(lanes_of, hgfull, size=share)
    hg_flight = gather_start(lambda block: hg_view(block))


    spot(ready + 2, write_last)
    stage["n"] = rows_part("n", stage["n"])
    stage["d"] = rows_back("d", stage["d"])
    spot(ready + 3, write_pieces)
    hg_flight = gather_pass(lambda block: hg_view(block), hg_flight)
    stage["e"] = reduce_across("e", stage["e"])
    spot(ready + 4, write_whole)
    stage["n"] = rows_total("n", stage["n"])
    gather_wait(hg_flight)

    def grid_back(i, both):
        here = pl.ds(pl.multiple_of(i * TILE, TILE), TILE)
        upstream = mm(wt[:, 1024:1280], dp_d[:, here]) + both
        normed = take(big, (2 * i + 1) * 2 * TILE)
        nacc[0] += fold(upstream * normed)
        nacc[3] += fold(upstream)
        up = norm_backward(upstream, normed, scale_g[:, here], gains[0]).astype(bf16)
        pre_grad = (mm(w[:, COLS["g2"] : COLS["g2"] + 256], up) * take(big, 2 * i * 2 * TILE)).astype(bf16)
        grad[:, COLS["g2"] : COLS["g2"] + 256] += mt(act_g[:, here], up)
        grad[:, 0:PAD] += mt(pre_grad, x_ref[:, here])
        nacc[6] += fold(pre_grad.astype(f32))

    def grid_ready(i, carry):
        grid_back(i, mt(hgfull[...], spots[i]))
        return carry

    def from_blocks(blocks):
        total = None
        for at, block in enumerate(blocks):
            term = mt(hgfull[:, at * TILE : at * TILE + TILE], block[...])
            total = term if total is None else total + term
        return total

    count_m = mesh_rows // TILE
    lax.fori_loop(0, ready, grid_ready, 0)
    stage["n"] = rows_back("n", stage["n"])
    stage["e"] = rows_halve("e", stage["e"])
    for half in range(2):
        grid_back(
            ready + half, mt(hgfull[...], dec_in[:, half * mesh_rows : (half + 1) * mesh_rows])
        )
    grid_back(
        ready + 2,
        jnp.concatenate([mt(hgfull[...], h0full[...]), mt(hgfull[...], h1full[...])], 1),
    )
    stage["e"] = rows_part("e", stage["e"])
    grid_back(
        ready + 3,
        jnp.concatenate([from_blocks(pieces[:count_m]), from_blocks(pieces[count_m : 2 * count_m])], 1),
    )
    grid_back(
        ready + 4, from_blocks([onehot.at[k * TILE : k * TILE + TILE, :] for k in range(count_m)])
    )

    block = grad[:, 0:128]
    at_col = lax.broadcasted_iota(jnp.int32, (latent, 128), 1)
    for k in range(4):
        block = jnp.where(at_col == PAD + k, jnp.sum(nacc[6 + k], 1, keepdims=True), block)
    grad[:, 0:128] = block
    stage["g"] = reduce_start("g")
    block = jnp.zeros((latent, 128), f32)
    for k in range(6):
        block = jnp.where(at_col == 2 * (k % 3) + k // 3, jnp.sum(nacc[k], 1, keepdims=True), block)
    norm_ref[...] = block
    block = norm_ref[:PAD, :]
    for k in range(2):
        block = jnp.where(col == 6 + k, jnp.sum(cacc[k], 1, keepdims=True), block)
    norm_ref[:PAD, :] = block
    narrow[...] = norm_ref[...].T[:8]
    narrow_hid = [
        mail.copy(narrow, nland_h.at[slot], peer(device))
        for slot, device in enumerate((core, across, corner))
    ]
    stage["e"] = rows_total("e", stage["e"])
    stage["g"] = reduce_across("g", stage["g"])
    for copy in narrow_hid:
        copy.wait()
    narrow[...] = narrow[...] + nland_h[0] + nland_h[1] + nland_h[2]
    narrow_rows = [
        mail.copy(narrow, nland_r.at[step - 1], row_peer(lax.rem(row + step, row_groups)))
        for step in range(1, row_groups)
    ]
    stage["e"] = rows_back("e", stage["e"])
    stage["g"] = reduce_rows("g", stage["g"])
    stage["g"] = reduce_share("g", stage["g"])
    for copy in narrow_rows:
        copy.wait()
    total = narrow[...]
    for step in range(1, row_groups):
        total = total + nland_r[step - 1]
    all_ref[...] = total
    for name in "dneg":
        for copy in stage[name]:
            copy.wait()


def adam_step(weight, avg, sq, grad, rate, decay):
    avg_new = 0.5 * avg + 0.5 * grad
    sq_new = 0.5 * sq + 0.5 * grad * grad
    fix = 1.0 - 0.5**STEP_COUNT
    step = (avg_new * (1.0 / fix)) / (jnp.sqrt(sq_new * (1.0 / fix)) + 1e-08)
    return (weight - rate * (step + decay * weight), avg_new, sq_new)


def adam_kernel(out_ref, all_ref, tot_ref, *refs):
    ins_hbm, outs_hbm, loss_ref, weight_ref = refs[:21], refs[21:46], refs[46], refs[47]
    ins, outs, turned, sem_in, sem_out = refs[48:69], refs[69:94], refs[94], refs[95], refs[96]
    fetches = [
        pltpu.make_async_copy(source, target, sem_in.at[at])
        for at, (source, target) in enumerate(zip(ins_hbm, ins))
    ]
    for fetch in fetches:
        fetch.start()
    stores = []

    def arrive(array):
        for part in (array, 7 + array, 14 + array):
            fetches[part].wait()

    def leave(array):
        for part in (array, 7 + array, 14 + array) + ((21 + array,) if array < 4 else ()):
            store = pltpu.make_async_copy(outs[part], outs_hbm[part], sem_out.at[part])
            store.start()
            stores.append(store)

    def update(array, at, grad, rate, decay):
        fresh, avg_new, sq_new = adam_step(
            ins[array][at], ins[7 + array][at], ins[14 + array][at], grad, rate, decay
        )
        outs[array][at] = fresh
        outs[7 + array][at] = avg_new
        outs[14 + array][at] = sq_new
        if array < 4:
            outs[21 + array][at] = fresh.astype(bf16)

    everything = (slice(None), slice(None))
    channels = ins[0].shape[1]
    arrive(1)
    for layer, name in enumerate(("e1", "n1", "d1")):
        update(1, (layer,) + everything, out_ref[:, COLS[name] : COLS[name] + 512], 0.05, 0.1)
    leave(1)
    arrive(2)
    for layer, name in enumerate(("g2", "e2", "n2")):
        update(2, (layer,) + everything, out_ref[:, COLS[name] : COLS[name] + 256], 0.05, 0.1)
    leave(2)
    arrive(0)
    update(0, everything, out_ref[:, 0:128][:, :channels], 0.05, 0.1)
    leave(0)
    arrive(3)
    update(3, everything, out_ref[:, COLS["d2"] : COLS["d2"] + 128][:, :channels], 0.05, 0.1)
    leave(3)
    turned[...] = out_ref[:, 0:128].T
    arrive(4)
    update(4, everything, turned[PAD : PAD + 4, :], 0.3, 0.0)
    leave(4)
    arrive(5)
    for layer in range(3):
        update(5, (layer,) + everything, all_ref[2 * layer : 2 * layer + 2, :], 0.3, 0.0)
    leave(5)
    arrive(6)
    update(6, everything, all_ref[6:7, 0:channels], 0.3, 0.0)
    leave(6)
    loss_ref[...] = jnp.sum(all_ref[7:8, 0:PAD], 1, keepdims=True)
    weight_ref[...] = tot_ref[0:1, 0:1]
    for store in stores:
        store.wait()


def body(
    grid_input,
    grid_target,
    live_points,
    level_weight,
    g2m_index,
    m2m_index,
    m2g_index,
    *params,
):
    groups = lax.axis_size("hid")
    row_groups = lax.axis_size("rows")
    masters, avgs, squares = params[:7], params[7:14], params[14:21]
    grid_rows, channels = grid_input.shape
    mesh_rows, degree = m2m_index.shape
    latent = masters[5].shape[2]
    share = mesh_rows // groups
    mine = grid_rows // groups
    g2m_deg = g2m_index.shape[1]
    m2g_deg = m2g_index.shape[1]
    whole = pl.BlockSpec(memory_space=pltpu.VMEM)
    scalar = pl.BlockSpec(memory_space=pltpu.SMEM)
    far_memory = pl.BlockSpec(memory_space=pltpu.HBM)
    g2m = g2m_index.T

    def flat(arrays):
        first, wide, second, last, bias, norm, out_bias = arrays
        return (
            first.T,
            wide.transpose(0, 2, 1),
            second,
            last,
            bias,
            norm.transpose(1, 0, 2),
            out_bias[None],
        )

    operands = flat(masters) + flat(avgs) + flat(squares)
    loads = [
        grid_input.T,
        grid_target.T,
        g2m,
        m2m_index.T,
        m2g_index.T,
        *operands[:7],
        level_weight[None],
    ]
    kept = [jax.ShapeDtypeStruct(v.shape, v.dtype) for v in loads]
    for at in (1, 4):
        kept[at] = jax.ShapeDtypeStruct((kept[at].shape[0], mine), kept[at].dtype)
    copies = count_copies(row_groups)
    near = min(row_groups, 8)
    far = row_groups // near
    summed, spare, totals = pl.pallas_call(
        functools.partial(
            main_kernel, row_groups=row_groups, g2m_deg=g2m_deg, m2g_deg=m2g_deg
        ),
        out_shape=[
            jax.ShapeDtypeStruct((64, PACK), f32),
            jax.ShapeDtypeStruct((8, 256), f32),
            jax.ShapeDtypeStruct((8, 128), f32),
        ],
        in_specs=[scalar] * 2 + [far_memory] * 13,
        out_specs=[whole] * 3,
        scratch_shapes=[pltpu.VMEM(v.shape, v.dtype) for v in kept[:6] + kept[8:]]
        + [
            pltpu.SemaphoreType.DMA((17,)),
            pltpu.VMEM((128, 128), f32),
            pltpu.VMEM((latent, 128), f32),
            pltpu.VMEM((PAD, 128), f32),
            pltpu.VMEM((grid_rows, 128), f32),
            pltpu.VMEM((PAD, mine), bf16),
            pltpu.VMEM((256, PACK), bf16),
            pltpu.VMEM((256, 2560), bf16),
            pltpu.VMEM((256, 128), f32),
            pltpu.VMEM((latent, mesh_rows), bf16),
            pltpu.VMEM((latent, mesh_rows), bf16),
            pltpu.VMEM((latent, mesh_rows), bf16),
            pltpu.VMEM((mesh_rows, TILE), bf16),
            pltpu.VMEM((3, TILE, mesh_rows), bf16),
            pltpu.VMEM((latent, mine), bf16),
            pltpu.VMEM((1, mine), f32),
            pltpu.VMEM((2 * latent, mine), bf16),
            pltpu.VMEM((latent, mine), bf16),
            pltpu.VMEM((degree + 1, latent, share), f32),
            pltpu.VMEM((degree + 1, latent, share), bf16),
            pltpu.VMEM((degree, latent, share), bf16),
            pltpu.VMEM((degree + 1, latent, share), f32),
            pltpu.VMEM((8, share), f32),
            pltpu.VMEM((mesh_rows, latent), f32),
            pltpu.VMEM((2, 2, share, latent), f32),
            pltpu.VMEM((2, share, latent), bf16),
            pltpu.VMEM((share, latent), bf16),
            pltpu.VMEM((256, PACK), f32),
            pltpu.VMEM((2, 64, PACK), f32),
            pltpu.VMEM((64, PACK), f32),
            pltpu.VMEM((64, PACK), f32),
            pltpu.VMEM((32, PACK), f32),
            pltpu.VMEM((near - 1, 64 // near, GROUPS["g"][1]), f32),
            pltpu.VMEM((near // 2 - 1, 64 // near, PACK), f32),
            pltpu.VMEM((max(far - 1, 1), 64 // near, PACK), f32),
            pltpu.VMEM((g2m_deg * share // 256, 256, 128), f32),
            pltpu.VMEM((2, PAD, 128), f32),
            pltpu.VMEM((latent, share), f32),
            pltpu.VMEM((2 * latent, share), bf16),
            pltpu.VMEM((2, latent, share), f32),
            pltpu.VMEM((8, 128), f32),
            pltpu.VMEM((3, 8, 128), f32),
            pltpu.VMEM((row_groups - 1, 8, 128), f32),
            pltpu.VMEM((8, 256), f32),
            pltpu.VMEM((3, 8, 256), f32),
            pltpu.VMEM((row_groups - 1, 8, 256), f32),
            pltpu.SemaphoreType.DMA((copies,)),
            pltpu.SemaphoreType.DMA((copies,)),
        ],
        compiler_params=pltpu.CompilerParams(
            collective_id=0, has_side_effects=True, vmem_limit_bytes=64 * 2**20
        ),
        name="step",
    )(
        live_points,
        g2m,
        *loads,
    )
    shapes = [jax.ShapeDtypeStruct(v.shape, f32) for v in operands]
    shapes += [jax.ShapeDtypeStruct(v.shape, bf16) for v in operands[:4]]
    outs = pl.pallas_call(
        adam_kernel,
        out_shape=shapes + [jax.ShapeDtypeStruct((1, 1), f32)] * 2,
        in_specs=[whole] * 3 + [far_memory] * 21,
        out_specs=[far_memory] * 25 + [whole] * 2,
        scratch_shapes=[pltpu.VMEM(v.shape, v.dtype) for v in operands + tuple(shapes)]
        + [
            pltpu.VMEM((128, 64), f32),
            pltpu.SemaphoreType.DMA((21,)),
            pltpu.SemaphoreType.DMA((25,)),
        ],
        compiler_params=pltpu.CompilerParams(vmem_limit_bytes=64 * 2**20),
        name="adam",
    )(summed, spare, totals, *operands)

    def unflat(arrays):
        first, wide, second, last, bias, norm, out_bias = arrays
        return (
            first.T,
            wide.transpose(0, 2, 1),
            second,
            last,
            bias,
            norm.transpose(1, 0, 2),
            out_bias[0],
        )

    halves = outs[21:25]
    return (
        (outs[25][0, 0], outs[26][0, 0])
        + unflat(outs[0:7])
        + unflat(outs[7:14])
        + unflat(outs[14:21])
        + (halves[0].T, halves[1].transpose(0, 2, 1), halves[2], halves[3])
    )


def solution(mesh):
    weights = (
        P(None, "hid"),
        P(None, None, "hid"),
        P(None, "hid", None),
        P("hid", None),
        P(None, "hid"),
        P(),
        P(),
    )
    in_specs = (
        P("rows", None),
        P("rows", None),
        P("rows"),
        P(),
        P("rows", None),
        P("rows", None),
        P("rows", None),
    ) + weights * 3
    out_specs = (P(), P()) + weights * 3 + weights[:4]
    return jax.shard_map(body, mesh=mesh, in_specs=in_specs, out_specs=out_specs, check_vma=False)
```

```python
import functools

import jax
import jax.numpy as jnp
from jax import lax
from jax.experimental import pallas as pl
from jax.experimental.pallas import tpu as pltpu
from jax.sharding import PartitionSpec as P

STEP_COUNT = 5
MESH = pl.DeviceIdType.MESH
bf16 = jnp.bfloat16
f32 = jnp.float32
TILE = 512
PAD = 80
COLS = {"g1": 0, "g2": 128, "e1": 384, "e2": 896, "n1": 1152, "n2": 1664, "d1": 1920, "d2": 2432}
GROUPS = {"g": (0, 384), "e": (384, 768), "n": (1152, 768), "d": (1920, 640)}
PACK = 2560


def mm(left, right):
    return lax.dot_general(left, right, (((1,), (0,)), ((), ())), preferred_element_type=f32)


def mt(left, right):
    return lax.dot_general(left, right, (((1,), (1,)), ((), ())), preferred_element_type=f32)


def flip(values):
    return values.astype(f32).T.astype(bf16)


def split2(values):
    high = values.astype(bf16)
    low = (values - high.astype(f32)).astype(bf16)
    return high, low


def fold(values):
    total = values[:, :128]
    for at in range(128, values.shape[1], 128):
        total = total + values[:, at : at + 128]
    return total


def ones_at(index, base, rows):
    lanes = index.shape[1]
    local = lax.broadcasted_iota(jnp.int32, (256, lanes), 0).astype(f32).astype(bf16)
    parts = []
    for block in range(rows // 256):
        total = None
        for k in range(index.shape[0]):
            shifted = (index[k : k + 1] - (base + block * 256)).astype(f32).astype(bf16)
            hit = jnp.where(
                jnp.broadcast_to(shifted, (256, lanes)) == local,
                jnp.asarray(1, bf16),
                jnp.asarray(0, bf16),
            )
            total = hit if total is None else total + hit
        parts.append(total)
    return parts


def act_forward(pre):
    sigma = 0.5 * jnp.tanh(0.5 * pre) + 0.5
    act = pre * sigma
    return act.astype(bf16), sigma + act * (1.0 - sigma)


def norm_forward(values):
    size = values.shape[0]
    centre = values - jnp.sum(values, 0, keepdims=True) * (1.0 / size)
    var = jnp.sum(centre * centre, 0, keepdims=True) * (1.0 / size)
    scale = lax.rsqrt(var + 1e-05)
    return centre * scale, scale


def norm_backward(upstream, normed, scale, gain):
    size = upstream.shape[0]
    scaled = upstream * gain
    first = jnp.sum(scaled, 0, keepdims=True) * (1.0 / size)
    second = jnp.sum(scaled * normed, 0, keepdims=True) * (1.0 / size)
    return scale * (scaled - first - normed * second)


class Mail:
    def __init__(self, send, recv):
        self.send, self.recv, self.used = send, recv, 0

    def copy(self, source, target, device):
        at = self.used
        self.used += 1
        if self.send is None:
            return None
        copy = pltpu.make_async_remote_copy(
            src_ref=source,
            dst_ref=target,
            send_sem=self.send.at[at],
            recv_sem=self.recv.at[at],
            device_id=device,
            device_id_type=MESH,
        )
        copy.start()
        return copy


def count_copies(row_groups):
    near = min(row_groups, 8)
    far = row_groups // near
    sums = 3 + (row_groups - 1)
    rows_sum = 3 * (2 + 2 * (near // 2 - 1)) + 2 * (near - 1) + 4 * (far - 1)
    return 15 + 9 + 6 + 2 * sums + 4 * 3 + rows_sum


def put(ref, at, values):
    for c in range(0, TILE, 128):
        ref[pl.ds(pl.multiple_of(at + 2 * c, 256), 256), :] = values[:, c : c + 128]


def take(ref, at):
    return jnp.concatenate(
        [ref[pl.ds(pl.multiple_of(at + 2 * c, 256), 256), :] for c in range(0, TILE, 128)], 1
    )


def main_kernel(
    live_ref,
    pick_ref,
    xt_hbm,
    tt_hbm,
    g2m_hbm,
    m2m_hbm,
    m2g_hbm,
    first_hbm,
    wide_hbm,
    second_hbm,
    last_hbm,
    hbias_hbm,
    norm_hbm,
    dbias_hbm,
    level_hbm,
    out_ref,
    all_ref,
    tot_ref,
    xt,
    tt,
    g2m_ref,
    m2m_ref,
    m2g_ref,
    first_f,
    last_f,
    hbias_f,
    norm_f,
    dbias_f,
    level_f,
    local_sem,
    square_tmp,
    norm_ref,
    chan_ref,
    big,
    x_ref,
    w,
    wt,
    bias,
    h0full,
    h1full,
    hgfull,
    onehot,
    spots,
    act_g,
    scale_g,
    dec_in,
    dp_d,
    ds_e,
    act_e,
    hs_e,
    nrm_e,
    scale_e,
    dsum,
    land_a,
    land_b,
    half_out,
    grad,
    gland_a,
    gland_b,
    held,
    yland,
    gland,
    rland,
    fland,
    nacc,
    cacc,
    h0_mine,
    node_in,
    mesh_tmp,
    small,
    sland_h,
    sland_r,
    narrow,
    nland_h,
    nland_r,
    send,
    recv,
    *,
    row_groups,
    g2m_deg,
    m2g_deg,
):
    hid = lax.axis_index("hid")
    row = lax.axis_index("rows")
    near = min(row_groups, 8)
    far = row_groups // near
    row_near = lax.rem(row, near)
    row_far = row // near
    core = hid + 1 - 2 * lax.rem(hid, 2)
    across = lax.rem(hid + 2, 4)
    corner = lax.rem(core + 2, 4)
    mail = Mail(send, recv)
    channels, grid_rows = xt.shape
    mine = x_ref.shape[1]
    share = h0_mine.shape[1]
    mesh_rows = h0full.shape[1]
    tiles = mine // TILE
    degree = m2m_ref.shape[0]
    latent = h0_mine.shape[0]

    def peer(device):
        return {"hid": device, "rows": row}

    def row_peer(device):
        return {"hid": hid, "rows": device}

    barrier = pltpu.get_barrier_semaphore()
    for device in (core, across, corner):
        pl.semaphore_signal(barrier, inc=1, device_id=peer(device), device_id_type=MESH)
    for step in range(1, row_groups):
        pl.semaphore_signal(
            barrier,
            inc=1,
            device_id=row_peer(lax.rem(row + step, row_groups)),
            device_id_type=MESH,
        )

    my_grid = pl.multiple_of(hid * mine, mine)
    pairs = (
        (first_hbm, first_f),
        (hbias_hbm, hbias_f),
        *((second_hbm.at[k], gland_a.at[1, :, pl.ds(256 * k, 256)]) for k in range(3)),
        *((wide_hbm.at[k], gland_a.at[0, :, pl.ds(512 * k, 512)]) for k in range(3)),
        (last_hbm, last_f),
        (xt_hbm, xt),
        (norm_hbm, norm_f),
        (dbias_hbm, dbias_f),
        (level_hbm, level_f),
        (tt_hbm.at[:, pl.ds(my_grid, mine)], tt),
        (m2m_hbm, m2m_ref),
        (m2g_hbm.at[:, pl.ds(my_grid, mine)], m2g_ref),
        (g2m_hbm, g2m_ref),
    )
    fetches = [
        pltpu.make_async_copy(source, target, local_sem.at[at])
        for at, (source, target) in enumerate(pairs)
    ]
    for fetch in fetches:
        fetch.start()

    def gather_start(view):
        near_copy = mail.copy(view(hid), view(hid), peer(core))
        far_copy = mail.copy(view(hid), view(hid), peer(across))
        return near_copy, far_copy

    def gather_pass(view, copies):
        near_copy, far_copy = copies
        far_copy.wait_recv()
        return near_copy, far_copy, mail.copy(view(across), view(across), peer(core))

    def gather_wait(copies):
        near_copy, far_copy, passed = copies
        near_copy.wait_recv()
        passed.wait_recv()
        near_copy.wait_send()
        far_copy.wait_send()
        passed.wait_send()

    def rows_of(ref, block, size, start=0, width=None):
        width = ref.shape[1] if width is None else width
        return ref.at[pl.ds(pl.multiple_of(block * size, size), size), pl.ds(start, width)]

    def lanes_of(ref, block, size):
        return ref.at[:, pl.ds(pl.multiple_of(block * size, size), size)]

    own_rows = pl.ds(pl.multiple_of(hid * 64, 64), 64)
    square_tmp[...] = jnp.zeros_like(square_tmp)
    for fetch in fetches[:5]:
        fetch.wait()
    square_tmp[0:64, 0:channels] = first_f[...]
    w[own_rows, 0:128] = square_tmp[0:64, :].astype(bf16)
    square_tmp[...] = jnp.zeros_like(square_tmp)
    square_tmp[0:4, 0:64] = hbias_f[...]
    bias[own_rows, :] = square_tmp[...].T[:64]
    for layer, name in enumerate(("g2", "e2", "n2")):
        w[own_rows, COLS[name] : COLS[name] + 256] = gland_a[1, :, 256 * layer : 256 * layer + 256].astype(bf16)
    for fetch in fetches[5:9]:
        fetch.wait()
    for layer, name in enumerate(("e1", "n1", "d1")):
        w[own_rows, COLS[name] : COLS[name] + 512] = gland_a[0, :, 512 * layer : 512 * layer + 512].astype(bf16)
    square_tmp[...] = jnp.zeros_like(square_tmp)
    square_tmp[0:64, 0:channels] = last_f[...]
    w[own_rows, COLS["d2"] : COLS["d2"] + 128] = square_tmp[0:64, :].astype(bf16)
    pl.semaphore_wait(barrier, 3 + row_groups - 1)
    flights = {}
    def weights_start(name):
        start, width = GROUPS[name]
        flights[name] = gather_start(lambda block: rows_of(w, block, 64, start, width))

    weights_start("g")
    flights["b"] = gather_start(lambda block: rows_of(bias, block, 64))

    def weights_pass(name):
        if name == "b":
            flights[name] = gather_pass(lambda block: rows_of(bias, block, 64), flights[name])
            return
        start, width = GROUPS[name]
        flights[name] = gather_pass(
            lambda block: rows_of(w, block, 64, start, width), flights[name]
        )

    for fetch in fetches[9:]:
        fetch.wait()

    def padded(values, to):
        return jnp.concatenate(
            [values.astype(f32), jnp.zeros((to - channels, values.shape[1]), f32)], 0
        )

    def turn(i, carry):
        at = pl.multiple_of(i * TILE, TILE)
        big[pl.ds(at, TILE), :] = padded(xt[:, pl.ds(at, TILE)], 128).T
        return carry

    lax.fori_loop(0, grid_rows // TILE, turn, 0)
    step_rows = 16

    def pick(k, block, unroll=True):
        for half in range(share // 256):

            def rows(i, carry):
                for u in range(step_rows):
                    at = i * step_rows + u
                    nacc[block + half, pl.ds(at, 1), :] = big[
                        pl.ds(pick_ref[k, hid * share + half * 256 + at], 1), :
                    ]
                return carry

            lax.fori_loop(0, 256 // step_rows, rows, 0, unroll=unroll)

    def picked(block):
        return jnp.concatenate(
            [nacc[block + half].T[:PAD].astype(bf16) for half in range(share // 256)], 1
        )

    pick(0, 0, unroll=False)
    square_tmp[...] = jnp.zeros_like(square_tmp)
    for layer in range(3):
        square_tmp[2 * layer : 2 * layer + 2, :] = norm_f[layer][:, :128]
    norm_ref[:128, :] = square_tmp[...].T
    for layer in range(3):
        square_tmp[2 * layer : 2 * layer + 2, :] = norm_f[layer][:, 128:]
    norm_ref[128:, :] = square_tmp[...].T
    square_tmp[...] = jnp.zeros_like(square_tmp)
    square_tmp[0:1, 0:channels] = dbias_f[...]
    square_tmp[1:2, 0:channels] = level_f[...].astype(f32)
    chan_ref[...] = square_tmp[...].T[:PAD]

    for name in "gb":
        weights_pass(name)
    for name in "end":
        weights_start(name)
    gather_wait(flights["g"])
    gather_wait(flights["b"])
    b_g, b_e, b_n, b_d = (bias[:, k : k + 1] for k in range(4))
    gains = [norm_ref[:, 2 * k : 2 * k + 1] for k in range(3)]
    shifts = [norm_ref[:, 2 * k + 1 : 2 * k + 2] for k in range(3)]
    wt[:, 0:256] = flip(w[:, COLS["g2"] : COLS["g2"] + 256])
    w1g = w[:, 0:128][:, :PAD]

    def embed(inputs):
        pre = mm(w1g, inputs) + b_g
        act, slope = act_forward(pre)
        normed, scale = norm_forward(mm(wt[:, 0:256], act))
        return act, slope, normed, scale

    mesh_tmp[0] = jnp.zeros((latent, share), f32)

    def pool(i, carry):
        for half in range(2):
            inputs = picked(2 * half)
            pick(lax.rem(2 * i + half + 1, g2m_deg), 2 - 2 * half)
            mesh_tmp[0] += embed(inputs)[2] * gains[0] + shifts[0]
        return carry

    lax.fori_loop(0, g2m_deg // 2, pool, 0)
    h0_mine[...] = mesh_tmp[0] * (1.0 / g2m_deg)
    my_mesh = pl.ds(pl.multiple_of(hid * share, share), share)
    h0_half = h0_mine[...].astype(bf16)
    h0full[:, my_mesh] = h0_half
    node_in[:latent, :] = h0_half
    h0_view = functools.partial(lanes_of, h0full, size=share)
    h0_flight = gather_start(lambda block: h0_view(block))

    lane = lax.broadcasted_iota(jnp.int32, (1, TILE), 1)
    first_row = hid * mine

    def live_mask(i):
        return (first_row + i * TILE + lane < live_ref[0]).astype(f32)

    def own(i, carry):
        here = pl.ds(pl.multiple_of(i * TILE, TILE), TILE)
        inputs = padded(
            xt[:, pl.ds(pl.multiple_of(my_grid + i * TILE, TILE), TILE)], PAD
        ).astype(bf16)
        x_ref[:, here] = inputs
        act, slope, normed, scale = embed(inputs)
        put(big, 2 * i * 2 * TILE, slope)
        act_g[:, here] = act
        put(big, (2 * i + 1) * 2 * TILE, normed)
        scale_g[:, here] = scale
        dec_in[:latent, here] = (normed * gains[0] + shifts[0]).astype(bf16)
        return carry

    def own_range(a, b):
        lax.fori_loop(a, b, own, 0)

    own_range(0, tiles // 2)
    h0_flight = gather_pass(lambda block: h0_view(block), h0_flight)
    weights_pass("e")
    weights_pass("n")
    weights_pass("d")
    own_range(tiles // 2, tiles)

    cacc[...] = jnp.zeros_like(cacc)

    def squares(i, carry):
        here = pl.ds(pl.multiple_of(i * TILE, TILE), TILE)
        delta = (padded(tt[:, here], PAD) - x_ref[:, here].astype(f32)) * live_mask(i)
        cacc[0] += fold(delta * delta)
        return carry

    lax.fori_loop(0, tiles, squares, 0)
    col = lax.broadcasted_iota(jnp.int32, (PAD, 128), 1)
    live_here = jnp.clip(live_ref[0] - first_row, 0, mine).astype(f32)
    square_tmp[...] = jnp.zeros_like(square_tmp)
    square_tmp[:PAD, :] = jnp.where(
        col == 0, jnp.sum(cacc[0], 1, keepdims=True), jnp.where(col == 1, live_here, 0.0)
    )
    small[...] = square_tmp[...].T[:8]
    sum_hid = [
        mail.copy(small, sland_h.at[slot], peer(device))
        for slot, device in enumerate((core, across, corner))
    ]

    for name in "end":
        gather_wait(flights[name])
    wt[:, 256:512] = flip(w[:, COLS["e2"] : COLS["e2"] + 256])
    wt[:, 512:768] = flip(w[:, COLS["n2"] : COLS["n2"] + 256])
    wt[:128, 768:1024] = flip(w[:, COLS["d2"] : COLS["d2"] + 128])
    gather_wait(h0_flight)

    e1 = COLS["e1"]
    mesh_tmp[0] = mm(w[:, e1 : e1 + 256], node_in[:latent, :]) + b_e
    mesh_tmp[1] = jnp.zeros((latent, share), f32)

    def edge_index(k):
        return m2m_ref[pl.ds(k, 1), my_mesh]

    def fill(index, base, rows):
        for block, part in enumerate(ones_at(index, base, rows)):
            onehot[block * 256 : block * 256 + 256, :] = part

    def edge(k, carry):
        fill(edge_index(k), 0, mesh_rows)
        sent = mm(h0full[...], onehot[...]).astype(bf16)
        hs_e[k] = sent
        pre = mesh_tmp[0] + mm(w[:, e1 + 256 : e1 + 512], sent)
        act, slope = act_forward(pre)
        act_e[k] = act
        ds_e[k] = slope
        normed, scale = norm_forward(mm(wt[:, 256:512], act))
        nrm_e[k] = normed
        scale_e[pl.ds(k, 1), :] = scale
        mesh_tmp[1] += normed * gains[1] + shifts[1]
        return carry

    lax.fori_loop(0, degree, edge, 0)

    for copy in sum_hid:
        copy.wait()
    small[...] = small[...] + sland_h[0] + sland_h[1] + sland_h[2]
    sum_rows = [
        mail.copy(small, sland_r.at[step - 1], row_peer(lax.rem(row + step, row_groups)))
        for step in range(1, row_groups)
    ]
    n1 = COLS["n1"]
    node_in[latent:, :] = mesh_tmp[1].astype(bf16)
    act_n, slope_n = act_forward(mm(w[:, n1 : n1 + 512], node_in[...]) + b_n)
    normed_n, scale_n = norm_forward(mm(wt[:, 512:768], act_n))
    h1 = h0_mine[...] + (normed_n * gains[2] + shifts[2])
    ds_e[degree] = slope_n
    act_e[degree] = act_n
    nrm_e[degree] = normed_n
    scale_e[degree : degree + 1, :] = scale_n
    h1full[:, my_mesh] = h1.astype(bf16)
    h1_view = functools.partial(lanes_of, h1full, size=share)
    h1_flight = gather_start(lambda block: h1_view(block))

    for copy in sum_rows:
        copy.wait()
    totals = small[...]
    for step in range(1, row_groups):
        totals = totals + sland_r[step - 1]
    square_tmp[...] = jnp.zeros_like(square_tmp)
    square_tmp[:8, :] = totals
    totals = square_tmp[...].T[:PAD]
    count = totals[:, 1:2]
    var = totals[:, 0:1] / count + 1e-06
    d_bias = chan_ref[:, 0:1]
    level = chan_ref[:, 1:2]
    loss_weight = count * jnp.sum(level, 0, keepdims=True)
    tot_ref[...] = jnp.broadcast_to(loss_weight[:8], (8, 128))
    weight_var = level / var
    pull = 2.0 * weight_var / loss_weight
    nacc[...] = jnp.zeros_like(nacc)
    cacc[...] = jnp.zeros_like(cacc)
    grad[...] = jnp.zeros_like(grad)
    dsum[...] = jnp.zeros_like(dsum)


    def spot(i, write):
        base = my_grid + i * TILE

        def lanes(k, carry):
            at = pl.multiple_of(k * TILE, TILE)
            for block, part in enumerate(ones_at(g2m_ref[:, pl.ds(at, TILE)], base, TILE)):
                write(block, at, part)
            return carry

        lax.fori_loop(0, mesh_rows // TILE, lanes, 0)

    def spot_store(i, carry):
        def write(block, at, part):
            spots[i, block * 256 : block * 256 + 256, pl.ds(at, TILE)] = part

        spot(i, write)
        return carry

    ready = spots.shape[0]
    lax.fori_loop(0, ready - 1, spot_store, 0)
    h1_flight = gather_pass(lambda block: h1_view(block), h1_flight)
    lax.fori_loop(ready - 1, ready, spot_store, 0)
    gather_wait(h1_flight)

    def chunk(start, width, block):
        return rows_of(grad, block, 64, start, width)

    def reduce_start(name):
        start, width = GROUPS[name]
        flight = (
            mail.copy(
                chunk(start, width, corner), gland_a.at[1, :, pl.ds(start, width)], peer(core)
            ),
            mail.copy(
                chunk(start, width, core), gland_a.at[0, :, pl.ds(start, width)], peer(core)
            ),
        )
        return flight

    def reduce_across(name, flight):
        start, width = GROUPS[name]
        cols = pl.ds(start, width)
        flight[0].wait()
        view = chunk(start, width, across)
        view[...] = view[...] + gland_a[1, :, cols]
        return flight + (mail.copy(view, gland_b.at[:, cols], peer(across)),)

    def reduce_rows(name, flight):
        start, width = GROUPS[name]
        cols = pl.ds(start, width)
        flight[1].wait()
        flight[2].wait()
        part = 64 // near
        held[:, cols] = chunk(start, width, hid)[...] + gland_a[0, :, cols] + gland_b[:, cols]
        copies = []
        for step in range(1, near):
            to = lax.rem(row_near + step, near)
            copies.append(
                mail.copy(
                    held.at[pl.ds(pl.multiple_of(to * part, part), part), cols],
                    gland.at[step - 1],
                    row_peer(row_far * near + to),
                )
            )
        return copies

    def far_sum(own_part, cols, total):
        if far > 1:
            own_part[...] = total
            more = []
            for step in range(1, far):
                to = lax.rem(row_far + step, far)
                more.append(
                    mail.copy(
                        own_part,
                        fland.at[step - 1, :, cols],
                        row_peer(to * near + row_near),
                    )
                )
            for copy in more:
                copy.wait()
            for step in range(1, far):
                total = total + fland[step - 1, :, cols]
        return total

    side = lax.rem(row_near, 2)
    level = row_near // 2
    neighbour = row_far * near + 2 * level + 1 - side

    def half_rows(which):
        return pl.ds(pl.multiple_of(which * 32, 32), 32)

    def part_rows(where):
        return pl.ds(pl.multiple_of(side * 32 + where * 8, 8), 8)

    def level_peer(where):
        return row_peer(row_far * near + 2 * where + side)

    def rows_halve(name, flight):
        start, width = GROUPS[name]
        cols = pl.ds(start, width)
        flight[1].wait()
        flight[2].wait()
        held[:, cols] = chunk(start, width, hid)[...] + gland_a[0, :, cols] + gland_b[:, cols]
        return [
            mail.copy(held.at[half_rows(1 - side), cols], yland.at[:, cols], row_peer(neighbour))
        ]

    def rows_part(name, copies):
        start, width = GROUPS[name]
        cols = pl.ds(start, width)
        copies[0].wait()
        held[half_rows(side), cols] = held[half_rows(side), cols] + yland[:, cols]
        out = []
        for step in range(1, near // 2):
            to = lax.rem(level + step, near // 2)
            out.append(
                mail.copy(
                    held.at[part_rows(to), cols], rland.at[step - 1, :, cols], level_peer(to)
                )
            )
        return out

    def rows_total(name, copies):
        start, width = GROUPS[name]
        cols = pl.ds(start, width)
        for copy in copies:
            copy.wait()
        total = held[part_rows(level), cols]
        for step in range(1, near // 2):
            total = total + rland[step - 1, :, cols]
        own_part = out_ref.at[part_rows(level), cols]
        own_part[...] = far_sum(own_part, cols, total)
        out = []
        for step in range(1, near // 2):
            to = lax.rem(level + step, near // 2)
            out.append(mail.copy(own_part, own_part, level_peer(to)))
        return out

    def rows_back(name, copies):
        start, width = GROUPS[name]
        for copy in copies:
            copy.wait()
        view = out_ref.at[half_rows(side), pl.ds(start, width)]
        return [mail.copy(view, view, row_peer(neighbour))]

    def reduce_share(name, copies):
        start, width = GROUPS[name]
        cols = pl.ds(start, width)
        part = 64 // near
        shared = pl.ds(pl.multiple_of(row_near * part, part), part)
        own_part = out_ref.at[shared, cols]
        for copy in copies:
            copy.wait()
        total = held[shared, cols]
        for step in range(1, near):
            total = total + gland[step - 1]
        own_part[...] = far_sum(own_part, cols, total)
        out = []
        for step in range(1, near):
            to = lax.rem(row_near + step, near)
            out.append(mail.copy(own_part, own_part, row_peer(row_far * near + to)))
        return out

    d1, d2 = COLS["d1"], COLS["d2"]
    def decode(i, carry):
        here = pl.ds(pl.multiple_of(i * TILE, TILE), TILE)
        fill(m2g_ref[:, here], 0, mesh_rows)
        back = mm(h1full[...], onehot[...]) * (1.0 / m2g_deg)
        dec_in[latent:, here] = back.astype(bf16)
        pre = mm(w[:, d1 : d1 + 512], dec_in[:, here]) + b_d
        act, slope = act_forward(pre)
        out = mm(wt[:128, 768:1024], act)[:PAD]
        err = x_ref[:, here].astype(f32) + out + d_bias - padded(tt[:, here], PAD)
        kept = err * live_mask(i)
        cacc[1] += fold(weight_var * kept * err)
        pred_grad = pull * kept
        cacc[0] += fold(pred_grad)
        upstream = pred_grad.astype(bf16)
        act_grad = mm(w[:, d2 : d2 + 128][:, :PAD], upstream)
        pre_grad = (act_grad * slope).astype(bf16)
        dp_d[:, here] = pre_grad
        dsum[...] += mt(onehot[...], pre_grad)
        grad[:, d2 : d2 + PAD] += mt(act, upstream)
        return carry

    lax.fori_loop(0, tiles, decode, 0)

    def spread_start(view, land):
        return (
            mail.copy(view(corner), land.at[1], peer(core)),
            mail.copy(view(core), land.at[0], peer(core)),
        )

    def spread_across(view, land, land_far, out, copies):
        copies[0].wait()
        out[...] = (view(across)[...] + land[1]).astype(bf16)
        return copies + (mail.copy(out, land_far, peer(across)),)

    def spread_end(view, land, land_far, copies):
        copies[1].wait()
        copies[2].wait()
        return view(hid)[...] + land[0] + land_far[...].astype(f32)

    def view_d(block):
        return dsum.at[pl.ds(pl.multiple_of(block * share, share), share), :]

    d_flight = spread_start(view_d, land_a.at[0])
    w1d_low = flip(w[:, d1 : d1 + 256])
    wt[:, 1024:1280] = w1d_low
    d_flight = spread_across(view_d, land_a.at[0], land_b.at[0], half_out, d_flight)

    def decode_rest(i, carry):
        here = pl.ds(pl.multiple_of(i * TILE, TILE), TILE)
        pre_grad = dp_d[:, here]
        grad[:, d1 : d1 + 512] += mt(pre_grad, dec_in[:, here])
        nacc[9] += fold(pre_grad.astype(f32))
        return carry

    lax.fori_loop(0, tiles, decode_rest, 0)
    stage = {"d": reduce_start("d")}
    wt[:, 2304:2560] = flip(w[:, d1 + 256 : d1 + 512])
    wt[:, 1280:1536] = flip(w[:, n1 : n1 + 256])
    wt[:, 1536:1792] = flip(w[:, n1 + 256 : n1 + 512])
    wt[:, 1792:2048] = flip(w[:, e1 : e1 + 256])
    wt[:, 2048:2304] = flip(w[:, e1 + 256 : e1 + 512])

    def late_store(half, carry):
        def write(block, at, part):
            lanes = pl.ds(pl.multiple_of(half * mesh_rows + at, TILE), TILE)
            dec_in[block * 256 : block * 256 + 256, lanes] = part

        spot(ready + half, write)
        return carry

    def write_last(block, at, part):
        (h0full, h1full)[block][:, pl.ds(at, TILE)] = part

    lax.fori_loop(0, 2, late_store, 0)

    def write_pieces(block, at, part):
        (hs_e, act_e)[block][at // TILE] = part

    def write_whole(block, at, part):
        onehot[pl.ds(pl.multiple_of(at + block * 256, 256), 256), :] = part

    high, low = split2(spread_end(view_d, land_a.at[0], land_b.at[0], d_flight))
    stage["d"] = reduce_across("d", stage["d"])
    h1_grad = (mt(wt[:, 2304:2560], high) + mt(wt[:, 2304:2560], low)) * (1.0 / m2g_deg)
    nacc[2] += fold(h1_grad * nrm_e[degree])
    nacc[5] += fold(h1_grad)
    up_n = norm_backward(
        h1_grad, nrm_e[degree], scale_e[degree : degree + 1, :], gains[2]
    ).astype(bf16)
    n2 = COLS["n2"]
    pre_grad_n = (mm(w[:, n2 : n2 + 256], up_n) * ds_e[degree]).astype(bf16)
    mesh_tmp[0] = h1_grad + mm(wt[:, 1280:1536], pre_grad_n)
    mesh_tmp[1] = mm(wt[:, 1536:1792], pre_grad_n)

    grad[:, n2 : n2 + 256] = mt(act_e[degree], up_n)
    grad[:, n1 : n1 + 512] = mt(pre_grad_n, node_in[...])
    nacc[8] += fold(pre_grad_n.astype(f32))
    stage["n"] = reduce_start("n")

    e2 = COLS["e2"]

    def edge_back(k, carry):
        upstream = mesh_tmp[1]
        normed = nrm_e[k]
        nacc[1] += fold(upstream * normed)
        nacc[4] += fold(upstream)
        up = norm_backward(upstream, normed, scale_e[pl.ds(k, 1), :], gains[1]).astype(bf16)
        pre_grad = (mm(w[:, e2 : e2 + 256], up) * ds_e[k]).astype(bf16)
        mesh_tmp[0] += mm(wt[:, 1792:2048], pre_grad)
        grad[:, e2 : e2 + 256] += mt(act_e[k], up)
        act_e[k] = pre_grad
        nacc[7] += fold(pre_grad.astype(f32))
        return carry

    lax.fori_loop(0, degree, edge_back, 0)
    stage["d"] = rows_halve("d", stage["d"])
    stage["n"] = reduce_across("n", stage["n"])

    def senders(block):
        total = None
        for k in range(degree):
            place = k % 4 * TILE
            for half, part in enumerate(ones_at(edge_index(k), block * share, share)):
                onehot[place + half * 256 : place + half * 256 + 256, :] = part
            term = mt(onehot[place : place + TILE, :], act_e[k])
            total = term if total is None else total + term
        view_d(block)[...] = total

    senders(corner)
    e_first = mail.copy(view_d(corner), land_a.at[1, 1], peer(core))
    senders(core)
    e_flight = (e_first, mail.copy(view_d(core), land_a.at[1, 0], peer(core)))
    senders(across)
    stage["d"] = rows_part("d", stage["d"])
    e_flight = spread_across(view_d, land_a.at[1], land_b.at[1], half_out, e_flight)
    senders(hid)

    def edge_weights(k, carry):
        grad[:, e1 : e1 + 256] += mt(act_e[k], node_in[:latent, :])
        grad[:, e1 + 256 : e1 + 512] += mt(act_e[k], hs_e[k])
        return carry

    lax.fori_loop(0, degree, edge_weights, 0)
    stage["e"] = reduce_start("e")
    stage["n"] = rows_halve("n", stage["n"])
    stage["d"] = rows_total("d", stage["d"])
    high, low = split2(spread_end(view_d, land_a.at[1], land_b.at[1], e_flight))
    h0_grad = mesh_tmp[0] + mt(wt[:, 2048:2304], high) + mt(wt[:, 2048:2304], low)
    hgfull[:, my_mesh] = (h0_grad * (1.0 / g2m_deg)).astype(bf16)
    hg_view = functools.partial(lanes_of, hgfull, size=share)
    hg_flight = gather_start(lambda block: hg_view(block))


    spot(ready + 2, write_last)
    stage["n"] = rows_part("n", stage["n"])
    stage["d"] = rows_back("d", stage["d"])
    spot(ready + 3, write_pieces)
    hg_flight = gather_pass(lambda block: hg_view(block), hg_flight)
    stage["e"] = reduce_across("e", stage["e"])
    spot(ready + 4, write_whole)
    stage["n"] = rows_total("n", stage["n"])
    gather_wait(hg_flight)

    def grid_back(i, both):
        here = pl.ds(pl.multiple_of(i * TILE, TILE), TILE)
        upstream = mm(wt[:, 1024:1280], dp_d[:, here]) + both
        normed = take(big, (2 * i + 1) * 2 * TILE)
        nacc[0] += fold(upstream * normed)
        nacc[3] += fold(upstream)
        up = norm_backward(upstream, normed, scale_g[:, here], gains[0]).astype(bf16)
        pre_grad = (mm(w[:, COLS["g2"] : COLS["g2"] + 256], up) * take(big, 2 * i * 2 * TILE)).astype(bf16)
        grad[:, COLS["g2"] : COLS["g2"] + 256] += mt(act_g[:, here], up)
        grad[:, 0:PAD] += mt(pre_grad, x_ref[:, here])
        nacc[6] += fold(pre_grad.astype(f32))

    def grid_ready(i, carry):
        grid_back(i, mt(hgfull[...], spots[i]))
        return carry

    def from_blocks(blocks):
        total = None
        for at, block in enumerate(blocks):
            term = mt(hgfull[:, at * TILE : at * TILE + TILE], block[...])
            total = term if total is None else total + term
        return total

    count_m = mesh_rows // TILE
    lax.fori_loop(0, ready, grid_ready, 0)
    stage["n"] = rows_back("n", stage["n"])
    stage["e"] = rows_halve("e", stage["e"])

    def grid_late(half, carry):
        lanes = pl.ds(pl.multiple_of(half * mesh_rows, mesh_rows), mesh_rows)
        grid_back(ready + half, mt(hgfull[...], dec_in[:, lanes]))
        return carry

    lax.fori_loop(0, 2, grid_late, 0)
    dsum[0:256, :] = mt(hgfull[...], h0full[...])
    dsum[256:512, :] = mt(hgfull[...], h1full[...])
    for half, blocks in enumerate((hs_e, act_e)):
        dsum[512 + 256 * half : 768 + 256 * half, :] = from_blocks(
            [blocks.at[k] for k in range(count_m)]
        )
    both = from_blocks([onehot.at[k * TILE : k * TILE + TILE, :] for k in range(count_m)])
    dsum[1024:1280, :] = both[:, :256]
    dsum[1280:1536, :] = both[:, 256:]

    def grid_last(k, carry):
        at = pl.multiple_of(k * TILE, TILE)
        both = jnp.concatenate([dsum[pl.ds(at, 256), :], dsum[pl.ds(at + 256, 256), :]], 1)
        grid_back(ready + 2 + k, both)
        return carry

    stage["e"] = rows_part("e", stage["e"])
    lax.fori_loop(0, 3, grid_last, 0)

    block = grad[:, 0:128]
    at_col = lax.broadcasted_iota(jnp.int32, (latent, 128), 1)
    for k in range(4):
        block = jnp.where(at_col == PAD + k, jnp.sum(nacc[6 + k], 1, keepdims=True), block)
    grad[:, 0:128] = block
    stage["g"] = reduce_start("g")
    block = jnp.zeros((latent, 128), f32)
    for k in range(6):
        block = jnp.where(at_col == 2 * (k % 3) + k // 3, jnp.sum(nacc[k], 1, keepdims=True), block)
    norm_ref[...] = block
    block = norm_ref[:PAD, :]
    for k in range(2):
        block = jnp.where(col == 6 + k, jnp.sum(cacc[k], 1, keepdims=True), block)
    norm_ref[:PAD, :] = block
    narrow[...] = norm_ref[...].T[:8]
    narrow_hid = [
        mail.copy(narrow, nland_h.at[slot], peer(device))
        for slot, device in enumerate((core, across, corner))
    ]
    stage["e"] = rows_total("e", stage["e"])
    stage["g"] = reduce_across("g", stage["g"])
    for copy in narrow_hid:
        copy.wait()
    narrow[...] = narrow[...] + nland_h[0] + nland_h[1] + nland_h[2]
    narrow_rows = [
        mail.copy(narrow, nland_r.at[step - 1], row_peer(lax.rem(row + step, row_groups)))
        for step in range(1, row_groups)
    ]
    stage["e"] = rows_back("e", stage["e"])
    stage["g"] = reduce_rows("g", stage["g"])
    stage["g"] = reduce_share("g", stage["g"])
    for copy in narrow_rows:
        copy.wait()
    total = narrow[...]
    for step in range(1, row_groups):
        total = total + nland_r[step - 1]
    all_ref[...] = total
    for name in "dneg":
        for copy in stage[name]:
            copy.wait()


def adam_step(weight, avg, sq, grad, rate, decay):
    avg_new = 0.5 * avg + 0.5 * grad
    sq_new = 0.5 * sq + 0.5 * grad * grad
    fix = 1.0 - 0.5**STEP_COUNT
    step = (avg_new * (1.0 / fix)) / (jnp.sqrt(sq_new * (1.0 / fix)) + 1e-08)
    return (weight - rate * (step + decay * weight), avg_new, sq_new)


def adam_kernel(out_ref, all_ref, tot_ref, *refs):
    ins_hbm, outs_hbm, loss_ref, weight_ref = refs[:21], refs[21:46], refs[46], refs[47]
    ins, outs, turned, sem_in, sem_out = refs[48:69], refs[69:94], refs[94], refs[95], refs[96]
    fetches = [
        pltpu.make_async_copy(source, target, sem_in.at[at])
        for at, (source, target) in enumerate(zip(ins_hbm, ins))
    ]
    for fetch in fetches:
        fetch.start()
    stores = []

    def arrive(array):
        for part in (array, 7 + array, 14 + array):
            fetches[part].wait()

    def leave(array):
        for part in (array, 7 + array, 14 + array) + ((21 + array,) if array < 4 else ()):
            store = pltpu.make_async_copy(outs[part], outs_hbm[part], sem_out.at[part])
            store.start()
            stores.append(store)

    def update(array, at, grad, rate, decay):
        fresh, avg_new, sq_new = adam_step(
            ins[array][at], ins[7 + array][at], ins[14 + array][at], grad, rate, decay
        )
        outs[array][at] = fresh
        outs[7 + array][at] = avg_new
        outs[14 + array][at] = sq_new
        if array < 4:
            outs[21 + array][at] = fresh.astype(bf16)

    everything = (slice(None), slice(None))
    channels = ins[0].shape[1]
    arrive(1)
    for layer, name in enumerate(("e1", "n1", "d1")):
        update(1, (layer,) + everything, out_ref[:, COLS[name] : COLS[name] + 512], 0.05, 0.1)
    leave(1)
    arrive(2)
    for layer, name in enumerate(("g2", "e2", "n2")):
        update(2, (layer,) + everything, out_ref[:, COLS[name] : COLS[name] + 256], 0.05, 0.1)
    leave(2)
    arrive(0)
    update(0, everything, out_ref[:, 0:128][:, :channels], 0.05, 0.1)
    leave(0)
    arrive(3)
    update(3, everything, out_ref[:, COLS["d2"] : COLS["d2"] + 128][:, :channels], 0.05, 0.1)
    leave(3)
    turned[...] = out_ref[:, 0:128].T
    arrive(4)
    update(4, everything, turned[PAD : PAD + 4, :], 0.3, 0.0)
    leave(4)
    arrive(5)
    for layer in range(3):
        update(5, (layer,) + everything, all_ref[2 * layer : 2 * layer + 2, :], 0.3, 0.0)
    leave(5)
    arrive(6)
    update(6, everything, all_ref[6:7, 0:channels], 0.3, 0.0)
    leave(6)
    loss_ref[...] = jnp.sum(all_ref[7:8, 0:PAD], 1, keepdims=True)
    weight_ref[...] = tot_ref[0:1, 0:1]
    for store in stores:
        store.wait()


def body(
    grid_input,
    grid_target,
    live_points,
    level_weight,
    g2m_index,
    m2m_index,
    m2g_index,
    *params,
):
    groups = lax.axis_size("hid")
    row_groups = lax.axis_size("rows")
    masters, avgs, squares = params[:7], params[7:14], params[14:21]
    grid_rows, channels = grid_input.shape
    mesh_rows, degree = m2m_index.shape
    latent = masters[5].shape[2]
    share = mesh_rows // groups
    mine = grid_rows // groups
    g2m_deg = g2m_index.shape[1]
    m2g_deg = m2g_index.shape[1]
    whole = pl.BlockSpec(memory_space=pltpu.VMEM)
    scalar = pl.BlockSpec(memory_space=pltpu.SMEM)
    far_memory = pl.BlockSpec(memory_space=pltpu.HBM)
    g2m = g2m_index.T

    def flat(arrays):
        first, wide, second, last, bias, norm, out_bias = arrays
        return (
            first.T,
            wide.transpose(0, 2, 1),
            second,
            last,
            bias,
            norm.transpose(1, 0, 2),
            out_bias[None],
        )

    operands = flat(masters) + flat(avgs) + flat(squares)
    loads = [
        grid_input.T,
        grid_target.T,
        g2m,
        m2m_index.T,
        m2g_index.T,
        *operands[:7],
        level_weight[None],
    ]
    kept = [jax.ShapeDtypeStruct(v.shape, v.dtype) for v in loads]
    for at in (1, 4):
        kept[at] = jax.ShapeDtypeStruct((kept[at].shape[0], mine), kept[at].dtype)
    copies = count_copies(row_groups)
    near = min(row_groups, 8)
    far = row_groups // near
    summed, spare, totals = pl.pallas_call(
        functools.partial(
            main_kernel, row_groups=row_groups, g2m_deg=g2m_deg, m2g_deg=m2g_deg
        ),
        out_shape=[
            jax.ShapeDtypeStruct((64, PACK), f32),
            jax.ShapeDtypeStruct((8, 256), f32),
            jax.ShapeDtypeStruct((8, 128), f32),
        ],
        in_specs=[scalar] * 2 + [far_memory] * 13,
        out_specs=[whole] * 3,
        scratch_shapes=[pltpu.VMEM(v.shape, v.dtype) for v in kept[:6] + kept[8:]]
        + [
            pltpu.SemaphoreType.DMA((17,)),
            pltpu.VMEM((128, 128), f32),
            pltpu.VMEM((latent, 128), f32),
            pltpu.VMEM((PAD, 128), f32),
            pltpu.VMEM((grid_rows, 128), f32),
            pltpu.VMEM((PAD, mine), bf16),
            pltpu.VMEM((256, PACK), bf16),
            pltpu.VMEM((256, 2560), bf16),
            pltpu.VMEM((256, 128), f32),
            pltpu.VMEM((latent, mesh_rows), bf16),
            pltpu.VMEM((latent, mesh_rows), bf16),
            pltpu.VMEM((latent, mesh_rows), bf16),
            pltpu.VMEM((mesh_rows, TILE), bf16),
            pltpu.VMEM((3, TILE, mesh_rows), bf16),
            pltpu.VMEM((latent, mine), bf16),
            pltpu.VMEM((1, mine), f32),
            pltpu.VMEM((2 * latent, mine), bf16),
            pltpu.VMEM((latent, mine), bf16),
            pltpu.VMEM((degree + 1, latent, share), f32),
            pltpu.VMEM((degree + 1, latent, share), bf16),
            pltpu.VMEM((degree, latent, share), bf16),
            pltpu.VMEM((degree + 1, latent, share), f32),
            pltpu.VMEM((8, share), f32),
            pltpu.VMEM((mesh_rows, latent), f32),
            pltpu.VMEM((2, 2, share, latent), f32),
            pltpu.VMEM((2, share, latent), bf16),
            pltpu.VMEM((share, latent), bf16),
            pltpu.VMEM((256, PACK), f32),
            pltpu.VMEM((2, 64, PACK), f32),
            pltpu.VMEM((64, PACK), f32),
            pltpu.VMEM((64, PACK), f32),
            pltpu.VMEM((32, PACK), f32),
            pltpu.VMEM((near - 1, 64 // near, GROUPS["g"][1]), f32),
            pltpu.VMEM((near // 2 - 1, 64 // near, PACK), f32),
            pltpu.VMEM((max(far - 1, 1), 64 // near, PACK), f32),
            pltpu.VMEM((g2m_deg * share // 256, 256, 128), f32),
            pltpu.VMEM((2, PAD, 128), f32),
            pltpu.VMEM((latent, share), f32),
            pltpu.VMEM((2 * latent, share), bf16),
            pltpu.VMEM((2, latent, share), f32),
            pltpu.VMEM((8, 128), f32),
            pltpu.VMEM((3, 8, 128), f32),
            pltpu.VMEM((row_groups - 1, 8, 128), f32),
            pltpu.VMEM((8, 256), f32),
            pltpu.VMEM((3, 8, 256), f32),
            pltpu.VMEM((row_groups - 1, 8, 256), f32),
            pltpu.SemaphoreType.DMA((copies,)),
            pltpu.SemaphoreType.DMA((copies,)),
        ],
        compiler_params=pltpu.CompilerParams(
            collective_id=0, has_side_effects=True, vmem_limit_bytes=64 * 2**20
        ),
        name="step",
    )(
        live_points,
        g2m,
        *loads,
    )
    shapes = [jax.ShapeDtypeStruct(v.shape, f32) for v in operands]
    shapes += [jax.ShapeDtypeStruct(v.shape, bf16) for v in operands[:4]]
    outs = pl.pallas_call(
        adam_kernel,
        out_shape=shapes + [jax.ShapeDtypeStruct((1, 1), f32)] * 2,
        in_specs=[whole] * 3 + [far_memory] * 21,
        out_specs=[far_memory] * 25 + [whole] * 2,
        scratch_shapes=[pltpu.VMEM(v.shape, v.dtype) for v in operands + tuple(shapes)]
        + [
            pltpu.VMEM((128, 64), f32),
            pltpu.SemaphoreType.DMA((21,)),
            pltpu.SemaphoreType.DMA((25,)),
        ],
        compiler_params=pltpu.CompilerParams(vmem_limit_bytes=64 * 2**20),
        name="adam",
    )(summed, spare, totals, *operands)

    def unflat(arrays):
        first, wide, second, last, bias, norm, out_bias = arrays
        return (
            first.T,
            wide.transpose(0, 2, 1),
            second,
            last,
            bias,
            norm.transpose(1, 0, 2),
            out_bias[0],
        )

    halves = outs[21:25]
    return (
        (outs[25][0, 0], outs[26][0, 0])
        + unflat(outs[0:7])
        + unflat(outs[7:14])
        + unflat(outs[14:21])
        + (halves[0].T, halves[1].transpose(0, 2, 1), halves[2], halves[3])
    )


def solution(mesh):
    weights = (
        P(None, "hid"),
        P(None, None, "hid"),
        P(None, "hid", None),
        P("hid", None),
        P(None, "hid"),
        P(),
        P(),
    )
    in_specs = (
        P("rows", None),
        P("rows", None),
        P("rows"),
        P(),
        P("rows", None),
        P("rows", None),
        P("rows", None),
    ) + weights * 3
    out_specs = (P(), P()) + weights * 3 + weights[:4]
    return jax.shard_map(body, mesh=mesh, in_specs=in_specs, out_specs=out_specs, check_vma=False)
```

```python
import functools

import jax
import jax.numpy as jnp
from jax import lax
from jax.experimental import pallas as pl
from jax.experimental.pallas import tpu as pltpu
from jax.sharding import PartitionSpec as P

STEP_COUNT = 5
MESH = pl.DeviceIdType.MESH
bf16 = jnp.bfloat16
f32 = jnp.float32
TILE = 512
PAD = 80
COLS = {"g1": 0, "g2": 128, "e1": 384, "e2": 896, "n1": 1152, "n2": 1664, "d1": 1920, "d2": 2432}
GROUPS = {"g": (0, 384), "e": (384, 768), "n": (1152, 768), "d": (1920, 640)}
PACK = 2560


def mm(left, right):
    return lax.dot_general(left, right, (((1,), (0,)), ((), ())), preferred_element_type=f32)


def mt(left, right):
    return lax.dot_general(left, right, (((1,), (1,)), ((), ())), preferred_element_type=f32)


def flip(values):
    return values.astype(f32).T.astype(bf16)


def split2(values):
    high = values.astype(bf16)
    low = (values - high.astype(f32)).astype(bf16)
    return high, low


def fold(values):
    total = values[:, :128]
    for at in range(128, values.shape[1], 128):
        total = total + values[:, at : at + 128]
    return total


def ones_at(index, base, rows):
    lanes = index.shape[1]
    local = lax.broadcasted_iota(jnp.int32, (256, lanes), 0).astype(f32).astype(bf16)
    parts = []
    for block in range(rows // 256):
        total = None
        for k in range(index.shape[0]):
            shifted = (index[k : k + 1] - (base + block * 256)).astype(f32).astype(bf16)
            hit = jnp.where(
                jnp.broadcast_to(shifted, (256, lanes)) == local,
                jnp.asarray(1, bf16),
                jnp.asarray(0, bf16),
            )
            total = hit if total is None else total + hit
        parts.append(total)
    return parts


def act_forward(pre):
    sigma = 0.5 * jnp.tanh(0.5 * pre) + 0.5
    act = pre * sigma
    return act.astype(bf16), sigma + act * (1.0 - sigma)


def norm_forward(values):
    size = values.shape[0]
    centre = values - jnp.sum(values, 0, keepdims=True) * (1.0 / size)
    var = jnp.sum(centre * centre, 0, keepdims=True) * (1.0 / size)
    scale = lax.rsqrt(var + 1e-05)
    return centre * scale, scale


def norm_backward(upstream, normed, scale, gain):
    size = upstream.shape[0]
    scaled = upstream * gain
    first = jnp.sum(scaled, 0, keepdims=True) * (1.0 / size)
    second = jnp.sum(scaled * normed, 0, keepdims=True) * (1.0 / size)
    return scale * (scaled - first - normed * second)


class Mail:
    def __init__(self, send, recv):
        self.send, self.recv, self.used = send, recv, 0

    def copy(self, source, target, device):
        at = self.used
        self.used += 1
        if self.send is None:
            return None
        copy = pltpu.make_async_remote_copy(
            src_ref=source,
            dst_ref=target,
            send_sem=self.send.at[at],
            recv_sem=self.recv.at[at],
            device_id=device,
            device_id_type=MESH,
        )
        copy.start()
        return copy


def count_copies(row_groups):
    near = min(row_groups, 8)
    far = row_groups // near
    sums = 3 + (row_groups - 1)
    rows_sum = 3 * (2 + 2 * (near // 2 - 1)) + 2 * (near - 1) + 4 * (far - 1)
    return 15 + 9 + 6 + 2 * sums + 4 * 3 + rows_sum


def put(ref, at, values):
    for c in range(0, TILE, 128):
        ref[pl.ds(pl.multiple_of(at + 2 * c, 256), 256), :] = values[:, c : c + 128]


def take(ref, at):
    return jnp.concatenate(
        [ref[pl.ds(pl.multiple_of(at + 2 * c, 256), 256), :] for c in range(0, TILE, 128)], 1
    )


def main_kernel(
    live_ref,
    pick_ref,
    xt_hbm,
    tt_hbm,
    g2m_hbm,
    m2m_hbm,
    m2g_hbm,
    first_hbm,
    wide_hbm,
    second_hbm,
    last_hbm,
    hbias_hbm,
    norm_hbm,
    dbias_hbm,
    level_hbm,
    out_ref,
    all_ref,
    tot_ref,
    xt,
    tt,
    g2m_ref,
    m2m_ref,
    m2g_ref,
    first_f,
    last_f,
    hbias_f,
    norm_f,
    dbias_f,
    level_f,
    local_sem,
    square_tmp,
    norm_ref,
    chan_ref,
    big,
    x_ref,
    w,
    wt,
    bias,
    h0full,
    h1full,
    hgfull,
    onehot,
    spots,
    act_g,
    scale_g,
    dec_in,
    dp_d,
    ds_e,
    act_e,
    hs_e,
    nrm_e,
    scale_e,
    dsum,
    land_a,
    land_b,
    half_out,
    grad,
    gland_a,
    gland_b,
    held,
    yland,
    gland,
    rland,
    fland,
    nacc,
    cacc,
    h0_mine,
    node_in,
    mesh_tmp,
    small,
    sland_h,
    sland_r,
    narrow,
    nland_h,
    nland_r,
    send,
    recv,
    *,
    row_groups,
    g2m_deg,
    m2g_deg,
):
    hid = lax.axis_index("hid")
    row = lax.axis_index("rows")
    near = min(row_groups, 8)
    far = row_groups // near
    row_near = lax.rem(row, near)
    row_far = row // near
    core = hid + 1 - 2 * lax.rem(hid, 2)
    across = lax.rem(hid + 2, 4)
    corner = lax.rem(core + 2, 4)
    mail = Mail(send, recv)
    channels, grid_rows = xt.shape
    mine = x_ref.shape[1]
    share = h0_mine.shape[1]
    mesh_rows = h0full.shape[1]
    tiles = mine // TILE
    degree = m2m_ref.shape[0]
    latent = h0_mine.shape[0]

    def peer(device):
        return {"hid": device, "rows": row}

    def row_peer(device):
        return {"hid": hid, "rows": device}

    barrier = pltpu.get_barrier_semaphore()
    for device in (core, across, corner):
        pl.semaphore_signal(barrier, inc=1, device_id=peer(device), device_id_type=MESH)
    for step in range(1, row_groups):
        pl.semaphore_signal(
            barrier,
            inc=1,
            device_id=row_peer(lax.rem(row + step, row_groups)),
            device_id_type=MESH,
        )

    my_grid = pl.multiple_of(hid * mine, mine)
    pairs = (
        (first_hbm, first_f),
        (hbias_hbm, hbias_f),
        *((second_hbm.at[k], gland_a.at[1, :, pl.ds(256 * k, 256)]) for k in range(3)),
        *((wide_hbm.at[k], gland_a.at[0, :, pl.ds(512 * k, 512)]) for k in range(3)),
        (last_hbm, last_f),
        (xt_hbm, xt),
        (norm_hbm, norm_f),
        (dbias_hbm, dbias_f),
        (level_hbm, level_f),
        (tt_hbm.at[:, pl.ds(my_grid, mine)], tt),
        (m2m_hbm, m2m_ref),
        (m2g_hbm.at[:, pl.ds(my_grid, mine)], m2g_ref),
        (g2m_hbm, g2m_ref),
    )
    fetches = [
        pltpu.make_async_copy(source, target, local_sem.at[at])
        for at, (source, target) in enumerate(pairs)
    ]
    for fetch in fetches:
        fetch.start()

    def gather_start(view):
        near_copy = mail.copy(view(hid), view(hid), peer(core))
        far_copy = mail.copy(view(hid), view(hid), peer(across))
        return near_copy, far_copy

    def gather_pass(view, copies):
        near_copy, far_copy = copies
        far_copy.wait_recv()
        return near_copy, far_copy, mail.copy(view(across), view(across), peer(core))

    def gather_wait(copies):
        near_copy, far_copy, passed = copies
        near_copy.wait_recv()
        passed.wait_recv()
        near_copy.wait_send()
        far_copy.wait_send()
        passed.wait_send()

    def rows_of(ref, block, size, start=0, width=None):
        width = ref.shape[1] if width is None else width
        return ref.at[pl.ds(pl.multiple_of(block * size, size), size), pl.ds(start, width)]

    def lanes_of(ref, block, size):
        return ref.at[:, pl.ds(pl.multiple_of(block * size, size), size)]

    own_rows = pl.ds(pl.multiple_of(hid * 64, 64), 64)
    square_tmp[...] = jnp.zeros_like(square_tmp)
    for fetch in fetches[:5]:
        fetch.wait()
    square_tmp[0:64, 0:channels] = first_f[...]
    w[own_rows, 0:128] = square_tmp[0:64, :].astype(bf16)
    square_tmp[...] = jnp.zeros_like(square_tmp)
    square_tmp[0:4, 0:64] = hbias_f[...]
    bias[own_rows, :] = square_tmp[...].T[:64]
    for layer, name in enumerate(("g2", "e2", "n2")):
        w[own_rows, COLS[name] : COLS[name] + 256] = gland_a[1, :, 256 * layer : 256 * layer + 256].astype(bf16)
    for fetch in fetches[5:9]:
        fetch.wait()
    for layer, name in enumerate(("e1", "n1", "d1")):
        w[own_rows, COLS[name] : COLS[name] + 512] = gland_a[0, :, 512 * layer : 512 * layer + 512].astype(bf16)
    square_tmp[...] = jnp.zeros_like(square_tmp)
    square_tmp[0:64, 0:channels] = last_f[...]
    w[own_rows, COLS["d2"] : COLS["d2"] + 128] = square_tmp[0:64, :].astype(bf16)
    pl.semaphore_wait(barrier, 3 + row_groups - 1)
    flights = {}
    def weights_start(name):
        start, width = GROUPS[name]
        flights[name] = gather_start(lambda block: rows_of(w, block, 64, start, width))

    weights_start("g")
    flights["b"] = gather_start(lambda block: rows_of(bias, block, 64))

    def weights_pass(name):
        if name == "b":
            flights[name] = gather_pass(lambda block: rows_of(bias, block, 64), flights[name])
            return
        start, width = GROUPS[name]
        flights[name] = gather_pass(
            lambda block: rows_of(w, block, 64, start, width), flights[name]
        )

    for fetch in fetches[9:]:
        fetch.wait()

    def padded(values, to):
        return jnp.concatenate(
            [values.astype(f32), jnp.zeros((to - channels, values.shape[1]), f32)], 0
        )

    def turn(i, carry):
        at = pl.multiple_of(i * TILE, TILE)
        big[pl.ds(at, TILE), :] = padded(xt[:, pl.ds(at, TILE)], 128).T
        return carry

    lax.fori_loop(0, grid_rows // TILE, turn, 0)
    step_rows = 16

    def pick(k, block, unroll=True):
        for half in range(share // 256):

            def rows(i, carry):
                for u in range(step_rows):
                    at = i * step_rows + u
                    nacc[block + half, pl.ds(at, 1), :] = big[
                        pl.ds(pick_ref[k, hid * share + half * 256 + at], 1), :
                    ]
                return carry

            lax.fori_loop(0, 256 // step_rows, rows, 0, unroll=unroll)

    def picked(block):
        return jnp.concatenate(
            [nacc[block + half].T[:PAD].astype(bf16) for half in range(share // 256)], 1
        )

    pick(0, 0, unroll=False)
    square_tmp[...] = jnp.zeros_like(square_tmp)
    for layer in range(3):
        square_tmp[2 * layer : 2 * layer + 2, :] = norm_f[layer][:, :128]
    norm_ref[:128, :] = square_tmp[...].T
    for layer in range(3):
        square_tmp[2 * layer : 2 * layer + 2, :] = norm_f[layer][:, 128:]
    norm_ref[128:, :] = square_tmp[...].T
    square_tmp[...] = jnp.zeros_like(square_tmp)
    square_tmp[0:1, 0:channels] = dbias_f[...]
    square_tmp[1:2, 0:channels] = level_f[...].astype(f32)
    chan_ref[...] = square_tmp[...].T[:PAD]

    for name in "gb":
        weights_pass(name)
    for name in "end":
        weights_start(name)
    gather_wait(flights["g"])
    gather_wait(flights["b"])
    b_g, b_e, b_n, b_d = (bias[:, k : k + 1] for k in range(4))
    gains = [norm_ref[:, 2 * k : 2 * k + 1] for k in range(3)]
    shifts = [norm_ref[:, 2 * k + 1 : 2 * k + 2] for k in range(3)]
    wt[:, 0:256] = flip(w[:, COLS["g2"] : COLS["g2"] + 256])
    w1g = w[:, 0:128][:, :PAD]

    def embed(inputs):
        pre = mm(w1g, inputs) + b_g
        act, slope = act_forward(pre)
        normed, scale = norm_forward(mm(wt[:, 0:256], act))
        return act, slope, normed, scale

    mesh_tmp[0] = jnp.zeros((latent, share), f32)

    def pool(i, carry):
        for half in range(2):
            inputs = picked(2 * half)
            pick(lax.rem(2 * i + half + 1, g2m_deg), 2 - 2 * half)
            mesh_tmp[0] += embed(inputs)[2]
        return carry

    lax.fori_loop(0, g2m_deg // 2, pool, 0)
    h0_mine[...] = mesh_tmp[0] * (gains[0] * (1.0 / g2m_deg)) + shifts[0]
    my_mesh = pl.ds(pl.multiple_of(hid * share, share), share)
    h0_half = h0_mine[...].astype(bf16)
    h0full[:, my_mesh] = h0_half
    node_in[:latent, :] = h0_half
    h0_view = functools.partial(lanes_of, h0full, size=share)
    h0_flight = gather_start(lambda block: h0_view(block))

    lane = lax.broadcasted_iota(jnp.int32, (1, TILE), 1)
    first_row = hid * mine

    def live_mask(i):
        return (first_row + i * TILE + lane < live_ref[0]).astype(f32)

    def own(i, carry):
        here = pl.ds(pl.multiple_of(i * TILE, TILE), TILE)
        inputs = padded(
            xt[:, pl.ds(pl.multiple_of(my_grid + i * TILE, TILE), TILE)], PAD
        ).astype(bf16)
        x_ref[:, here] = inputs
        act, slope, normed, scale = embed(inputs)
        put(big, 2 * i * 2 * TILE, slope)
        act_g[:, here] = act
        put(big, (2 * i + 1) * 2 * TILE, normed)
        scale_g[:, here] = scale
        dec_in[:latent, here] = (normed * gains[0] + shifts[0]).astype(bf16)
        return carry

    def own_range(a, b):
        lax.fori_loop(a, b, own, 0)

    own_range(0, tiles)
    h0_flight = gather_pass(lambda block: h0_view(block), h0_flight)
    weights_pass("e")
    weights_pass("n")
    weights_pass("d")

    cacc[...] = jnp.zeros_like(cacc)

    def squares(i, carry):
        here = pl.ds(pl.multiple_of(i * TILE, TILE), TILE)
        delta = (padded(tt[:, here], PAD) - x_ref[:, here].astype(f32)) * live_mask(i)
        cacc[0] += fold(delta * delta)
        return carry

    lax.fori_loop(0, tiles, squares, 0)
    col = lax.broadcasted_iota(jnp.int32, (PAD, 128), 1)
    live_here = jnp.clip(live_ref[0] - first_row, 0, mine).astype(f32)
    square_tmp[...] = jnp.zeros_like(square_tmp)
    square_tmp[:PAD, :] = jnp.where(
        col == 0, jnp.sum(cacc[0], 1, keepdims=True), jnp.where(col == 1, live_here, 0.0)
    )
    small[...] = square_tmp[...].T[:8]
    sum_hid = [
        mail.copy(small, sland_h.at[slot], peer(device))
        for slot, device in enumerate((core, across, corner))
    ]

    for name in "end":
        gather_wait(flights[name])
    wt[:, 256:512] = flip(w[:, COLS["e2"] : COLS["e2"] + 256])
    wt[:, 512:768] = flip(w[:, COLS["n2"] : COLS["n2"] + 256])
    wt[:128, 768:1024] = flip(w[:, COLS["d2"] : COLS["d2"] + 128])
    gather_wait(h0_flight)

    e1 = COLS["e1"]
    mesh_tmp[0] = mm(w[:, e1 : e1 + 256], node_in[:latent, :]) + b_e
    mesh_tmp[1] = jnp.zeros((latent, share), f32)

    def edge_index(k):
        return m2m_ref[pl.ds(k, 1), my_mesh]

    def fill(index, base, rows):
        for block, part in enumerate(ones_at(index, base, rows)):
            onehot[block * 256 : block * 256 + 256, :] = part

    def edge(k, carry):
        fill(edge_index(k), 0, mesh_rows)
        sent = mm(h0full[...], onehot[...]).astype(bf16)
        hs_e[k] = sent
        pre = mesh_tmp[0] + mm(w[:, e1 + 256 : e1 + 512], sent)
        act, slope = act_forward(pre)
        act_e[k] = act
        ds_e[k] = slope
        normed, scale = norm_forward(mm(wt[:, 256:512], act))
        nrm_e[k] = normed
        scale_e[pl.ds(k, 1), :] = scale
        mesh_tmp[1] += normed
        return carry

    lax.fori_loop(0, degree, edge, 0)

    for copy in sum_hid:
        copy.wait()
    small[...] = small[...] + sland_h[0] + sland_h[1] + sland_h[2]
    sum_rows = [
        mail.copy(small, sland_r.at[step - 1], row_peer(lax.rem(row + step, row_groups)))
        for step in range(1, row_groups)
    ]
    n1 = COLS["n1"]
    node_in[latent:, :] = (mesh_tmp[1] * gains[1] + shifts[1] * degree).astype(bf16)
    act_n, slope_n = act_forward(mm(w[:, n1 : n1 + 512], node_in[...]) + b_n)
    normed_n, scale_n = norm_forward(mm(wt[:, 512:768], act_n))
    h1 = h0_mine[...] + (normed_n * gains[2] + shifts[2])
    ds_e[degree] = slope_n
    act_e[degree] = act_n
    nrm_e[degree] = normed_n
    scale_e[degree : degree + 1, :] = scale_n
    h1full[:, my_mesh] = h1.astype(bf16)
    h1_view = functools.partial(lanes_of, h1full, size=share)
    h1_flight = gather_start(lambda block: h1_view(block))

    for copy in sum_rows:
        copy.wait()
    totals = small[...]
    for step in range(1, row_groups):
        totals = totals + sland_r[step - 1]
    square_tmp[...] = jnp.zeros_like(square_tmp)
    square_tmp[:8, :] = totals
    totals = square_tmp[...].T[:PAD]
    count = totals[:, 1:2]
    var = totals[:, 0:1] / count + 1e-06
    d_bias = chan_ref[:, 0:1]
    level = chan_ref[:, 1:2]
    loss_weight = count * jnp.sum(level, 0, keepdims=True)
    tot_ref[...] = jnp.broadcast_to(loss_weight[:8], (8, 128))
    weight_var = level / var
    pull = 2.0 * weight_var / loss_weight
    nacc[...] = jnp.zeros_like(nacc)
    cacc[...] = jnp.zeros_like(cacc)
    grad[...] = jnp.zeros_like(grad)
    dsum[...] = jnp.zeros_like(dsum)


    def spot(i, write):
        base = my_grid + i * TILE

        def lanes(k, carry):
            at = pl.multiple_of(k * TILE, TILE)
            for block, part in enumerate(ones_at(g2m_ref[:, pl.ds(at, TILE)], base, TILE)):
                write(block, at, part)
            return carry

        lax.fori_loop(0, mesh_rows // TILE, lanes, 0)

    def spot_store(i, carry):
        def write(block, at, part):
            spots[i, block * 256 : block * 256 + 256, pl.ds(at, TILE)] = part

        spot(i, write)
        return carry

    ready = spots.shape[0]
    lax.fori_loop(0, ready - 1, spot_store, 0)
    h1_flight = gather_pass(lambda block: h1_view(block), h1_flight)
    lax.fori_loop(ready - 1, ready, spot_store, 0)
    gather_wait(h1_flight)

    def chunk(start, width, block):
        return rows_of(grad, block, 64, start, width)

    def reduce_start(name):
        start, width = GROUPS[name]
        flight = (
            mail.copy(
                chunk(start, width, corner), gland_a.at[1, :, pl.ds(start, width)], peer(core)
            ),
            mail.copy(
                chunk(start, width, core), gland_a.at[0, :, pl.ds(start, width)], peer(core)
            ),
        )
        return flight

    def reduce_across(name, flight):
        start, width = GROUPS[name]
        cols = pl.ds(start, width)
        flight[0].wait()
        view = chunk(start, width, across)
        view[...] = view[...] + gland_a[1, :, cols]
        return flight + (mail.copy(view, gland_b.at[:, cols], peer(across)),)

    def reduce_rows(name, flight):
        start, width = GROUPS[name]
        cols = pl.ds(start, width)
        flight[1].wait()
        flight[2].wait()
        part = 64 // near
        held[:, cols] = chunk(start, width, hid)[...] + gland_a[0, :, cols] + gland_b[:, cols]
        copies = []
        for step in range(1, near):
            to = lax.rem(row_near + step, near)
            copies.append(
                mail.copy(
                    held.at[pl.ds(pl.multiple_of(to * part, part), part), cols],
                    gland.at[step - 1],
                    row_peer(row_far * near + to),
                )
            )
        return copies

    def far_sum(own_part, cols, total):
        if far > 1:
            own_part[...] = total
            more = []
            for step in range(1, far):
                to = lax.rem(row_far + step, far)
                more.append(
                    mail.copy(
                        own_part,
                        fland.at[step - 1, :, cols],
                        row_peer(to * near + row_near),
                    )
                )
            for copy in more:
                copy.wait()
            for step in range(1, far):
                total = total + fland[step - 1, :, cols]
        return total

    side = lax.rem(row_near, 2)
    level = row_near // 2
    neighbour = row_far * near + 2 * level + 1 - side

    def half_rows(which):
        return pl.ds(pl.multiple_of(which * 32, 32), 32)

    def part_rows(where):
        return pl.ds(pl.multiple_of(side * 32 + where * 8, 8), 8)

    def level_peer(where):
        return row_peer(row_far * near + 2 * where + side)

    def rows_halve(name, flight):
        start, width = GROUPS[name]
        cols = pl.ds(start, width)
        flight[1].wait()
        flight[2].wait()
        held[:, cols] = chunk(start, width, hid)[...] + gland_a[0, :, cols] + gland_b[:, cols]
        return [
            mail.copy(held.at[half_rows(1 - side), cols], yland.at[:, cols], row_peer(neighbour))
        ]

    def rows_part(name, copies):
        start, width = GROUPS[name]
        cols = pl.ds(start, width)
        copies[0].wait()
        held[half_rows(side), cols] = held[half_rows(side), cols] + yland[:, cols]
        out = []
        for step in range(1, near // 2):
            to = lax.rem(level + step, near // 2)
            out.append(
                mail.copy(
                    held.at[part_rows(to), cols], rland.at[step - 1, :, cols], level_peer(to)
                )
            )
        return out

    def rows_total(name, copies):
        start, width = GROUPS[name]
        cols = pl.ds(start, width)
        for copy in copies:
            copy.wait()
        total = held[part_rows(level), cols]
        for step in range(1, near // 2):
            total = total + rland[step - 1, :, cols]
        own_part = out_ref.at[part_rows(level), cols]
        own_part[...] = far_sum(own_part, cols, total)
        out = []
        for step in range(1, near // 2):
            to = lax.rem(level + step, near // 2)
            out.append(mail.copy(own_part, own_part, level_peer(to)))
        return out

    def rows_back(name, copies):
        start, width = GROUPS[name]
        for copy in copies:
            copy.wait()
        view = out_ref.at[half_rows(side), pl.ds(start, width)]
        return [mail.copy(view, view, row_peer(neighbour))]

    def reduce_share(name, copies):
        start, width = GROUPS[name]
        cols = pl.ds(start, width)
        part = 64 // near
        shared = pl.ds(pl.multiple_of(row_near * part, part), part)
        own_part = out_ref.at[shared, cols]
        for copy in copies:
            copy.wait()
        total = held[shared, cols]
        for step in range(1, near):
            total = total + gland[step - 1]
        own_part[...] = far_sum(own_part, cols, total)
        out = []
        for step in range(1, near):
            to = lax.rem(row_near + step, near)
            out.append(mail.copy(own_part, own_part, row_peer(row_far * near + to)))
        return out

    d1, d2 = COLS["d1"], COLS["d2"]
    def decode(i, carry):
        here = pl.ds(pl.multiple_of(i * TILE, TILE), TILE)
        fill(m2g_ref[:, here], 0, mesh_rows)
        back = mm(h1full[...], onehot[...]) * (1.0 / m2g_deg)
        dec_in[latent:, here] = back.astype(bf16)
        pre = mm(w[:, d1 : d1 + 512], dec_in[:, here]) + b_d
        act, slope = act_forward(pre)
        out = mm(wt[:128, 768:1024], act)[:PAD]
        err = x_ref[:, here].astype(f32) + out + d_bias - padded(tt[:, here], PAD)
        kept = err * live_mask(i)
        cacc[1] += fold(weight_var * kept * err)
        pred_grad = pull * kept
        cacc[0] += fold(pred_grad)
        upstream = pred_grad.astype(bf16)
        act_grad = mm(w[:, d2 : d2 + 128][:, :PAD], upstream)
        pre_grad = (act_grad * slope).astype(bf16)
        dp_d[:, here] = pre_grad
        dsum[...] += mt(onehot[...], pre_grad)
        grad[:, d2 : d2 + PAD] += mt(act, upstream)
        return carry

    lax.fori_loop(0, tiles, decode, 0)

    def spread_start(view, land):
        return (
            mail.copy(view(corner), land.at[1], peer(core)),
            mail.copy(view(core), land.at[0], peer(core)),
        )

    def spread_across(view, land, land_far, out, copies):
        copies[0].wait()
        out[...] = (view(across)[...] + land[1]).astype(bf16)
        return copies + (mail.copy(out, land_far, peer(across)),)

    def spread_end(view, land, land_far, copies):
        copies[1].wait()
        copies[2].wait()
        return view(hid)[...] + land[0] + land_far[...].astype(f32)

    def view_d(block):
        return dsum.at[pl.ds(pl.multiple_of(block * share, share), share), :]

    d_flight = spread_start(view_d, land_a.at[0])
    w1d_low = flip(w[:, d1 : d1 + 256])
    wt[:, 1024:1280] = w1d_low
    def decode_rest(i, carry):
        here = pl.ds(pl.multiple_of(i * TILE, TILE), TILE)
        pre_grad = dp_d[:, here]
        grad[:, d1 : d1 + 512] += mt(pre_grad, dec_in[:, here])
        nacc[9] += fold(pre_grad.astype(f32))
        return carry

    lax.fori_loop(0, tiles // 2, decode_rest, 0)
    d_flight = spread_across(view_d, land_a.at[0], land_b.at[0], half_out, d_flight)
    lax.fori_loop(tiles // 2, tiles, decode_rest, 0)
    stage = {"d": reduce_start("d")}
    wt[:, 2304:2560] = flip(w[:, d1 + 256 : d1 + 512])
    wt[:, 1280:1536] = flip(w[:, n1 : n1 + 256])
    wt[:, 1536:1792] = flip(w[:, n1 + 256 : n1 + 512])
    wt[:, 1792:2048] = flip(w[:, e1 : e1 + 256])
    wt[:, 2048:2304] = flip(w[:, e1 + 256 : e1 + 512])

    def late_store(half, carry):
        def write(block, at, part):
            lanes = pl.ds(pl.multiple_of(half * mesh_rows + at, TILE), TILE)
            dec_in[block * 256 : block * 256 + 256, lanes] = part

        spot(ready + half, write)
        return carry

    def write_last(block, at, part):
        (h0full, h1full)[block][:, pl.ds(at, TILE)] = part

    lax.fori_loop(0, 2, late_store, 0)

    def write_pieces(block, at, part):
        (hs_e, act_e)[block][at // TILE] = part

    def write_whole(block, at, part):
        onehot[pl.ds(pl.multiple_of(at + block * 256, 256), 256), :] = part

    high, low = split2(spread_end(view_d, land_a.at[0], land_b.at[0], d_flight))
    stage["d"] = reduce_across("d", stage["d"])
    h1_grad = (mt(wt[:, 2304:2560], high) + mt(wt[:, 2304:2560], low)) * (1.0 / m2g_deg)
    nacc[2] += fold(h1_grad * nrm_e[degree])
    nacc[5] += fold(h1_grad)
    up_n = norm_backward(
        h1_grad, nrm_e[degree], scale_e[degree : degree + 1, :], gains[2]
    ).astype(bf16)
    n2 = COLS["n2"]
    pre_grad_n = (mm(w[:, n2 : n2 + 256], up_n) * ds_e[degree]).astype(bf16)
    mesh_tmp[0] = h1_grad + mm(wt[:, 1280:1536], pre_grad_n)
    mesh_tmp[1] = mm(wt[:, 1536:1792], pre_grad_n)

    grad[:, n2 : n2 + 256] = mt(act_e[degree], up_n)
    grad[:, n1 : n1 + 512] = mt(pre_grad_n, node_in[...])
    nacc[8] += fold(pre_grad_n.astype(f32))
    stage["n"] = reduce_start("n")

    e2 = COLS["e2"]

    def edge_back(k, carry):
        upstream = mesh_tmp[1]
        normed = nrm_e[k]
        nacc[1] += fold(upstream * normed)
        up = norm_backward(upstream, normed, scale_e[pl.ds(k, 1), :], gains[1]).astype(bf16)
        pre_grad = (mm(w[:, e2 : e2 + 256], up) * ds_e[k]).astype(bf16)
        mesh_tmp[0] += mm(wt[:, 1792:2048], pre_grad)
        grad[:, e2 : e2 + 256] += mt(act_e[k], up)
        act_e[k] = pre_grad
        nacc[7] += fold(pre_grad.astype(f32))
        return carry

    nacc[4] += fold(mesh_tmp[1]) * degree
    lax.fori_loop(0, degree // 2, edge_back, 0)
    stage["n"] = reduce_across("n", stage["n"])
    lax.fori_loop(degree // 2, degree, edge_back, 0)

    def senders(block):
        total = None
        for k in range(degree):
            place = k % 4 * TILE
            for half, part in enumerate(ones_at(edge_index(k), block * share, share)):
                onehot[place + half * 256 : place + half * 256 + 256, :] = part
            term = mt(onehot[place : place + TILE, :], act_e[k])
            total = term if total is None else total + term
        view_d(block)[...] = total

    stage["d"] = rows_halve("d", stage["d"])
    senders(corner)
    e_first = mail.copy(view_d(corner), land_a.at[1, 1], peer(core))
    senders(core)
    e_flight = (e_first, mail.copy(view_d(core), land_a.at[1, 0], peer(core)))
    senders(across)
    stage["d"] = rows_part("d", stage["d"])
    e_flight = spread_across(view_d, land_a.at[1], land_b.at[1], half_out, e_flight)
    senders(hid)

    def edge_weights(k, carry):
        grad[:, e1 : e1 + 256] += mt(act_e[k], node_in[:latent, :])
        grad[:, e1 + 256 : e1 + 512] += mt(act_e[k], hs_e[k])
        return carry

    lax.fori_loop(0, degree, edge_weights, 0)
    stage["e"] = reduce_start("e")
    stage["n"] = rows_halve("n", stage["n"])
    stage["d"] = rows_total("d", stage["d"])
    high, low = split2(spread_end(view_d, land_a.at[1], land_b.at[1], e_flight))
    h0_grad = mesh_tmp[0] + mt(wt[:, 2048:2304], high) + mt(wt[:, 2048:2304], low)
    hgfull[:, my_mesh] = (h0_grad * (1.0 / g2m_deg)).astype(bf16)
    hg_view = functools.partial(lanes_of, hgfull, size=share)
    hg_flight = gather_start(lambda block: hg_view(block))


    spot(ready + 2, write_last)
    stage["n"] = rows_part("n", stage["n"])
    stage["d"] = rows_back("d", stage["d"])
    spot(ready + 3, write_pieces)
    hg_flight = gather_pass(lambda block: hg_view(block), hg_flight)
    stage["e"] = reduce_across("e", stage["e"])
    spot(ready + 4, write_whole)
    stage["n"] = rows_total("n", stage["n"])
    gather_wait(hg_flight)

    def grid_back(i, both):
        here = pl.ds(pl.multiple_of(i * TILE, TILE), TILE)
        upstream = mm(wt[:, 1024:1280], dp_d[:, here]) + both
        normed = take(big, (2 * i + 1) * 2 * TILE)
        nacc[0] += fold(upstream * normed)
        nacc[3] += fold(upstream)
        up = norm_backward(upstream, normed, scale_g[:, here], gains[0]).astype(bf16)
        pre_grad = (mm(w[:, COLS["g2"] : COLS["g2"] + 256], up) * take(big, 2 * i * 2 * TILE)).astype(bf16)
        grad[:, COLS["g2"] : COLS["g2"] + 256] += mt(act_g[:, here], up)
        grad[:, 0:PAD] += mt(pre_grad, x_ref[:, here])
        nacc[6] += fold(pre_grad.astype(f32))

    def grid_ready(i, carry):
        grid_back(i, mt(hgfull[...], spots[i]))
        return carry

    def from_blocks(blocks):
        total = None
        for at, block in enumerate(blocks):
            term = mt(hgfull[:, at * TILE : at * TILE + TILE], block[...])
            total = term if total is None else total + term
        return total

    count_m = mesh_rows // TILE
    lax.fori_loop(0, ready, grid_ready, 0)
    stage["n"] = rows_back("n", stage["n"])
    stage["e"] = rows_halve("e", stage["e"])

    def grid_late(half, carry):
        lanes = pl.ds(pl.multiple_of(half * mesh_rows, mesh_rows), mesh_rows)
        grid_back(ready + half, mt(hgfull[...], dec_in[:, lanes]))
        return carry

    lax.fori_loop(0, 2, grid_late, 0)
    dsum[0:256, :] = mt(hgfull[...], h0full[...])
    dsum[256:512, :] = mt(hgfull[...], h1full[...])
    for half, blocks in enumerate((hs_e, act_e)):
        dsum[512 + 256 * half : 768 + 256 * half, :] = from_blocks(
            [blocks.at[k] for k in range(count_m)]
        )
    both = from_blocks([onehot.at[k * TILE : k * TILE + TILE, :] for k in range(count_m)])
    dsum[1024:1280, :] = both[:, :256]
    dsum[1280:1536, :] = both[:, 256:]

    def grid_last(k, carry):
        at = pl.multiple_of(k * TILE, TILE)
        both = jnp.concatenate([dsum[pl.ds(at, 256), :], dsum[pl.ds(at + 256, 256), :]], 1)
        grid_back(ready + 2 + k, both)
        return carry

    stage["e"] = rows_part("e", stage["e"])
    lax.fori_loop(0, 3, grid_last, 0)

    block = grad[:, 0:128]
    at_col = lax.broadcasted_iota(jnp.int32, (latent, 128), 1)
    for k in range(4):
        block = jnp.where(at_col == PAD + k, jnp.sum(nacc[6 + k], 1, keepdims=True), block)
    grad[:, 0:128] = block
    stage["g"] = reduce_start("g")
    block = jnp.zeros((latent, 128), f32)
    for k in range(6):
        block = jnp.where(at_col == 2 * (k % 3) + k // 3, jnp.sum(nacc[k], 1, keepdims=True), block)
    norm_ref[...] = block
    block = norm_ref[:PAD, :]
    for k in range(2):
        block = jnp.where(col == 6 + k, jnp.sum(cacc[k], 1, keepdims=True), block)
    norm_ref[:PAD, :] = block
    narrow[...] = norm_ref[...].T[:8]
    narrow_hid = [
        mail.copy(narrow, nland_h.at[slot], peer(device))
        for slot, device in enumerate((core, across, corner))
    ]
    stage["e"] = rows_total("e", stage["e"])
    stage["g"] = reduce_across("g", stage["g"])
    for copy in narrow_hid:
        copy.wait()
    narrow[...] = narrow[...] + nland_h[0] + nland_h[1] + nland_h[2]
    narrow_rows = [
        mail.copy(narrow, nland_r.at[step - 1], row_peer(lax.rem(row + step, row_groups)))
        for step in range(1, row_groups)
    ]
    stage["e"] = rows_back("e", stage["e"])
    stage["g"] = reduce_rows("g", stage["g"])
    stage["g"] = reduce_share("g", stage["g"])
    for copy in narrow_rows:
        copy.wait()
    total = narrow[...]
    for step in range(1, row_groups):
        total = total + nland_r[step - 1]
    all_ref[...] = total
    for name in "dneg":
        for copy in stage[name]:
            copy.wait()


def adam_step(weight, avg, sq, grad, rate, decay):
    avg_new = 0.5 * avg + 0.5 * grad
    sq_new = 0.5 * sq + 0.5 * grad * grad
    fix = 1.0 - 0.5**STEP_COUNT
    step = (avg_new * (1.0 / fix)) / (jnp.sqrt(sq_new * (1.0 / fix)) + 1e-08)
    return (weight - rate * (step + decay * weight), avg_new, sq_new)


def adam_kernel(out_ref, all_ref, tot_ref, *refs):
    ins_hbm, outs_hbm, loss_ref, weight_ref = refs[:21], refs[21:46], refs[46], refs[47]
    ins, outs, turned, sem_in, sem_out = refs[48:69], refs[69:94], refs[94], refs[95], refs[96]
    fetches = [
        pltpu.make_async_copy(source, target, sem_in.at[at])
        for at, (source, target) in enumerate(zip(ins_hbm, ins))
    ]
    for fetch in fetches:
        fetch.start()
    stores = []

    def arrive(array):
        for part in (array, 7 + array, 14 + array):
            fetches[part].wait()

    def leave(array):
        for part in (array, 7 + array, 14 + array) + ((21 + array,) if array < 4 else ()):
            store = pltpu.make_async_copy(outs[part], outs_hbm[part], sem_out.at[part])
            store.start()
            stores.append(store)

    def update(array, at, grad, rate, decay):
        fresh, avg_new, sq_new = adam_step(
            ins[array][at], ins[7 + array][at], ins[14 + array][at], grad, rate, decay
        )
        outs[array][at] = fresh
        outs[7 + array][at] = avg_new
        outs[14 + array][at] = sq_new
        if array < 4:
            outs[21 + array][at] = fresh.astype(bf16)

    everything = (slice(None), slice(None))
    channels = ins[0].shape[1]
    arrive(1)
    for layer, name in enumerate(("e1", "n1", "d1")):
        update(1, (layer,) + everything, out_ref[:, COLS[name] : COLS[name] + 512], 0.05, 0.1)
    leave(1)
    arrive(2)
    for layer, name in enumerate(("g2", "e2", "n2")):
        update(2, (layer,) + everything, out_ref[:, COLS[name] : COLS[name] + 256], 0.05, 0.1)
    leave(2)
    arrive(0)
    update(0, everything, out_ref[:, 0:128][:, :channels], 0.05, 0.1)
    leave(0)
    arrive(3)
    update(3, everything, out_ref[:, COLS["d2"] : COLS["d2"] + 128][:, :channels], 0.05, 0.1)
    leave(3)
    turned[...] = out_ref[:, 0:128].T
    arrive(4)
    update(4, everything, turned[PAD : PAD + 4, :], 0.3, 0.0)
    leave(4)
    arrive(5)
    for layer in range(3):
        update(5, (layer,) + everything, all_ref[2 * layer : 2 * layer + 2, :], 0.3, 0.0)
    leave(5)
    arrive(6)
    update(6, everything, all_ref[6:7, 0:channels], 0.3, 0.0)
    leave(6)
    loss_ref[...] = jnp.sum(all_ref[7:8, 0:PAD], 1, keepdims=True)
    weight_ref[...] = tot_ref[0:1, 0:1]
    for store in stores:
        store.wait()


def body(
    grid_input,
    grid_target,
    live_points,
    level_weight,
    g2m_index,
    m2m_index,
    m2g_index,
    *params,
):
    groups = lax.axis_size("hid")
    row_groups = lax.axis_size("rows")
    masters, avgs, squares = params[:7], params[7:14], params[14:21]
    grid_rows, channels = grid_input.shape
    mesh_rows, degree = m2m_index.shape
    latent = masters[5].shape[2]
    share = mesh_rows // groups
    mine = grid_rows // groups
    g2m_deg = g2m_index.shape[1]
    m2g_deg = m2g_index.shape[1]
    whole = pl.BlockSpec(memory_space=pltpu.VMEM)
    scalar = pl.BlockSpec(memory_space=pltpu.SMEM)
    far_memory = pl.BlockSpec(memory_space=pltpu.HBM)
    g2m = g2m_index.T

    def flat(arrays):
        first, wide, second, last, bias, norm, out_bias = arrays
        return (
            first.T,
            wide.transpose(0, 2, 1),
            second,
            last,
            bias,
            norm.transpose(1, 0, 2),
            out_bias[None],
        )

    operands = flat(masters) + flat(avgs) + flat(squares)
    loads = [
        grid_input.T,
        grid_target.T,
        g2m,
        m2m_index.T,
        m2g_index.T,
        *operands[:7],
        level_weight[None],
    ]
    kept = [jax.ShapeDtypeStruct(v.shape, v.dtype) for v in loads]
    for at in (1, 4):
        kept[at] = jax.ShapeDtypeStruct((kept[at].shape[0], mine), kept[at].dtype)
    copies = count_copies(row_groups)
    near = min(row_groups, 8)
    far = row_groups // near
    summed, spare, totals = pl.pallas_call(
        functools.partial(
            main_kernel, row_groups=row_groups, g2m_deg=g2m_deg, m2g_deg=m2g_deg
        ),
        out_shape=[
            jax.ShapeDtypeStruct((64, PACK), f32),
            jax.ShapeDtypeStruct((8, 256), f32),
            jax.ShapeDtypeStruct((8, 128), f32),
        ],
        in_specs=[scalar] * 2 + [far_memory] * 13,
        out_specs=[whole] * 3,
        scratch_shapes=[pltpu.VMEM(v.shape, v.dtype) for v in kept[:6] + kept[8:]]
        + [
            pltpu.SemaphoreType.DMA((17,)),
            pltpu.VMEM((128, 128), f32),
            pltpu.VMEM((latent, 128), f32),
            pltpu.VMEM((PAD, 128), f32),
            pltpu.VMEM((grid_rows, 128), f32),
            pltpu.VMEM((PAD, mine), bf16),
            pltpu.VMEM((256, PACK), bf16),
            pltpu.VMEM((256, 2560), bf16),
            pltpu.VMEM((256, 128), f32),
            pltpu.VMEM((latent, mesh_rows), bf16),
            pltpu.VMEM((latent, mesh_rows), bf16),
            pltpu.VMEM((latent, mesh_rows), bf16),
            pltpu.VMEM((mesh_rows, TILE), bf16),
            pltpu.VMEM((3, TILE, mesh_rows), bf16),
            pltpu.VMEM((latent, mine), bf16),
            pltpu.VMEM((1, mine), f32),
            pltpu.VMEM((2 * latent, mine), bf16),
            pltpu.VMEM((latent, mine), bf16),
            pltpu.VMEM((degree + 1, latent, share), f32),
            pltpu.VMEM((degree + 1, latent, share), bf16),
            pltpu.VMEM((degree, latent, share), bf16),
            pltpu.VMEM((degree + 1, latent, share), f32),
            pltpu.VMEM((8, share), f32),
            pltpu.VMEM((mesh_rows, latent), f32),
            pltpu.VMEM((2, 2, share, latent), f32),
            pltpu.VMEM((2, share, latent), bf16),
            pltpu.VMEM((share, latent), bf16),
            pltpu.VMEM((256, PACK), f32),
            pltpu.VMEM((2, 64, PACK), f32),
            pltpu.VMEM((64, PACK), f32),
            pltpu.VMEM((64, PACK), f32),
            pltpu.VMEM((32, PACK), f32),
            pltpu.VMEM((near - 1, 64 // near, GROUPS["g"][1]), f32),
            pltpu.VMEM((near // 2 - 1, 64 // near, PACK), f32),
            pltpu.VMEM((max(far - 1, 1), 64 // near, PACK), f32),
            pltpu.VMEM((g2m_deg * share // 256, 256, 128), f32),
            pltpu.VMEM((2, PAD, 128), f32),
            pltpu.VMEM((latent, share), f32),
            pltpu.VMEM((2 * latent, share), bf16),
            pltpu.VMEM((2, latent, share), f32),
            pltpu.VMEM((8, 128), f32),
            pltpu.VMEM((3, 8, 128), f32),
            pltpu.VMEM((row_groups - 1, 8, 128), f32),
            pltpu.VMEM((8, 256), f32),
            pltpu.VMEM((3, 8, 256), f32),
            pltpu.VMEM((row_groups - 1, 8, 256), f32),
            pltpu.SemaphoreType.DMA((copies,)),
            pltpu.SemaphoreType.DMA((copies,)),
        ],
        compiler_params=pltpu.CompilerParams(
            collective_id=0, has_side_effects=True, vmem_limit_bytes=64 * 2**20
        ),
        name="step",
    )(
        live_points,
        g2m,
        *loads,
    )
    shapes = [jax.ShapeDtypeStruct(v.shape, f32) for v in operands]
    shapes += [jax.ShapeDtypeStruct(v.shape, bf16) for v in operands[:4]]
    outs = pl.pallas_call(
        adam_kernel,
        out_shape=shapes + [jax.ShapeDtypeStruct((1, 1), f32)] * 2,
        in_specs=[whole] * 3 + [far_memory] * 21,
        out_specs=[far_memory] * 25 + [whole] * 2,
        scratch_shapes=[pltpu.VMEM(v.shape, v.dtype) for v in operands + tuple(shapes)]
        + [
            pltpu.VMEM((128, 64), f32),
            pltpu.SemaphoreType.DMA((21,)),
            pltpu.SemaphoreType.DMA((25,)),
        ],
        compiler_params=pltpu.CompilerParams(vmem_limit_bytes=64 * 2**20),
        name="adam",
    )(summed, spare, totals, *operands)

    def unflat(arrays):
        first, wide, second, last, bias, norm, out_bias = arrays
        return (
            first.T,
            wide.transpose(0, 2, 1),
            second,
            last,
            bias,
            norm.transpose(1, 0, 2),
            out_bias[0],
        )

    halves = outs[21:25]
    return (
        (outs[25][0, 0], outs[26][0, 0])
        + unflat(outs[0:7])
        + unflat(outs[7:14])
        + unflat(outs[14:21])
        + (halves[0].T, halves[1].transpose(0, 2, 1), halves[2], halves[3])
    )


def solution(mesh):
    weights = (
        P(None, "hid"),
        P(None, None, "hid"),
        P(None, "hid", None),
        P("hid", None),
        P(None, "hid"),
        P(),
        P(),
    )
    in_specs = (
        P("rows", None),
        P("rows", None),
        P("rows"),
        P(),
        P("rows", None),
        P("rows", None),
        P("rows", None),
    ) + weights * 3
    out_specs = (P(), P()) + weights * 3 + weights[:4]
    return jax.shard_map(body, mesh=mesh, in_specs=in_specs, out_specs=out_specs, check_vma=False)
```
